32 devices in a mesh: dp: 2 (over x), expert: 16 (over z, y, core).
Axes of the slice: x: 2, y: 2, z: 4, core: 2. Of those that a mesh axis runs over, the one named last changes fastest.
Arguments:
- tokens: bfloat16 [1024, 3584], P(('dp', 'expert')), may hold values from -6 to 6
- expert_ids: int32 [1024, 8], P(('dp', 'expert')), may hold values from 0 to 15, all different within a row; in each aligned block of 32 rows (0 to 31, 32 to 63, ...) at most 24 rows name the same one
- route_weights: float32 [1024, 8], P(('dp', 'expert')), may hold values from 0.1 to 1
- out_grad: bfloat16 [1024, 3584], P(('dp', 'expert')), may hold values from -6 to 6
- gate_weight: bfloat16 [16, 3584, 1024], P('expert', 'dp'), may hold values from -0.09375 to 0.09375
- up_weight: bfloat16 [16, 3584, 1024], P('expert', 'dp'), may hold values from -0.09375 to 0.09375
- down_weight: bfloat16 [16, 1024, 3584], P('expert', None, 'dp'), may hold values from -0.1875 to 0.1875
Outputs:
- mixed: bfloat16 [1024, 3584], P(('dp', 'expert'))
- tokens_grad: bfloat16 [1024, 3584], P(('dp', 'expert'))
- route_grad: float32 [1024, 8], P(('dp', 'expert'))
- gate_grad: bfloat16 [16, 3584, 1024], P('expert', 'dp')
- up_grad: bfloat16 [16, 3584, 1024], P('expert', 'dp')
- down_grad: bfloat16 [16, 1024, 3584], P('expert', None, 'dp')
The draws below stay inside these ranges and needn't reach their ends.
Inputs may be any that keep to these rules, and one draw needn't show every extreme that they name: `expert_ids`: each row names 8 different experts; in each aligned block of 32 rows (the rows of one device) no expert is named by more than 24 rows, a bound that some block reaches.
All inputs are finite; a program needn't handle non-finite values.
Results may differ from the reference program's by a relative error of at most 0.0065.
Values may be sent and summed in bfloat16 or wider, within the bound.
No kernel may reach another device: no remote copies, remote signals or barrier semaphores. Data moves between devices by JAX's collectives and lax.ppermute only.
A program may use at most 192 MiB of HBM per device.

```python
import math
import jax
import jax.numpy as jnp
import numpy as np
from jax import lax

D = 3584
H = 1024
TOP = 8
TOK_DEV = 32
EXPERTS = 16
MOST = 24
TOKENS = 1024
N_DP = 2
N_EXPERT = 16


def levels(key, dims, split, least, top_value):
    def one(dim, blocks):
        steps = jax.random.uniform(jax.random.fold_in(jax.random.fold_in(key, 6), dim), (blocks,), jnp.float32, least / len(split), top_value / len(split))
        return jnp.repeat(jnp.exp(steps), dims[dim] // blocks).reshape((-1,) + (1,) * (len(dims) - dim - 1))

    loudness = one(*split[0])
    for cut in split[1:]:
        loudness = loudness * one(*cut)
    return loudness


def assign_block(stream_key, own, number, rows, count, top, limit, slope):
    sequence = jax.random.permutation(stream_key, count)
    packed, usual = shares(count, rows * top, limit, slope, True), shares(count, rows * top, limit, slope, False)
    places = jnp.arange(count)

    def named(sizes, offset_by):
        used = int((sizes > 0).sum())
        fixed = max(1, used // 4)
        moved = fixed + (places - fixed + offset_by * (used - fixed)) % max(1, count - fixed)
        return jnp.zeros((count,), jnp.int32).at[sequence[jnp.where(places < fixed, places, moved)]].set(jnp.asarray(sizes, jnp.int32))

    sizes = jnp.where(number % 4 == 0, named(packed, number // 4), named(usual, number - number // 4 - 1))
    mixed = jax.random.permutation(jax.random.fold_in(own, 3), count)
    donor, taker = mixed[0:count // 2 * 2:2], mixed[1:count // 2 * 2:2]
    room = jnp.minimum(sizes[donor] - 1, limit - sizes[taker]) // 2
    room = jnp.where((donor == sequence[0]) | (taker == sequence[0]) | (sizes[taker] == 0), 0, jnp.maximum(room, 0))
    moved = jax.random.randint(jax.random.fold_in(own, 4), (count // 2,), 0, 1 << 20) % (room + 1)
    sizes = sizes.at[donor].add(-moved).at[taker].add(moved)
    items = jnp.searchsorted(jnp.cumsum(sizes), jnp.arange(rows * top), side="right").astype(jnp.int32)
    table = items.reshape(top, rows).T
    table = table[jax.random.permutation(jax.random.fold_in(own, 1), rows)]
    offset_by = jax.random.randint(jax.random.fold_in(own, 2), (rows, 1), 0, top)
    return jnp.take_along_axis(table, (jnp.arange(top)[None, :] + offset_by) % top, axis=1)


def shares(count, total, reach, lean, full):
    loads = [(1 << 20) // math.isqrt(grade ** lean) + 1 for grade in range(1, count + 1)]
    largest = reach if full else min(reach, max(-(-total // count), total * loads[0] // sum(loads)))
    least = 1 if total - largest >= count - 1 else 0
    counts, surplus = [largest] + [least] * (count - 1), total - largest - least * (count - 1)
    while surplus > 0:
        candidates = [i for i in range(1, count) if counts[i] < largest] or [i for i in range(1, count) if counts[i] < reach]
        whole, left = sum([loads[i] for i in candidates]), surplus
        for i in candidates:
            addition = min(reach - counts[i], max(1, left * loads[i] // whole), surplus)
            counts[i] = counts[i] + addition
            surplus = surplus - addition
    return np.array(counts)


def noise(key, dims, width, bound, cuts=(), kind=jnp.bfloat16):
    array = jax.random.normal(key, dims, jnp.float32) * width
    if len(cuts) > 0:
        array = levels(key, dims, cuts, -0.22, 0.18) * array
    return jnp.clip(array, min=-bound, max=bound).astype(kind)


def setup_inputs(seed: int = 0) -> dict:
    key_list = jax.random.split(jax.random.key(seed), 8)
    tokens = noise(key_list[0], (TOKENS, D), 1.0, 6.0, ((0, 32),))
    expert_ids_keys = jax.random.split(jax.random.fold_in(key_list[1], 1), TOKENS // TOK_DEV)
    expert_ids_turns = jax.random.permutation(jax.random.fold_in(key_list[1], 3), TOKENS // TOK_DEV)
    expert_ids = jax.vmap(lambda own, number: assign_block(jax.random.fold_in(key_list[1], 2), own, number, TOK_DEV, EXPERTS, TOP, MOST, 2))(expert_ids_keys, expert_ids_turns).reshape((TOKENS, TOP))
    route_weights = jnp.clip(jnp.exp(math.log(1.0) - 2.3025851 * jax.random.uniform(key_list[2], (TOKENS, TOP), jnp.float32) ** levels(key_list[2], (TOKENS, TOP), ((0, 32),), -0.2, 0.2)), 0.1, 1.0)
    out_grad = noise(key_list[3], (TOKENS, D), 1.0, 6.0, ((0, 32),))
    gate_weight = noise(key_list[4], (EXPERTS, D, H), D ** -0.5, 0.09375, ((0, 16), (1, 2)))
    up_weight = noise(key_list[5], (EXPERTS, D, H), D ** -0.5, 0.09375, ((0, 16), (1, 2)))
    down_weight = noise(key_list[6], (EXPERTS, H, D), H ** -0.5, 0.1875, ((0, 16), (2, 2)))
    return {"tokens": tokens, "expert_ids": expert_ids, "route_weights": route_weights, "out_grad": out_grad, "gate_weight": gate_weight, "up_weight": up_weight, "down_weight": down_weight}


def silu_parts(pre_act):
    sigmoid_val = jax.nn.sigmoid(pre_act)
    return pre_act * sigmoid_val, sigmoid_val * (1.0 + pre_act * (1.0 - sigmoid_val))


def reference(tokens, expert_ids, route_weights, out_grad, gate_weight, up_weight, down_weight):
    capacity = N_DP * N_EXPERT * MOST
    flat_ids = expert_ids.reshape(-1)
    flat_weights = route_weights.reshape(-1)
    grad32 = out_grad.astype(jnp.float32)
    rows_total = tokens.shape[0]

    def per_expert(buffers, inputs):
        mixed_acc, grad_acc, route_acc = buffers
        expert_index, gate_w, up_w, down_w = inputs
        chosen = flat_ids == expert_index
        pick_rows = jnp.nonzero(chosen, size=capacity, fill_value=0)[0].astype(jnp.int32)
        live_rows = jnp.arange(capacity, dtype=jnp.int32) < jnp.sum(chosen.astype(jnp.int32))
        owner_rows = pick_rows // TOP
        x_rows = jnp.where(live_rows[:, None], tokens[owner_rows], jnp.zeros((), jnp.bfloat16))
        gate_pre = jnp.dot(x_rows, gate_w, preferred_element_type=jnp.float32)
        up_pre = jnp.dot(x_rows, up_w, preferred_element_type=jnp.float32)
        act_val, act_slope = silu_parts(gate_pre)
        hidden = (act_val * up_pre).astype(jnp.bfloat16)
        expert_out = jnp.dot(hidden, down_w, preferred_element_type=jnp.float32).astype(jnp.bfloat16)
        out32 = expert_out.astype(jnp.float32)
        live_weights = jnp.where(live_rows, flat_weights[pick_rows], jnp.float32(0.0))
        mixed_acc = mixed_acc.at[owner_rows].add(live_weights[:, None] * out32)
        route_term = jnp.where(live_rows, jnp.sum(grad32[owner_rows] * out32, axis=1), jnp.float32(0.0))
        route_acc = route_acc.at[pick_rows].add(route_term)
        out_term = (live_weights[:, None] * grad32[owner_rows]).astype(jnp.bfloat16)
        hidden_grad = jnp.dot(out_term, down_w.T, preferred_element_type=jnp.float32)
        gate_term = (hidden_grad * up_pre * act_slope).astype(jnp.bfloat16)
        up_term = (hidden_grad * act_val).astype(jnp.bfloat16)
        input_term = (jnp.dot(gate_term, gate_w.T, preferred_element_type=jnp.float32)
                      + jnp.dot(up_term, up_w.T, preferred_element_type=jnp.float32)).astype(jnp.bfloat16)
        grad_acc = grad_acc.at[owner_rows].add(jnp.where(live_rows[:, None], input_term.astype(jnp.float32), jnp.float32(0.0)))
        gate_g = jnp.dot(x_rows.T, gate_term, preferred_element_type=jnp.float32).astype(jnp.bfloat16)
        up_g = jnp.dot(x_rows.T, up_term, preferred_element_type=jnp.float32).astype(jnp.bfloat16)
        down_g = jnp.dot(hidden.T, out_term, preferred_element_type=jnp.float32).astype(jnp.bfloat16)
        return (mixed_acc, grad_acc, route_acc), (gate_g, up_g, down_g)

    start_buffers = (jnp.zeros((rows_total, D), jnp.float32), jnp.zeros((rows_total, D), jnp.float32),
                     jnp.zeros((rows_total * TOP,), jnp.float32))
    expert_list = jnp.arange(EXPERTS, dtype=jnp.int32)
    finals, grads = lax.scan(per_expert, start_buffers, (expert_list, gate_weight, up_weight, down_weight))
    mixed_acc, grad_acc, route_acc = finals
    return (mixed_acc.astype(jnp.bfloat16), grad_acc.astype(jnp.bfloat16), route_acc.reshape(rows_total, TOP),
            grads[0], grads[1], grads[2])
```

```python
import jax
import jax.numpy as jnp
from jax import lax
from jax.sharding import PartitionSpec as P

BF = jnp.bfloat16
F32 = jnp.float32


def silu_parts(pre_act):
    sigmoid_val = jax.nn.sigmoid(pre_act)
    return (pre_act * sigmoid_val, sigmoid_val * (1.0 + pre_act * (1.0 - sigmoid_val)))


def dot_nn(first, second):
    return lax.dot_general(first, second, (((1,), (0,)), ((), ())), preferred_element_type=F32)


def dot_nt(first, second):
    return lax.dot_general(first, second, (((1,), (1,)), ((), ())), preferred_element_type=F32)


def dot_tn(first, second):
    return lax.dot_general(first, second, (((0,), (0,)), ((), ())), preferred_element_type=F32)


def shift(value, step):
    groups = lax.axis_size("dp")
    return lax.ppermute(value, "dp", [(i, (i + step) % groups) for i in range(groups)])


def choose(parts, index):
    picked = parts[0]
    for number in range(1, len(parts)):
        picked = jnp.where(index == number, parts[number], picked)
    return picked


def swap_groups(parts):
    groups = len(parts)
    mine = lax.axis_index("dp")
    by_step = [choose(parts, mine)]
    for step in range(1, groups):
        by_step.append(shift(choose(parts, (mine + step) % groups), step))
    return [choose(by_step, (mine - group) % groups) for group in range(groups)]


def sum_partials(partial):
    total = partial
    sent = partial.astype(BF)
    for step in range(1, lax.axis_size("dp")):
        total = total + shift(sent, step).astype(F32)
    return total


def per_device(tokens, expert_ids, route_weights, out_grad, gate_weight, up_weight, down_weight):
    experts = lax.axis_size("expert")
    groups = lax.axis_size("dp")
    mine = lax.axis_index("dp")
    my_expert = lax.axis_index("expert")
    rows, width = tokens.shape
    choices = expert_ids.shape[1]
    part = width // groups
    most = min(rows, 3 * rows * choices // (2 * experts))
    all_rows = experts * rows
    slots = experts * most
    gate_w, up_w, down_w = gate_weight[0], up_weight[0], down_weight[0]

    chosen = expert_ids[:, :, None] == jnp.arange(experts, dtype=jnp.int32)[None, None, :]
    weight_table = jnp.sum(jnp.where(chosen, route_weights[:, :, None], 0.0), axis=1)
    weight_all = lax.all_gather(weight_table.T.reshape(-1), ("dp", "expert"), axis=0, tiled=True)
    weight_mine = lax.dynamic_index_in_dim(
        weight_all.reshape(groups, experts, experts, rows), my_expert, 2, keepdims=False
    )

    both = [
        jnp.concatenate(
            [tokens[:, g * part : (g + 1) * part], out_grad[:, g * part : (g + 1) * part]], axis=1
        )
        for g in range(groups)
    ]
    both = swap_groups(both)
    gathered = [lax.all_gather(both[g], "expert", axis=0, tiled=True) for g in range(groups)]

    xs, terms_out, hiddens, gate_terms, up_terms = [], [], [], [], []
    mixed_parts, grad_parts, route_parts = [], [], []
    for g in range(groups):
        weight = weight_mine[g]
        live = weight > 0.0
        place = jnp.cumsum(live.astype(jnp.int32), axis=1) - 1
        slot = jnp.where(live, place + most * jnp.arange(experts, dtype=jnp.int32)[:, None], -1)
        pick = slot.reshape(1, all_rows) == jnp.arange(slots, dtype=jnp.int32)[:, None]
        pick_bf = pick.astype(BF)
        weight_rows = jnp.sum(jnp.where(pick, weight.reshape(1, all_rows), 0.0), axis=1)
        picked = dot_nn(pick_bf, gathered[g]).astype(BF)
        x_rows = picked[:, :part]
        grad_rows = picked[:, part:].astype(F32)
        out_term = (weight_rows[:, None] * grad_rows).astype(BF)
        gate_pre = sum_partials(dot_nn(x_rows, gate_w))
        up_pre = sum_partials(dot_nn(x_rows, up_w))
        hidden_grad = sum_partials(dot_nt(out_term, down_w))
        act_val, act_slope = silu_parts(gate_pre)
        hidden = (act_val * up_pre).astype(BF)
        gate_term = (hidden_grad * up_pre * act_slope).astype(BF)
        up_term = (hidden_grad * act_val).astype(BF)
        expert_out = dot_nn(hidden, down_w).astype(BF).astype(F32)
        route_rows = jnp.sum(grad_rows * expert_out, axis=1)
        route_parts.append(jnp.sum(jnp.where(pick, route_rows[:, None], 0.0), axis=0))
        dense_out = dot_tn(pick_bf, (weight_rows[:, None] * expert_out).astype(BF)).astype(BF)
        mixed_parts.append(lax.psum_scatter(dense_out, "expert", scatter_dimension=0, tiled=True))
        input_term = (dot_nt(gate_term, gate_w) + dot_nt(up_term, up_w)).astype(BF)
        dense_in = dot_tn(pick_bf, input_term).astype(BF)
        grad_parts.append(lax.psum_scatter(dense_in, "expert", scatter_dimension=0, tiled=True))
        xs.append(x_rows)
        terms_out.append(out_term)
        hiddens.append(hidden)
        gate_terms.append(gate_term)
        up_terms.append(up_term)

    x_all = jnp.concatenate(xs, axis=0)
    gate_grad = dot_tn(x_all, jnp.concatenate(gate_terms, axis=0)).astype(BF)[None]
    up_grad = dot_tn(x_all, jnp.concatenate(up_terms, axis=0)).astype(BF)[None]
    down_grad = dot_tn(
        jnp.concatenate(hiddens, axis=0), jnp.concatenate(terms_out, axis=0)
    ).astype(BF)[None]

    route_all = lax.all_gather(
        jnp.concatenate(route_parts, axis=0), ("dp", "expert"), axis=0, tiled=True
    ).reshape(groups, experts, groups, experts, rows)
    route_mine = lax.dynamic_index_in_dim(
        lax.dynamic_index_in_dim(route_all, mine, 2, keepdims=False), my_expert, 2, keepdims=False
    )
    route_table = jnp.sum(route_mine, axis=0)
    route_grad = jnp.sum(jnp.where(chosen, route_table.T[:, None, :], 0.0), axis=2)

    mixed = jnp.concatenate(swap_groups(mixed_parts), axis=1)
    tokens_grad = jnp.concatenate(swap_groups(grad_parts), axis=1)
    return (mixed, tokens_grad, route_grad, gate_grad, up_grad, down_grad)


def solution(mesh):
    return jax.shard_map(
        per_device,
        mesh=mesh,
        in_specs=(
            P(("dp", "expert"), None),
            P(("dp", "expert"), None),
            P(("dp", "expert"), None),
            P(("dp", "expert"), None),
            P("expert", "dp", None),
            P("expert", "dp", None),
            P("expert", None, "dp"),
        ),
        out_specs=(
            P(("dp", "expert"), None),
            P(("dp", "expert"), None),
            P(("dp", "expert"), None),
            P("expert", "dp", None),
            P("expert", "dp", None),
            P("expert", None, "dp"),
        ),
        check_vma=False,
    )
```

```python
import jax
import jax.numpy as jnp
from jax import lax
from jax.sharding import PartitionSpec as P

BF = jnp.bfloat16
F32 = jnp.float32


def silu_parts(pre_act):
    sigmoid_val = jax.nn.sigmoid(pre_act)
    return (pre_act * sigmoid_val, sigmoid_val * (1.0 + pre_act * (1.0 - sigmoid_val)))


def dot_nn(first, second):
    return lax.dot_general(first, second, (((1,), (0,)), ((), ())), preferred_element_type=F32)


def dot_nt(first, second):
    return lax.dot_general(first, second, (((1,), (1,)), ((), ())), preferred_element_type=F32)


def dot_tn(first, second):
    return lax.dot_general(first, second, (((0,), (0,)), ((), ())), preferred_element_type=F32)


def shift_dp(value, step):
    groups = lax.axis_size("dp")
    return lax.ppermute(value, "dp", [(i, (i + step) % groups) for i in range(groups)])


def choose(parts, index):
    picked = parts[0]
    for number in range(1, len(parts)):
        picked = jnp.where(index == number, parts[number], picked)
    return picked


def swap_groups(parts):
    groups = len(parts)
    mine = lax.axis_index("dp")
    by_step = [choose(parts, mine)]
    for step in range(1, groups):
        by_step.append(shift_dp(choose(parts, (mine + step) % groups), step))
    return [choose(by_step, (mine - group) % groups) for group in range(groups)]


def sum_partials(partial):
    total = partial
    sent = partial.astype(BF)
    for step in range(1, lax.axis_size("dp")):
        total = total + shift_dp(sent, step).astype(F32)
    return total


def factors(experts):
    core = 2 if experts % 2 == 0 else 1
    rest = experts // core
    inner = 1
    while rest % (inner * 2) == 0 and (inner * 2) ** 2 <= rest:
        inner = inner * 2
    return (rest // inner, inner, core)


def shift_expert(value, level, step):
    dims = factors(lax.axis_size("expert"))
    stride = 1
    for dim in dims[level + 1 :]:
        stride = stride * dim
    size = dims[level]
    pairs = []
    for source in range(lax.axis_size("expert")):
        place = source // stride % size
        pairs.append((source, source + ((place + step) % size - place) * stride))
    return lax.ppermute(value, "expert", pairs)


def gather_level(piece, level):
    size = factors(lax.axis_size("expert"))[level]
    if size == 1:
        return piece
    return jnp.concatenate(
        [piece] + [shift_expert(piece, level, step) for step in range(1, size)], axis=0
    )


def scatter_level(rows, level):
    size = factors(lax.axis_size("expert"))[level]
    count = rows.shape[0] // size
    total = rows[:count].astype(F32)
    for step in range(1, size):
        sent = rows[step * count : (step + 1) * count].astype(BF)
        total = total + shift_expert(sent, level, -step).astype(F32)
    return total


def three_pieces(value):
    high = lax.reduce_precision(value, 8, 7)
    rest = value - high
    mid = lax.reduce_precision(rest, 8, 7)
    return [high.astype(BF), mid.astype(BF), (rest - mid).astype(BF)]


def per_device(tokens, expert_ids, route_weights, out_grad, gate_weight, up_weight, down_weight):
    experts = lax.axis_size("expert")
    groups = lax.axis_size("dp")
    my_expert = lax.axis_index("expert")
    outer, inner, core = factors(experts)
    rows, width = tokens.shape
    choices = expert_ids.shape[1]
    part = width // groups
    most = min(rows, 3 * rows * choices // (2 * experts))
    extra = -(-3 * experts // 128) * 128
    gate_w, up_w, down_w = gate_weight[0], up_weight[0], down_weight[0]

    chosen = expert_ids[:, :, None] == jnp.arange(experts, dtype=jnp.int32)[None, None, :]
    weight_table = jnp.sum(jnp.where(chosen, route_weights[:, :, None], 0.0), axis=1)
    weight_cols = jnp.concatenate(
        three_pieces(weight_table) + [jnp.zeros((rows, extra - 3 * experts), BF)], axis=1
    )
    payload = jnp.concatenate(
        swap_groups(
            [
                jnp.concatenate(
                    [
                        tokens[:, g * part : (g + 1) * part],
                        out_grad[:, g * part : (g + 1) * part],
                        weight_cols,
                    ],
                    axis=1,
                )
                for g in range(groups)
            ]
        ),
        axis=0,
    )

    distances = [[0]]
    if outer > 1:
        distances.append(sorted({1, outer - 1}))
    if outer > 3:
        distances.append(list(range(2, outer - 1)))
    column = jnp.arange(extra, dtype=jnp.int32)[None, :]
    my_column = (column % experts == my_expert) & (column < 3 * experts)

    def gather_chunk(steps):
        piece = jnp.concatenate(
            [payload if step == 0 else shift_expert(payload, 0, step) for step in steps], axis=0
        )
        return gather_level(gather_level(piece, 1), 2)

    chunks = []
    for steps in distances:
        arrived = gather_chunk(steps)
        count = arrived.shape[0]
        blocks = count // rows
        slots = blocks * most
        weight = jnp.sum(
            jnp.where(my_column, arrived[:, 2 * part :].astype(F32), 0.0), axis=1
        )
        live = (weight > 0.0).reshape(blocks, rows)
        place = jnp.cumsum(live.astype(jnp.int32), axis=1) - 1
        slot = jnp.where(live, place + most * jnp.arange(blocks, dtype=jnp.int32)[:, None], -1)
        pick = slot.reshape(1, count) == jnp.arange(slots, dtype=jnp.int32)[:, None]
        weight_rows = jnp.sum(jnp.where(pick, weight[None, :], 0.0), axis=1)
        pick = pick.astype(BF)
        picked = dot_nn(pick, arrived[:, : 2 * part]).astype(BF)
        x_rows = picked[:, :part]
        grad_rows = picked[:, part:].astype(F32)
        out_term = (weight_rows[:, None] * grad_rows).astype(BF)
        gate_pre = sum_partials(dot_nn(x_rows, gate_w))
        up_pre = sum_partials(dot_nn(x_rows, up_w))
        hidden_grad = sum_partials(dot_nt(out_term, down_w))
        chunks.append((pick, weight_rows, x_rows, grad_rows, out_term, gate_pre, up_pre, hidden_grad))

    final = jnp.zeros((), F32)
    saved = []
    for steps, chunk in zip(distances, chunks):
        pick, weight_rows, x_rows, grad_rows, out_term, gate_pre, up_pre, hidden_grad = chunk
        act_val, act_slope = silu_parts(gate_pre)
        hidden = (act_val * up_pre).astype(BF)
        gate_term = (hidden_grad * up_pre * act_slope).astype(BF)
        up_term = (hidden_grad * act_val).astype(BF)
        expert_out = dot_nn(hidden, down_w).astype(BF).astype(F32)
        route_rows = jnp.sum(grad_rows * expert_out, axis=1)
        pieces = three_pieces(route_rows)
        route_cols = jnp.zeros((), BF)
        for number in range(3):
            route_cols = jnp.where(
                column == number * experts + my_expert, pieces[number][:, None], route_cols
            )
        input_term = (dot_nt(gate_term, gate_w) + dot_nt(up_term, up_w)).astype(BF)
        back = jnp.concatenate(
            [(weight_rows[:, None] * expert_out).astype(BF), input_term, route_cols], axis=1
        )
        dense = dot_tn(pick, back).astype(BF)
        mine = scatter_level(scatter_level(dense, 2), 1)
        count = mine.shape[0] // len(steps)
        for number, step in enumerate(steps):
            piece = mine[number * count : (number + 1) * count]
            if step:
                piece = shift_expert(piece.astype(BF), 0, -step).astype(F32)
            final = final + piece
        saved.append((x_rows, out_term, hidden, gate_term, up_term))

    x_all, out_all, hidden_all, gate_all, up_all = (
        jnp.concatenate(arrays, axis=0) for arrays in zip(*saved)
    )
    gate_grad = dot_tn(x_all, gate_all).astype(BF)[None]
    up_grad = dot_tn(x_all, up_all).astype(BF)[None]
    down_grad = dot_tn(hidden_all, out_all).astype(BF)[None]

    final = final.astype(BF)
    parts = swap_groups([final[g * rows : (g + 1) * rows] for g in range(groups)])
    mixed = jnp.concatenate([value[:, :part] for value in parts], axis=1)
    tokens_grad = jnp.concatenate([value[:, part : 2 * part] for value in parts], axis=1)
    route_table = jnp.zeros((), F32)
    for value in parts:
        for number in range(3):
            start = 2 * part + number * experts
            route_table = route_table + value[:, start : start + experts].astype(F32)
    route_grad = jnp.sum(jnp.where(chosen, route_table[:, None, :], 0.0), axis=2)
    return (mixed, tokens_grad, route_grad, gate_grad, up_grad, down_grad)


def solution(mesh):
    return jax.shard_map(
        per_device,
        mesh=mesh,
        in_specs=(
            P(("dp", "expert"), None),
            P(("dp", "expert"), None),
            P(("dp", "expert"), None),
            P(("dp", "expert"), None),
            P("expert", "dp", None),
            P("expert", "dp", None),
            P("expert", None, "dp"),
        ),
        out_specs=(
            P(("dp", "expert"), None),
            P(("dp", "expert"), None),
            P(("dp", "expert"), None),
            P("expert", "dp", None),
            P("expert", "dp", None),
            P("expert", None, "dp"),
        ),
        check_vma=False,
    )
```

```python
import jax
import jax.numpy as jnp
from jax import lax
from jax.sharding import PartitionSpec as P

BF = jnp.bfloat16
F32 = jnp.float32


def silu_parts(pre_act):
    sigmoid_val = jax.nn.sigmoid(pre_act)
    return (pre_act * sigmoid_val, sigmoid_val * (1.0 + pre_act * (1.0 - sigmoid_val)))


def dot_nn(first, second):
    return lax.dot_general(first, second, (((1,), (0,)), ((), ())), preferred_element_type=F32)


def dot_nt(first, second):
    return lax.dot_general(first, second, (((1,), (1,)), ((), ())), preferred_element_type=F32)


def dot_tn(first, second):
    return lax.dot_general(first, second, (((0,), (0,)), ((), ())), preferred_element_type=F32)


def shift_dp(value, step):
    groups = lax.axis_size("dp")
    return lax.ppermute(value, "dp", [(i, (i + step) % groups) for i in range(groups)])


def choose(parts, index):
    picked = parts[0]
    for number in range(1, len(parts)):
        picked = jnp.where(index == number, parts[number], picked)
    return picked


def swap_groups(parts):
    groups = len(parts)
    mine = lax.axis_index("dp")
    by_step = [choose(parts, mine)]
    for step in range(1, groups):
        by_step.append(shift_dp(choose(parts, (mine + step) % groups), step))
    return [choose(by_step, (mine - group) % groups) for group in range(groups)]


def exchange(sent):
    return [shift_dp(sent, step) for step in range(1, lax.axis_size("dp"))]


def add_all(total, arrived):
    for value in arrived:
        total = total + value.astype(F32)
    return total


class Order:
    def __init__(self):
        self.last = []

    def enter(self, *values):
        flat, tree = jax.tree.flatten(values)
        tied = lax.optimization_barrier(tuple(flat) + tuple(self.last))[: len(flat)]
        return jax.tree.unflatten(tree, tied)

    def leave(self, *values):
        self.last = list(values)


def factors(experts):
    core = 2 if experts % 2 == 0 else 1
    rest = experts // core
    inner = 1
    while rest % (inner * 2) == 0 and (inner * 2) ** 2 <= rest:
        inner = inner * 2
    return (rest // inner, inner, core)


def shift_expert(value, level, step):
    dims = factors(lax.axis_size("expert"))
    stride = 1
    for dim in dims[level + 1 :]:
        stride = stride * dim
    size = dims[level]
    pairs = []
    for source in range(lax.axis_size("expert")):
        place = source // stride % size
        pairs.append((source, source + ((place + step) % size - place) * stride))
    return lax.ppermute(value, "expert", pairs)


def level_size(level):
    return factors(lax.axis_size("expert"))[level]


def gather_start(piece, level):
    return [piece] + [shift_expert(piece, level, step) for step in range(1, level_size(level))]


def scatter_start(rows, level):
    size = level_size(level)
    count = rows.shape[0] // size
    parts = [rows[step * count : (step + 1) * count] for step in range(size)]
    return (
        parts[0].astype(F32),
        [shift_expert(parts[step].astype(BF), level, -step) for step in range(1, size)],
    )


def three_pieces(value):
    high = lax.reduce_precision(value, 8, 7)
    rest = value - high
    mid = lax.reduce_precision(rest, 8, 7)
    return [high.astype(BF), mid.astype(BF), (rest - mid).astype(BF)]


def per_device(tokens, expert_ids, route_weights, out_grad, gate_weight, up_weight, down_weight):
    experts = lax.axis_size("expert")
    groups = lax.axis_size("dp")
    my_expert = lax.axis_index("expert")
    outer, inner, core = factors(experts)
    rows, width = tokens.shape
    hidden_width = gate_weight.shape[2]
    choices = expert_ids.shape[1]
    part = width // groups
    most = min(rows, 3 * rows * choices // (2 * experts))
    extra = -(-3 * experts // 128) * 128
    gate_w, up_w, down_w = gate_weight[0], up_weight[0], down_weight[0]

    chosen = expert_ids[:, :, None] == jnp.arange(experts, dtype=jnp.int32)[None, None, :]
    weight_table = jnp.sum(jnp.where(chosen, route_weights[:, :, None], 0.0), axis=1)
    weight_cols = jnp.concatenate(
        three_pieces(weight_table) + [jnp.zeros((rows, extra - 3 * experts), BF)], axis=1
    )
    payload = jnp.concatenate(
        swap_groups(
            [
                jnp.concatenate(
                    [
                        tokens[:, g * part : (g + 1) * part],
                        out_grad[:, g * part : (g + 1) * part],
                        weight_cols,
                    ],
                    axis=1,
                )
                for g in range(groups)
            ]
        ),
        axis=0,
    )

    joined_w = jnp.concatenate([gate_w, up_w], axis=1)
    column = jnp.arange(extra, dtype=jnp.int32)[None, :]
    my_column = (column % experts == my_expert) & (column < 3 * experts)
    count = inner * core * groups * rows
    blocks = inner * core * groups
    slots = blocks * most
    order = Order()

    def pick_rows(arrived):
        weight = jnp.sum(jnp.where(my_column, arrived[:, 2 * part :].astype(F32), 0.0), axis=1)
        live = (weight > 0.0).reshape(blocks, rows)
        place = jnp.cumsum(live.astype(jnp.int32), axis=1) - 1
        slot = jnp.where(live, place + most * jnp.arange(blocks, dtype=jnp.int32)[:, None], -1)
        pick = slot.reshape(1, count) == jnp.arange(slots, dtype=jnp.int32)[:, None]
        weight_rows = jnp.sum(jnp.where(pick, weight[None, :], 0.0), axis=1)
        pick = pick.astype(BF)
        picked = dot_nn(pick, arrived[:, : 2 * part]).astype(BF)
        x_rows = picked[:, :part]
        grad_rows = picked[:, part:]
        out_term = (weight_rows[:, None] * grad_rows.astype(F32)).astype(BF)
        return (pick, weight_rows, x_rows, grad_rows, out_term)

    def start_inner(number):
        (piece,) = order.enter(pieces[number])
        around[number] = gather_start(piece, 1)

    def start_core(number):
        (parts,) = order.enter(around[number])
        rows_here = jnp.concatenate(parts, axis=0)
        order.leave(rows_here)
        around[number] = gather_start(rows_here, 2)

    def partial_sums(number):
        (parts,) = order.enter(around[number])
        chunk = pick_rows(jnp.concatenate(parts, axis=0))
        joined = dot_nn(chunk[2], joined_w)
        hidden_grad = dot_nt(chunk[4], down_w)
        sent = (joined.astype(BF), hidden_grad.astype(BF))
        order.leave(*sent)
        picked[number] = chunk
        sums[number] = [joined, exchange(sent[0]), hidden_grad, exchange(sent[1])]

    def forward(number):
        pick, weight_rows, x_rows, grad_rows, out_term = picked[number]
        joined, arrived, grad_rows = order.enter(sums[number][0], sums[number][1], grad_rows)
        joined = add_all(joined, arrived)
        gate_pre, up_pre = joined[:, :hidden_width], joined[:, hidden_width:]
        act_val, act_slope = silu_parts(gate_pre)
        hidden = (act_val * up_pre).astype(BF)
        expert_out = dot_nn(hidden, down_w).astype(BF).astype(F32)
        route_rows = jnp.sum(grad_rows.astype(F32) * expert_out, axis=1)
        values = three_pieces(route_rows)
        route_cols = jnp.zeros((), BF)
        for index in range(3):
            route_cols = jnp.where(
                column == index * experts + my_expert, values[index][:, None], route_cols
            )
        back = jnp.concatenate(
            [(weight_rows[:, None] * expert_out).astype(BF), route_cols], axis=1
        )
        hiddens[number] = hidden
        slopes[number] = (up_pre * act_slope, act_val)
        return back

    def backward(number):
        hidden_grad, arrived, slope = order.enter(sums[number][2], sums[number][3], slopes[number])
        hidden_grad = add_all(hidden_grad, arrived)
        terms = jnp.concatenate(
            [(hidden_grad * slope[0]).astype(BF), (hidden_grad * slope[1]).astype(BF)], axis=1
        )
        all_terms[number] = terms
        return dot_nt(terms, joined_w).astype(BF)

    def start_back(number, back):
        dense = dot_tn(picked[number][0], back).astype(BF)
        order.leave(dense)
        return scatter_start(dense, 2)

    def next_inner(moving):
        total, arrived = order.enter(*moving)
        total = add_all(total, arrived)
        order.leave(total)
        return scatter_start(total, 1)

    def next_outer(number, moving):
        total, arrived = order.enter(*moving)
        total = add_all(total, arrived)
        order.leave(total)
        if number == 0:
            return total
        return shift_expert(total.astype(BF), 0, -number)

    around, picked, sums, hiddens, slopes, all_terms = {}, {}, {}, {}, {}, {}
    pieces = {0: payload}
    start_inner(0)
    if outer > 1:
        pieces[1] = shift_expert(payload, 0, 1)
    tied = around[0][1:] + [payload]
    for step in range(2, outer):
        tied = lax.optimization_barrier(tuple(tied))
        pieces[step] = shift_expert(tied[-1], 0, step)
        tied = [pieces[step - 1], payload]

    last = outer - 1
    moving, finals, wide = {}, [], {}
    start_core(0)
    partial_sums(0)
    if outer > 1:
        start_inner(1)
        start_core(1)
        partial_sums(1)
    for number in range(outer):
        later = number + 2
        if later < outer:
            start_inner(later)
        forward_back = forward(number)
        if number == last:
            moving[number] = start_back(number, forward_back)
        else:
            moving[number] = start_back(
                number, jnp.concatenate([forward_back, backward(number)], axis=1)
            )
        if later < outer:
            start_core(later)
            partial_sums(later)
        if number > 0:
            finals.append(next_outer(number - 1, moving[number - 1]))
        if number != last:
            moving[number] = next_inner(moving[number])

    out_all = jnp.concatenate([picked[number][4] for number in range(outer)], axis=0)
    hidden_all = jnp.concatenate([hiddens[number] for number in range(outer)], axis=0)
    hidden_all, out_all = order.enter(hidden_all, out_all)
    down_grad = dot_tn(hidden_all, out_all).astype(BF)[None]
    order.leave(down_grad)
    moving_grad = start_back(last, backward(last))
    moving[last] = next_inner(moving[last])
    moving_grad = next_inner(moving_grad)
    x_all = jnp.concatenate([picked[number][2] for number in range(outer)], axis=0)
    terms_all = jnp.concatenate([all_terms[number] for number in range(outer)], axis=0)
    x_all, terms_all = order.enter(x_all, terms_all)
    gate_grad = dot_tn(x_all, terms_all[:, :hidden_width]).astype(BF)[None]
    order.leave(gate_grad)
    last_out = next_outer(last, moving[last])
    last_grad = next_outer(last, moving_grad)
    x_all, terms_all = order.enter(x_all, terms_all)
    up_grad = dot_tn(x_all, terms_all[:, hidden_width:]).astype(BF)[None]
    order.leave(up_grad)
    finals, last_out, last_grad = order.enter(finals, last_out, last_grad)
    out_sum = last_out.astype(F32)
    grad_sum = last_grad.astype(F32)
    for value in finals:
        out_sum = out_sum + value[:, : part + extra].astype(F32)
        grad_sum = grad_sum + value[:, part + extra :].astype(F32)
    final = jnp.concatenate([out_sum, grad_sum], axis=1)

    final = final.astype(BF)
    parts = swap_groups([final[g * rows : (g + 1) * rows] for g in range(groups)])
    mixed = jnp.concatenate([value[:, :part] for value in parts], axis=1)
    tokens_grad = jnp.concatenate([value[:, part + extra :] for value in parts], axis=1)
    route_table = jnp.zeros((), F32)
    for value in parts:
        for number in range(3):
            start = part + number * experts
            route_table = route_table + value[:, start : start + experts].astype(F32)
    route_grad = jnp.sum(jnp.where(chosen, route_table[:, None, :], 0.0), axis=2)
    return (mixed, tokens_grad, route_grad, gate_grad, up_grad, down_grad)


def solution(mesh):
    return jax.shard_map(
        per_device,
        mesh=mesh,
        in_specs=(
            P(("dp", "expert"), None),
            P(("dp", "expert"), None),
            P(("dp", "expert"), None),
            P(("dp", "expert"), None),
            P("expert", "dp", None),
            P("expert", "dp", None),
            P("expert", None, "dp"),
        ),
        out_specs=(
            P(("dp", "expert"), None),
            P(("dp", "expert"), None),
            P(("dp", "expert"), None),
            P("expert", "dp", None),
            P("expert", "dp", None),
            P("expert", None, "dp"),
        ),
        check_vma=False,
    )
```

```python
import jax
import jax.numpy as jnp
from jax import lax
from jax.experimental import pallas as pl
from jax.experimental.pallas import tpu as pltpu
from jax.sharding import PartitionSpec as P

BF = jnp.bfloat16
F32 = jnp.float32


def silu_parts(pre_act):
    sigmoid_val = jax.nn.sigmoid(pre_act)
    return (pre_act * sigmoid_val, sigmoid_val * (1.0 + pre_act * (1.0 - sigmoid_val)))


def dot_nn(first, second):
    return lax.dot_general(first, second, (((1,), (0,)), ((), ())), preferred_element_type=F32)


def dot_nt(first, second):
    return lax.dot_general(first, second, (((1,), (1,)), ((), ())), preferred_element_type=F32)


def dot_tn(first, second):
    return lax.dot_general(first, second, (((0,), (0,)), ((), ())), preferred_element_type=F32)


def shift_dp(value, step):
    groups = lax.axis_size("dp")
    return lax.ppermute(value, "dp", [(i, (i + step) % groups) for i in range(groups)])


def choose(parts, index):
    picked = parts[0]
    for number in range(1, len(parts)):
        picked = jnp.where(index == number, parts[number], picked)
    return picked


def swap_groups(parts):
    groups = len(parts)
    mine = lax.axis_index("dp")
    by_step = [choose(parts, mine)]
    for step in range(1, groups):
        by_step.append(shift_dp(choose(parts, (mine + step) % groups), step))
    return [choose(by_step, (mine - group) % groups) for group in range(groups)]


def exchange(sent):
    return [shift_dp(sent, step) for step in range(1, lax.axis_size("dp"))]


def add_all(total, arrived):
    for value in arrived:
        total = total + value.astype(F32)
    return total


class Order:
    def __init__(self):
        self.last = []

    def enter(self, *values):
        flat, tree = jax.tree.flatten(values)
        tied = lax.optimization_barrier(tuple(flat) + tuple(self.last))[: len(flat)]
        return jax.tree.unflatten(tree, tied)

    def leave(self, *values):
        self.last = list(values)


def factors(experts):
    core = 2 if experts % 2 == 0 else 1
    rest = experts // core
    inner = 1
    while rest % (inner * 2) == 0 and (inner * 2) ** 2 <= rest:
        inner = inner * 2
    return (rest // inner, inner, core)


def shift_expert(value, level, step):
    dims = factors(lax.axis_size("expert"))
    stride = 1
    for dim in dims[level + 1 :]:
        stride = stride * dim
    size = dims[level]
    pairs = []
    for source in range(lax.axis_size("expert")):
        place = source // stride % size
        pairs.append((source, source + ((place + step) % size - place) * stride))
    return lax.ppermute(value, "expert", pairs)


def level_size(level):
    return factors(lax.axis_size("expert"))[level]


def gather_start(piece, level):
    return [piece] + [shift_expert(piece, level, step) for step in range(1, level_size(level))]


def three_pieces(value):
    high = lax.reduce_precision(value, 8, 7)
    rest = value - high
    mid = lax.reduce_precision(rest, 8, 7)
    return [high.astype(BF), mid.astype(BF), (rest - mid).astype(BF)]


def rows_of(values):
    return jnp.concatenate(values, axis=0) if len(values) > 1 else values[0]


def project_body(number_parts, part, *refs):
    mask_ref, order_ref, base_ref = refs[:3]
    part_refs = refs[3 : 3 + number_parts]
    gate_ref, up_ref, down_ref = refs[3 + number_parts : 6 + number_parts]
    x_ref, grad_ref, term_ref, weight_ref, pick_ref, own_ref, sent_ref = refs[6 + number_parts :]

    @pl.when(pl.program_id(0) == 0)
    def _():
        slots = x_ref.shape[0]
        arrived = rows_of([ref[...] for ref in part_refs])
        count = arrived.shape[0]
        mask = mask_ref[...]
        weight = dot_nt(mask, arrived[:, 2 * part :])
        live = weight > 0.0
        place = dot_nn(jnp.where(live, 1.0, 0.0).astype(BF), order_ref[...])
        slot = jnp.where(live, place - 1.0 + base_ref[...], -1.0)[:1]
        index = lax.broadcasted_iota(jnp.int32, (slots, count), 0).astype(F32)
        pick = jnp.where(index == slot, 1.0, 0.0).astype(BF)
        pick_ref[...] = pick
        x_ref[...] = dot_nn(pick, arrived[:, :part]).astype(BF)
        grad = dot_nn(pick, arrived[:, part : 2 * part])
        grad_ref[...] = grad.astype(BF)
        chosen = dot_nn(pick, arrived[:, 2 * part :]) * mask[:1].astype(F32)
        weight_rows = jnp.sum(chosen, axis=1, keepdims=True)
        weight_ref[...] = jnp.broadcast_to(weight_rows, weight_ref.shape)
        term_ref[...] = (weight_rows * grad).astype(BF)

    x_rows = x_ref[...]
    values = (
        dot_nn(x_rows, gate_ref[...]),
        dot_nn(x_rows, up_ref[...]),
        dot_nt(term_ref[...], down_ref[...]),
    )
    for number, value in enumerate(values):
        own_ref[number] = value
        sent_ref[number] = value.astype(BF)


def project(parts, mask, order, base, slots, gate_w, up_w, down_w):
    part, hidden = gate_w.shape
    tile = min(256, hidden)
    count = sum(value.shape[0] for value in parts)
    whole = lambda shape: pl.BlockSpec(shape, lambda j: (0,) * len(shape))
    columns = lambda rows: pl.BlockSpec((rows, tile), lambda j: (0, j))
    stacked = pl.BlockSpec((3, slots, tile), lambda j: (0, 0, j))
    row_out = jax.ShapeDtypeStruct((slots, part), BF)
    return pl.pallas_call(
        lambda *refs: project_body(len(parts), part, *refs),
        grid=(hidden // tile,),
        in_specs=[whole(mask.shape), whole(order.shape), whole(base.shape)]
        + [whole(value.shape) for value in parts]
        + [columns(part), columns(part), pl.BlockSpec((tile, part), lambda j: (j, 0))],
        out_specs=[whole((slots, part))] * 3
        + [whole((slots, 128)), whole((slots, count)), stacked, stacked],
        out_shape=[row_out] * 3
        + [
            jax.ShapeDtypeStruct((slots, 128), F32),
            jax.ShapeDtypeStruct((slots, count), BF),
            jax.ShapeDtypeStruct((3, slots, hidden), F32),
            jax.ShapeDtypeStruct((3, slots, hidden), BF),
        ],
        compiler_params=pltpu.CompilerParams(vmem_limit_bytes=56 * 2**20),
        name="project",
    )(mask, order, base, *parts, gate_w, up_w, down_w)


def join(values):
    if len(values) == 1:
        return values[0]
    rows, wide = values[0].shape

    def body(*refs):
        for number, ref in enumerate(refs[:-1]):
            refs[-1][number * rows : (number + 1) * rows] = ref[...]

    return pl.pallas_call(
        body,
        out_shape=jax.ShapeDtypeStruct((rows * len(values), wide), values[0].dtype),
        compiler_params=pltpu.CompilerParams(vmem_limit_bytes=56 * 2**20),
        name="join",
    )(*values)


def merge(values, pieces, kind):
    rows, wide = values[0].shape
    rows = rows // pieces
    kinds = [kind] + [BF] * (pieces - 1)

    def body(*refs):
        for number in range(pieces):
            here = slice(number * rows, (number + 1) * rows)
            total = refs[0][here].astype(F32)
            for ref in refs[1 : len(values)]:
                total = total + ref[here].astype(F32)
            refs[len(values) + number][...] = total.astype(kinds[number])

    return pl.pallas_call(
        body,
        out_shape=[jax.ShapeDtypeStruct((rows, wide), kind) for kind in kinds],
        compiler_params=pltpu.CompilerParams(vmem_limit_bytes=56 * 2**20),
        name="merge",
    )(*values)


def finish_body(number_sent, number_parts, *refs):
    own_ref = refs[0]
    sent_refs = refs[1 : 1 + number_sent]
    grad_ref, weight_ref, pick_ref, route_ref, gate_ref, up_ref, down_ref = refs[
        1 + number_sent : 8 + number_sent
    ]
    hidden_ref, gate_term_ref, up_term_ref = refs[8 + number_sent : 11 + number_sent]
    back_refs = refs[11 + number_sent : 11 + number_sent + number_parts]
    out_acc, in_acc = refs[11 + number_sent + number_parts :]
    step = pl.program_id(0)
    gate_pre, up_pre, hidden_grad = (
        add_all(own_ref[number], [ref[number] for ref in sent_refs]) for number in range(3)
    )
    act_val, act_slope = silu_parts(gate_pre)
    hidden = (act_val * up_pre).astype(BF)
    gate_term = (hidden_grad * up_pre * act_slope).astype(BF)
    up_term = (hidden_grad * act_val).astype(BF)
    hidden_ref[...] = hidden
    gate_term_ref[...] = gate_term
    up_term_ref[...] = up_term
    out_part = dot_nn(hidden, down_ref[...])
    in_part = dot_nt(gate_term, gate_ref[...]) + dot_nt(up_term, up_ref[...])

    @pl.when(step == 0)
    def _():
        out_acc[...] = out_part
        in_acc[...] = in_part

    @pl.when(step > 0)
    def _():
        out_acc[...] += out_part
        in_acc[...] += in_part

    @pl.when(step == pl.num_programs(0) - 1)
    def _():
        part = out_acc.shape[1]
        extra = route_ref.shape[1]
        expert_out = out_acc[...].astype(BF).astype(F32)
        rest = jnp.sum(grad_ref[...].astype(F32) * expert_out, axis=1, keepdims=True)
        route = jnp.zeros((rest.shape[0], extra), F32)
        for number in range(3):
            piece = rest.astype(BF).astype(F32)
            route = route + piece * route_ref[number : number + 1]
            rest = rest - piece
        pick = pick_ref[...]
        weighted = (weight_ref[:, :1] * expert_out).astype(BF)
        backs = (
            dot_tn(pick, weighted).astype(BF),
            dot_tn(pick, route.astype(BF)).astype(BF),
            dot_tn(pick, in_acc[...].astype(BF)).astype(BF),
        )
        rows = back_refs[0].shape[0]
        for number, ref in enumerate(back_refs):
            here = slice(number * rows, (number + 1) * rows)
            ref[:, :part] = backs[0][here]
            ref[:, part : part + extra] = backs[1][here]
            ref[:, part + extra :] = backs[2][here]


def finish(own, sent, grad, weight, pick, route, gate_w, up_w, down_w, number_parts):
    part, hidden = gate_w.shape
    tile = min(256, hidden)
    slots, count = pick.shape
    rows = count // number_parts
    wide = 2 * part + route.shape[1]
    whole = lambda shape: pl.BlockSpec(shape, lambda j: (0,) * len(shape))
    columns = lambda size: pl.BlockSpec((size, tile), lambda j: (0, j))
    stacked = pl.BlockSpec((3, slots, tile), lambda j: (0, 0, j))
    return pl.pallas_call(
        lambda *refs: finish_body(len(sent), number_parts, *refs),
        grid=(hidden // tile,),
        in_specs=[stacked] * (1 + len(sent))
        + [whole(value.shape) for value in (grad, weight, pick, route)]
        + [columns(part), columns(part), pl.BlockSpec((tile, part), lambda j: (j, 0))],
        out_specs=[columns(slots)] * 3 + [whole((rows, wide))] * number_parts,
        out_shape=[jax.ShapeDtypeStruct((slots, hidden), BF)] * 3
        + [jax.ShapeDtypeStruct((rows, wide), BF)] * number_parts,
        scratch_shapes=[pltpu.VMEM((slots, part), F32), pltpu.VMEM((slots, part), F32)],
        compiler_params=pltpu.CompilerParams(vmem_limit_bytes=56 * 2**20),
        name="finish",
    )(own, *sent, grad, weight, pick, route, gate_w, up_w, down_w)


def per_device(tokens, expert_ids, route_weights, out_grad, gate_weight, up_weight, down_weight):
    experts = lax.axis_size("expert")
    groups = lax.axis_size("dp")
    my_expert = lax.axis_index("expert")
    outer, inner, core = factors(experts)
    rows, width = tokens.shape
    hidden_width = gate_weight.shape[2]
    choices = expert_ids.shape[1]
    part = width // groups
    most = min(rows, 3 * rows * choices // (2 * experts))
    extra = -(-3 * experts // 128) * 128
    gate_w, up_w, down_w = gate_weight[0], up_weight[0], down_weight[0]

    chosen = expert_ids[:, :, None] == jnp.arange(experts, dtype=jnp.int32)[None, None, :]
    weight_table = jnp.sum(jnp.where(chosen, route_weights[:, :, None], 0.0), axis=1)
    weight_cols = jnp.concatenate(
        three_pieces(weight_table) + [jnp.zeros((rows, extra - 3 * experts), BF)], axis=1
    )
    payload = jnp.concatenate(
        swap_groups(
            [
                jnp.concatenate(
                    [
                        tokens[:, g * part : (g + 1) * part],
                        out_grad[:, g * part : (g + 1) * part],
                        weight_cols,
                    ],
                    axis=1,
                )
                for g in range(groups)
            ]
        ),
        axis=0,
    )

    column = jnp.arange(extra, dtype=jnp.int32)[None, :]
    mask = jnp.broadcast_to(
        (column % experts == my_expert) & (column < 3 * experts), (8, extra)
    ).astype(BF)
    route_cols = (
        column == jnp.arange(8, dtype=jnp.int32)[:, None] * experts + my_expert
    ) & (jnp.arange(8)[:, None] < 3)
    route_cols = route_cols.astype(F32)
    count = inner * core * groups * rows
    slots = inner * core * groups * most
    token = jnp.arange(count, dtype=jnp.int32)
    block = token // rows
    before = (block[:, None] == block[None, :]) & (token[:, None] <= token[None, :])
    before = before.astype(BF)
    base = jnp.broadcast_to((block * most).astype(F32)[None, :], (8, count))
    order = Order()
    around, picked, sums, ends = {}, {}, {}, {}
    moving, pieces = {}, {0: payload}
    last = outer - 1

    def start_core(number):
        (parts,) = order.enter(around[number])
        rows_here = join(parts)
        order.leave(rows_here)
        around[number] = gather_start(rows_here, 2)

    def start_inner(number):
        (piece,) = order.enter(pieces[number])
        around[number] = gather_start(piece, 1)

    def partial_sums(number):
        (parts,) = order.enter(around[number])
        picked[number] = project(parts, mask, before, base, slots, gate_w, up_w, down_w)
        own, sent = picked[number][5:]
        order.leave(sent)
        sums[number] = (own, exchange(sent))

    def finish_chunk(number):
        own, arrived = order.enter(*sums[number])
        x_rows, grad, term, weight, pick = picked[number][:5]
        results = finish(
            own, arrived, grad, weight, pick, route_cols, gate_w, up_w, down_w, core
        )
        ends[number] = results[:3]
        back = results[3:]
        order.leave(*back)
        moving[number] = (
            back[0],
            [shift_expert(back[step], 2, -step) for step in range(1, core)],
        )

    def next_inner(number):
        total, arrived = order.enter(*moving[number])
        parts = merge([total] + arrived, inner, F32)
        order.leave(*parts)
        moving[number] = (
            parts[0],
            [shift_expert(parts[step], 1, -step) for step in range(1, inner)],
        )

    def next_outer(number):
        total, arrived = order.enter(*moving[number])
        (total,) = merge([total] + arrived, 1, BF if number else F32)
        order.leave(total)
        if number:
            moving[number] = shift_expert(total, 0, -number)
        else:
            finals.append(total)

    def add_final(number):
        arrived, total = order.enter(moving[number], finals[-1])
        (total,) = merge([total, arrived], 1, BF if number == last else F32)
        finals.append(total)
        order.leave(total)

    finals = []
    start_inner(0)
    if outer > 1:
        pieces[1] = shift_expert(payload, 0, 1)
        around[0], pieces[1] = order.enter(around[0], pieces[1])
    start_core(0)
    if outer > 1:
        start_inner(1)
    if outer > 2:
        (tied,) = order.enter(payload)
        pieces[2] = shift_expert(tied, 0, 2)
    partial_sums(0)
    if outer > 1:
        start_core(1)
        partial_sums(1)
    for number in range(outer):
        later = number + 2
        if later < outer:
            start_inner(later)
            if later + 1 < outer:
                (tied,) = order.enter(payload)
                pieces[later + 1] = shift_expert(tied, 0, later + 1)
        finish_chunk(number)
        if number > 0:
            next_inner(number - 1)
        if number > 1:
            next_outer(number - 2)
        if later < outer:
            start_core(later)
            partial_sums(later)

    def rows_all(table, index):
        return jnp.concatenate([table[number][index] for number in range(outer)], axis=0)

    next_inner(last)
    if outer > 1:
        next_outer(last - 1)
    hidden_all, out_all = order.enter(rows_all(ends, 0), rows_all(picked, 2))
    down_grad = dot_tn(hidden_all, out_all).astype(BF)[None]
    order.leave(down_grad)
    next_outer(last)
    for number in range(1, last):
        add_final(number)
    x_all, gate_all, up_all = order.enter(
        rows_all(picked, 0), rows_all(ends, 1), rows_all(ends, 2)
    )
    gate_grad = dot_tn(x_all, gate_all).astype(BF)[None]
    up_grad = dot_tn(x_all, up_all).astype(BF)[None]
    order.leave(gate_grad, up_grad)
    if outer > 1:
        add_final(last)
    final = finals[-1].astype(BF)
    parts = swap_groups([final[g * rows : (g + 1) * rows] for g in range(groups)])
    mixed = jnp.concatenate([value[:, :part] for value in parts], axis=1)
    tokens_grad = jnp.concatenate([value[:, part + extra :] for value in parts], axis=1)
    route_table = jnp.zeros((), F32)
    for value in parts:
        for number in range(3):
            start = part + number * experts
            route_table = route_table + value[:, start : start + experts].astype(F32)
    route_grad = jnp.sum(jnp.where(chosen, route_table[:, None, :], 0.0), axis=2)
    return (mixed, tokens_grad, route_grad, gate_grad, up_grad, down_grad)


def solution(mesh):
    return jax.shard_map(
        per_device,
        mesh=mesh,
        in_specs=(
            P(("dp", "expert"), None),
            P(("dp", "expert"), None),
            P(("dp", "expert"), None),
            P(("dp", "expert"), None),
            P("expert", "dp", None),
            P("expert", "dp", None),
            P("expert", None, "dp"),
        ),
        out_specs=(
            P(("dp", "expert"), None),
            P(("dp", "expert"), None),
            P(("dp", "expert"), None),
            P("expert", "dp", None),
            P("expert", "dp", None),
            P("expert", None, "dp"),
        ),
        check_vma=False,
    )
```

```python
import jax
import jax.numpy as jnp
from jax import lax
from jax.sharding import PartitionSpec as P

BF = jnp.bfloat16
F32 = jnp.float32


def silu_parts(pre_act):
    sigmoid_val = jax.nn.sigmoid(pre_act)
    return (pre_act * sigmoid_val, sigmoid_val * (1.0 + pre_act * (1.0 - sigmoid_val)))


def dot_nn(first, second):
    return lax.dot_general(first, second, (((1,), (0,)), ((), ())), preferred_element_type=F32)


def dot_nt(first, second):
    return lax.dot_general(first, second, (((1,), (1,)), ((), ())), preferred_element_type=F32)


def dot_tn(first, second):
    return lax.dot_general(first, second, (((0,), (0,)), ((), ())), preferred_element_type=F32)


def shift_dp(value, step):
    groups = lax.axis_size("dp")
    return lax.ppermute(value, "dp", [(i, (i + step) % groups) for i in range(groups)])


def choose(parts, index):
    picked = parts[0]
    for number in range(1, len(parts)):
        picked = jnp.where(index == number, parts[number], picked)
    return picked


def swap_groups(parts):
    groups = len(parts)
    mine = lax.axis_index("dp")
    by_step = [choose(parts, mine)]
    for step in range(1, groups):
        by_step.append(shift_dp(choose(parts, (mine + step) % groups), step))
    return [choose(by_step, (mine - group) % groups) for group in range(groups)]


def exchange(sent):
    return [shift_dp(sent, step) for step in range(1, lax.axis_size("dp"))]


def add_all(total, arrived):
    for value in arrived:
        total = total + value.astype(F32)
    return total


class Order:
    def __init__(self):
        self.last = []

    def enter(self, *values):
        flat, tree = jax.tree.flatten(values)
        tied = lax.optimization_barrier(tuple(flat) + tuple(self.last))[: len(flat)]
        return jax.tree.unflatten(tree, tied)

    def leave(self, *values):
        self.last = list(values)


def factors(experts):
    core = 2 if experts % 2 == 0 else 1
    rest = experts // core
    inner = 1
    while rest % (inner * 2) == 0 and (inner * 2) ** 2 <= rest:
        inner = inner * 2
    return (rest // inner, inner, core)


def shift_expert(value, level, step):
    dims = factors(lax.axis_size("expert"))
    stride = 1
    for dim in dims[level + 1 :]:
        stride = stride * dim
    size = dims[level]
    pairs = []
    for source in range(lax.axis_size("expert")):
        place = source // stride % size
        pairs.append((source, source + ((place + step) % size - place) * stride))
    return lax.ppermute(value, "expert", pairs)


def level_size(level):
    return factors(lax.axis_size("expert"))[level]


def gather_start(piece, level):
    return [piece] + [shift_expert(piece, level, step) for step in range(1, level_size(level))]


def three_pieces(value):
    high = lax.reduce_precision(value, 8, 7)
    rest = value - high
    mid = lax.reduce_precision(rest, 8, 7)
    return [high.astype(BF), mid.astype(BF), (rest - mid).astype(BF)]


def pick_rows(parts, weight, most, block_rows):
    count = weight.shape[0]
    blocks = count // block_rows
    live = (weight > 0.0).reshape(blocks, block_rows)
    place = jnp.cumsum(live.astype(jnp.int32), axis=1) - 1
    slot = jnp.where(live, place + most * jnp.arange(blocks, dtype=jnp.int32)[:, None], -1)
    pick = slot.reshape(1, count) == jnp.arange(blocks * most, dtype=jnp.int32)[:, None]
    return pick


def project(parts, weight, most, block_rows, gate_w, up_w, down_w):
    part = gate_w.shape[0]
    pick = pick_rows(parts, weight, most, block_rows)
    weight_rows = jnp.sum(jnp.where(pick, weight[None, :], 0.0), axis=1)
    pick = pick.astype(BF)
    arrived = jnp.concatenate(parts, axis=0)
    picked = dot_nn(pick, arrived[:, : 2 * part]).astype(BF)
    x_rows, grad = picked[:, :part], picked[:, part:]
    term = (weight_rows[:, None] * grad.astype(F32)).astype(BF)
    own = (dot_nn(x_rows, gate_w), dot_nn(x_rows, up_w), dot_nt(term, down_w))
    sent = jnp.concatenate([value.astype(BF) for value in own], axis=1)
    return x_rows, grad, term, weight_rows, pick, own, sent


def finish(own, arrived, grad, weight_rows, pick, route, gate_w, up_w, down_w, number_parts):
    width = own[0].shape[1]
    gate_pre, up_pre, hidden_grad = (
        add_all(own[k], [value[:, k * width : (k + 1) * width] for value in arrived])
        for k in range(3)
    )
    act_val, act_slope = silu_parts(gate_pre)
    hidden = (act_val * up_pre).astype(BF)
    gate_term = (hidden_grad * up_pre * act_slope).astype(BF)
    up_term = (hidden_grad * act_val).astype(BF)
    expert_out = dot_nn(hidden, down_w).astype(BF).astype(F32)
    in_term = (dot_nt(gate_term, gate_w) + dot_nt(up_term, up_w)).astype(BF)
    values = three_pieces(jnp.sum(grad.astype(F32) * expert_out, axis=1))
    route_cols = jnp.zeros((), BF)
    for number in range(3):
        route_cols = jnp.where(
            route[number : number + 1] > 0, values[number][:, None], route_cols
        )
    back = jnp.concatenate(
        [(weight_rows[:, None] * expert_out).astype(BF), route_cols, in_term], axis=1
    )
    dense = dot_tn(pick, back).astype(BF)
    rows = dense.shape[0] // number_parts
    return (hidden, gate_term, up_term) + tuple(
        dense[number * rows : (number + 1) * rows] for number in range(number_parts)
    )


def skip_unless(needed, function, operands, always=lambda: (), others=()):
    shapes = jax.eval_shape(function, *operands)

    def work(operands, others):
        return function(*operands), always(*others)

    def skip(operands, others):
        zeros = jax.tree.map(lambda leaf: jnp.zeros(leaf.shape, leaf.dtype), shapes)
        return zeros, always(*others)

    return lax.cond(needed, work, skip, tuple(operands), tuple(others))


def join(values):
    return jnp.concatenate(values, axis=0)


def merge(values, pieces, kind):
    total = add_all(values[0].astype(F32), values[1:])
    rows = total.shape[0] // pieces
    kinds = [kind] + [BF] * (pieces - 1)
    return [
        total[number * rows : (number + 1) * rows].astype(kinds[number])
        for number in range(pieces)
    ]


def per_device(tokens, expert_ids, route_weights, out_grad, gate_weight, up_weight, down_weight):
    experts = lax.axis_size("expert")
    groups = lax.axis_size("dp")
    my_expert = lax.axis_index("expert")
    outer, inner, core = factors(experts)
    rows, width = tokens.shape
    hidden_width = gate_weight.shape[2]
    choices = expert_ids.shape[1]
    part = width // groups
    most = min(rows, 3 * rows * choices // (2 * experts))
    extra = -(-3 * experts // 128) * 128
    gate_w, up_w, down_w = gate_weight[0], up_weight[0], down_weight[0]

    chosen = expert_ids[:, :, None] == jnp.arange(experts, dtype=jnp.int32)[None, None, :]
    weight_table = jnp.sum(jnp.where(chosen, route_weights[:, :, None], 0.0), axis=1)
    weight_cols = jnp.concatenate(
        three_pieces(weight_table) + [jnp.zeros((rows, extra - 3 * experts), BF)], axis=1
    )
    payload = jnp.concatenate(
        swap_groups(
            [
                jnp.concatenate(
                    [
                        tokens[:, g * part : (g + 1) * part],
                        out_grad[:, g * part : (g + 1) * part],
                        weight_cols,
                    ],
                    axis=1,
                )
                for g in range(groups)
            ]
        ),
        axis=0,
    )

    column = jnp.arange(extra, dtype=jnp.int32)[None, :]
    my_column = (column % experts == my_expert) & (column < 3 * experts)
    route_cols = (
        column == jnp.arange(8, dtype=jnp.int32)[:, None] * experts + my_expert
    ) & (jnp.arange(8)[:, None] < 3)
    route_cols = route_cols.astype(F32)
    order = Order()
    around, picked, sums, ends, needed = {}, {}, {}, {}, {}
    moving, pieces = {}, {0: payload}
    last = outer - 1

    def start_inner(number):
        (piece,) = order.enter(pieces[number])
        around[number] = gather_start(piece, 1)

    def start_outer(number):
        if number < outer:
            (tied,) = order.enter(payload)
            pieces[number] = shift_expert(tied, 0, number)

    def partial_sums(number):
        (parts,) = order.enter(around[number])
        weight = jnp.concatenate(
            [
                jnp.sum(jnp.where(my_column, value[:, 2 * part :].astype(F32), 0.0), axis=1)
                for value in parts
            ]
        )
        needed[number] = jnp.max(weight) > 0.0
        picked[number], _ = skip_unless(
            needed[number],
            lambda *values: project(values[0], values[1], most, rows, *values[2:]),
            (parts, weight, gate_w, up_w, down_w),
        )
        own, sent = picked[number][5:]
        order.leave(sent)
        sums[number] = (own, exchange(sent))

    def moved_sums(joins, inners, outers):
        return (
            [join(values) for values in joins],
            [merge([total] + arrived, inner, F32) for total, arrived in inners],
            [merge([total] + arrived, 1, F32)[0] for total, arrived in outers],
        )

    def start_moves(numbers, moved):
        joined, inners, outers = numbers
        for number, value in zip(joined, moved[0]):
            around[number] = gather_start(value, 2)
        for number, parts in zip(inners, moved[1]):
            moving[number] = (
                parts[0],
                [shift_expert(parts[step], 1, -step) for step in range(1, inner)],
            )
        for number, value in zip(outers, moved[2]):
            finals[number] = (
                shift_expert(value.astype(BF), 0, -number) if number else value
            )

    def finish_chunk(number):
        later = number + 2
        numbers = (
            [later] if later < outer else [],
            [number - 1] if number > 0 else [],
            [number - 2] if number > 1 else [],
        )
        if number == 0 and later < outer:
            start_inner(later)
        own, arrived = order.enter(*sums[number])
        if number > 0 and later < outer:
            order.leave(*arrived)
            start_inner(later)
        grad, term, weight, pick = picked[number][1:5]
        results, moved = skip_unless(
            needed[number],
            lambda *values: finish(*values, core),
            (own, arrived, grad, weight, pick, route_cols, gate_w, up_w, down_w),
            moved_sums,
            (
                [around[k] for k in numbers[0]],
                [moving[k] for k in numbers[1]],
                [moving[k] for k in numbers[2]],
            ),
        )
        ends[number] = results[:3]
        back = results[3:]
        order.leave(*back)
        moving[number] = (
            back[0],
            [shift_expert(back[step], 2, -step) for step in range(1, core)],
        )
        start_moves(numbers, moved)

    def move(joins, inners, outers):
        values = order.enter(
            [around[k] for k in joins], [moving[k] for k in inners], [moving[k] for k in outers]
        )
        moved = moved_sums(*values)
        order.leave(*jax.tree.leaves(moved))
        start_moves((joins, inners, outers), moved)

    finals = {}
    start_inner(0)
    if outer > 1:
        pieces[1] = shift_expert(payload, 0, 1)
        around[0], pieces[1] = order.enter(around[0], pieces[1])
    move([0], [], [])
    if outer > 1:
        start_inner(1)
    start_outer(2)
    partial_sums(0)
    if outer > 1:
        move([1], [], [])
        partial_sums(1)
    start_outer(3)
    for number in range(outer):
        finish_chunk(number)
        if number + 2 < outer:
            partial_sums(number + 2)
            if number + 4 < outer:
                start_outer(number + 4)

    def rows_all(table, index):
        return jnp.concatenate([table[number][index] for number in range(outer)], axis=0)

    move([], [last], [last - 1] if outer > 1 else [])
    hidden_all, out_all = order.enter(rows_all(ends, 0), rows_all(picked, 2))
    down_grad = dot_tn(hidden_all, out_all).astype(BF)[None]
    order.leave(down_grad)
    move([], [], [last])
    x_all, gate_all, up_all = order.enter(
        rows_all(picked, 0), rows_all(ends, 1), rows_all(ends, 2)
    )
    gate_grad = dot_tn(x_all, gate_all).astype(BF)[None]
    up_grad = dot_tn(x_all, up_all).astype(BF)[None]
    order.leave(gate_grad, up_grad)
    (arrived,) = order.enter([finals[number] for number in range(outer)])
    final = add_all(arrived[0].astype(F32), arrived[1:]).astype(BF)
    parts = swap_groups([final[g * rows : (g + 1) * rows] for g in range(groups)])
    mixed = jnp.concatenate([value[:, :part] for value in parts], axis=1)
    tokens_grad = jnp.concatenate([value[:, part + extra :] for value in parts], axis=1)
    route_table = jnp.zeros((), F32)
    for value in parts:
        for number in range(3):
            start = part + number * experts
            route_table = route_table + value[:, start : start + experts].astype(F32)
    route_grad = jnp.sum(jnp.where(chosen, route_table[:, None, :], 0.0), axis=2)
    return (mixed, tokens_grad, route_grad, gate_grad, up_grad, down_grad)


def solution(mesh):
    return jax.shard_map(
        per_device,
        mesh=mesh,
        in_specs=(
            P(("dp", "expert"), None),
            P(("dp", "expert"), None),
            P(("dp", "expert"), None),
            P(("dp", "expert"), None),
            P("expert", "dp", None),
            P("expert", "dp", None),
            P("expert", None, "dp"),
        ),
        out_specs=(
            P(("dp", "expert"), None),
            P(("dp", "expert"), None),
            P(("dp", "expert"), None),
            P("expert", "dp", None),
            P("expert", "dp", None),
            P("expert", None, "dp"),
        ),
        check_vma=False,
    )
```

```python
import jax
import jax.numpy as jnp
from jax import lax
from jax.experimental import pallas as pl
from jax.experimental.pallas import tpu as pltpu
from jax.sharding import PartitionSpec as P

BF = jnp.bfloat16
F32 = jnp.float32


def silu_parts(pre_act):
    sigmoid_val = jax.nn.sigmoid(pre_act)
    return (pre_act * sigmoid_val, sigmoid_val * (1.0 + pre_act * (1.0 - sigmoid_val)))


def dot_nn(first, second):
    return lax.dot_general(first, second, (((1,), (0,)), ((), ())), preferred_element_type=F32)


def dot_nt(first, second):
    return lax.dot_general(first, second, (((1,), (1,)), ((), ())), preferred_element_type=F32)


def dot_tn(first, second):
    return lax.dot_general(first, second, (((0,), (0,)), ((), ())), preferred_element_type=F32)


def shift_dp(value, step):
    groups = lax.axis_size("dp")
    return lax.ppermute(value, "dp", [(i, (i + step) % groups) for i in range(groups)])


def choose(parts, index):
    picked = parts[0]
    for number in range(1, len(parts)):
        picked = jnp.where(index == number, parts[number], picked)
    return picked


def swap_groups(parts):
    groups = len(parts)
    mine = lax.axis_index("dp")
    by_step = [choose(parts, mine)]
    for step in range(1, groups):
        by_step.append(shift_dp(choose(parts, (mine + step) % groups), step))
    return [choose(by_step, (mine - group) % groups) for group in range(groups)]


def exchange(sent):
    return [shift_dp(sent, step) for step in range(1, lax.axis_size("dp"))]


def add_all(total, arrived):
    for value in arrived:
        total = total + value.astype(F32)
    return total


class Order:
    def __init__(self):
        self.last = []

    def enter(self, *values):
        flat, tree = jax.tree.flatten(values)
        tied = lax.optimization_barrier(tuple(flat) + tuple(self.last))[: len(flat)]
        return jax.tree.unflatten(tree, tied)

    def leave(self, *values):
        self.last = list(values)


def factors(experts):
    core = 2 if experts % 2 == 0 else 1
    rest = experts // core
    inner = 1
    while rest % (inner * 2) == 0 and (inner * 2) ** 2 <= rest:
        inner = inner * 2
    return (rest // inner, inner, core)


def shift_expert(value, level, step):
    dims = factors(lax.axis_size("expert"))
    stride = 1
    for dim in dims[level + 1 :]:
        stride = stride * dim
    size = dims[level]
    pairs = []
    for source in range(lax.axis_size("expert")):
        place = source // stride % size
        pairs.append((source, source + ((place + step) % size - place) * stride))
    return lax.ppermute(value, "expert", pairs)


def level_size(level):
    return factors(lax.axis_size("expert"))[level]


def gather_start(piece, level):
    return [piece] + [shift_expert(piece, level, step) for step in range(1, level_size(level))]


def three_pieces(value):
    high = lax.reduce_precision(value, 8, 7)
    rest = value - high
    mid = lax.reduce_precision(rest, 8, 7)
    return [high.astype(BF), mid.astype(BF), (rest - mid).astype(BF)]


def stacked_rows(values):
    return jnp.concatenate(values, axis=0) if len(values) > 1 else values[0]


def project_body(number_parts, part, *refs):
    mask_ref, order_ref, base_ref = refs[:3]
    part_refs = refs[3 : 3 + number_parts]
    gate_ref, up_ref, down_ref = refs[3 + number_parts : 6 + number_parts]
    x_ref, grad_ref, term_ref, weight_ref, pick_ref, own_ref, sent_ref = refs[6 + number_parts :]

    @pl.when(pl.program_id(0) == 0)
    def _():
        slots = x_ref.shape[0]
        arrived = stacked_rows([ref[...] for ref in part_refs])
        count = arrived.shape[0]
        mask = mask_ref[...]
        weight = dot_nt(mask, arrived[:, 2 * part :])
        live = weight > 0.0
        place = dot_nn(jnp.where(live, 1.0, 0.0).astype(BF), order_ref[...])
        slot = jnp.where(live, place - 1.0 + base_ref[...], -1.0)[:1]
        index = lax.broadcasted_iota(jnp.int32, (slots, count), 0).astype(F32)
        pick = jnp.where(index == slot, 1.0, 0.0).astype(BF)
        pick_ref[...] = pick
        x_ref[...] = dot_nn(pick, arrived[:, :part]).astype(BF)
        grad = dot_nn(pick, arrived[:, part : 2 * part])
        grad_ref[...] = grad.astype(BF)
        chosen = dot_nn(pick, arrived[:, 2 * part :]) * mask[:1].astype(F32)
        weight_rows = jnp.sum(chosen, axis=1, keepdims=True)
        weight_ref[...] = jnp.broadcast_to(weight_rows, weight_ref.shape)
        term_ref[...] = (weight_rows * grad).astype(BF)

    x_rows = x_ref[...]
    values = (
        dot_nn(x_rows, gate_ref[...]),
        dot_nn(x_rows, up_ref[...]),
        dot_nt(term_ref[...], down_ref[...]),
    )
    for number, value in enumerate(values):
        own_ref[number] = value
        sent_ref[number] = value.astype(BF)


def project(parts, mask, order, base, slots, gate_w, up_w, down_w):
    part, hidden = gate_w.shape
    tile = min(256, hidden)
    count = sum(value.shape[0] for value in parts)
    whole = lambda shape: pl.BlockSpec(shape, lambda j: (0,) * len(shape))
    columns = lambda rows: pl.BlockSpec((rows, tile), lambda j: (0, j))
    stacked = pl.BlockSpec((3, slots, tile), lambda j: (0, 0, j))
    row_out = jax.ShapeDtypeStruct((slots, part), BF)
    return pl.pallas_call(
        lambda *refs: project_body(len(parts), part, *refs),
        grid=(hidden // tile,),
        in_specs=[whole(mask.shape), whole(order.shape), whole(base.shape)]
        + [whole(value.shape) for value in parts]
        + [columns(part), columns(part), pl.BlockSpec((tile, part), lambda j: (j, 0))],
        out_specs=[whole((slots, part))] * 3
        + [whole((slots, 128)), whole((slots, count)), stacked, stacked],
        out_shape=[row_out] * 3
        + [
            jax.ShapeDtypeStruct((slots, 128), F32),
            jax.ShapeDtypeStruct((slots, count), BF),
            jax.ShapeDtypeStruct((3, slots, hidden), F32),
            jax.ShapeDtypeStruct((3, slots, hidden), BF),
        ],
        compiler_params=pltpu.CompilerParams(vmem_limit_bytes=56 * 2**20),
        name="project",
    )(mask, order, base, *parts, gate_w, up_w, down_w)


def merge(values, pieces):
    total = add_all(values[0].astype(F32), values[1:])
    rows = total.shape[0] // pieces
    parts = [total[number * rows : (number + 1) * rows] for number in range(pieces)]
    return parts[:1] + [part.astype(BF) for part in parts[1:]]


def merge_between(values, pieces):
    rows, wide = values[0].shape
    rows = rows // pieces
    kinds = [F32] + [BF] * (pieces - 1)

    def body(*refs):
        for number in range(pieces):
            here = slice(number * rows, (number + 1) * rows)
            total = add_all(refs[0][here].astype(F32), [ref[here] for ref in refs[1 : len(values)]])
            refs[len(values) + number][...] = total.astype(kinds[number])

    return pl.pallas_call(
        body,
        out_shape=[jax.ShapeDtypeStruct((rows, wide), kind) for kind in kinds],
        compiler_params=pltpu.CompilerParams(vmem_limit_bytes=56 * 2**20),
        name="merge",
    )(*values)


def finish_body(number_sent, number_parts, *refs):
    own_ref = refs[0]
    sent_refs = refs[1 : 1 + number_sent]
    grad_ref, weight_ref, pick_ref, route_ref, gate_ref, up_ref, down_ref = refs[
        1 + number_sent : 8 + number_sent
    ]
    hidden_ref, gate_term_ref, up_term_ref = refs[8 + number_sent : 11 + number_sent]
    back_refs = refs[11 + number_sent : 11 + number_sent + number_parts]
    out_acc, in_acc = refs[11 + number_sent + number_parts :]
    step = pl.program_id(0)
    gate_pre, up_pre, hidden_grad = (
        add_all(own_ref[number], [ref[number] for ref in sent_refs]) for number in range(3)
    )
    act_val, act_slope = silu_parts(gate_pre)
    hidden = (act_val * up_pre).astype(BF)
    gate_term = (hidden_grad * up_pre * act_slope).astype(BF)
    up_term = (hidden_grad * act_val).astype(BF)
    hidden_ref[...] = hidden
    gate_term_ref[...] = gate_term
    up_term_ref[...] = up_term
    out_part = dot_nn(hidden, down_ref[...])
    in_part = dot_nt(gate_term, gate_ref[...]) + dot_nt(up_term, up_ref[...])

    @pl.when(step == 0)
    def _():
        out_acc[...] = out_part
        in_acc[...] = in_part

    @pl.when(step > 0)
    def _():
        out_acc[...] += out_part
        in_acc[...] += in_part

    @pl.when(step == pl.num_programs(0) - 1)
    def _():
        part = out_acc.shape[1]
        extra = route_ref.shape[1]
        expert_out = out_acc[...].astype(BF).astype(F32)
        rest = jnp.sum(grad_ref[...].astype(F32) * expert_out, axis=1, keepdims=True)
        route = jnp.zeros((rest.shape[0], extra), F32)
        for number in range(3):
            piece = rest.astype(BF).astype(F32)
            route = route + piece * route_ref[number : number + 1]
            rest = rest - piece
        pick = pick_ref[...]
        weighted = (weight_ref[:, :1] * expert_out).astype(BF)
        backs = (
            dot_tn(pick, weighted).astype(BF),
            dot_tn(pick, route.astype(BF)).astype(BF),
            dot_tn(pick, in_acc[...].astype(BF)).astype(BF),
        )
        rows = back_refs[0].shape[0]
        for number, ref in enumerate(back_refs):
            here = slice(number * rows, (number + 1) * rows)
            ref[:, :part] = backs[0][here]
            ref[:, part : part + extra] = backs[1][here]
            ref[:, part + extra :] = backs[2][here]


def finish(own, sent, grad, weight, pick, route, gate_w, up_w, down_w, number_parts):
    part, hidden = gate_w.shape
    tile = min(256, hidden)
    slots, count = pick.shape
    rows = count // number_parts
    wide = 2 * part + route.shape[1]
    whole = lambda shape: pl.BlockSpec(shape, lambda j: (0,) * len(shape))
    columns = lambda size: pl.BlockSpec((size, tile), lambda j: (0, j))
    stacked = pl.BlockSpec((3, slots, tile), lambda j: (0, 0, j))
    return pl.pallas_call(
        lambda *refs: finish_body(len(sent), number_parts, *refs),
        grid=(hidden // tile,),
        in_specs=[stacked] * (1 + len(sent))
        + [whole(value.shape) for value in (grad, weight, pick, route)]
        + [columns(part), columns(part), pl.BlockSpec((tile, part), lambda j: (j, 0))],
        out_specs=[columns(slots)] * 3 + [whole((rows, wide))] * number_parts,
        out_shape=[jax.ShapeDtypeStruct((slots, hidden), BF)] * 3
        + [jax.ShapeDtypeStruct((rows, wide), BF)] * number_parts,
        scratch_shapes=[pltpu.VMEM((slots, part), F32), pltpu.VMEM((slots, part), F32)],
        compiler_params=pltpu.CompilerParams(vmem_limit_bytes=56 * 2**20),
        name="finish",
    )(own, *sent, grad, weight, pick, route, gate_w, up_w, down_w)


def per_device(tokens, expert_ids, route_weights, out_grad, gate_weight, up_weight, down_weight):
    experts = lax.axis_size("expert")
    groups = lax.axis_size("dp")
    my_expert = lax.axis_index("expert")
    outer, inner, core = factors(experts)
    rows, width = tokens.shape
    hidden_width = gate_weight.shape[2]
    choices = expert_ids.shape[1]
    part = width // groups
    most = min(rows, 3 * rows * choices // (2 * experts))
    extra = -(-3 * experts // 128) * 128
    gate_w, up_w, down_w = gate_weight[0], up_weight[0], down_weight[0]

    chosen = expert_ids[:, :, None] == jnp.arange(experts, dtype=jnp.int32)[None, None, :]
    weight_table = jnp.sum(jnp.where(chosen, route_weights[:, :, None], 0.0), axis=1)
    weight_cols = jnp.concatenate(
        three_pieces(weight_table) + [jnp.zeros((rows, extra - 3 * experts), BF)], axis=1
    )
    payload = jnp.concatenate(
        swap_groups(
            [
                jnp.concatenate(
                    [
                        tokens[:, g * part : (g + 1) * part],
                        out_grad[:, g * part : (g + 1) * part],
                        weight_cols,
                    ],
                    axis=1,
                )
                for g in range(groups)
            ]
        ),
        axis=0,
    )

    column = jnp.arange(extra, dtype=jnp.int32)[None, :]
    mask = jnp.broadcast_to(
        (column % experts == my_expert) & (column < 3 * experts), (8, extra)
    ).astype(BF)
    route_cols = (
        column == jnp.arange(8, dtype=jnp.int32)[:, None] * experts + my_expert
    ) & (jnp.arange(8)[:, None] < 3)
    route_cols = route_cols.astype(F32)
    if outer > 2:
        chunks = [[0], sorted({1, outer - 1})] + [[step] for step in range(2, outer - 1)]
    else:
        chunks = [[step] for step in range(outer)]
    last = len(chunks) - 1

    def tables(number):
        count = len(chunks[number]) * inner * core * groups * rows
        token = jnp.arange(count, dtype=jnp.int32)
        block = token // rows
        before = (block[:, None] == block[None, :]) & (token[:, None] <= token[None, :])
        base = jnp.broadcast_to((block * most).astype(F32)[None, :], (8, count))
        return before.astype(BF), base

    order = Order()
    rows_of_core, rows_of_inner, picked, sums, ends = {}, {}, {}, {}, {}
    moving, finals, pieces = {}, {}, {0: payload}

    def start_outer(step):
        (tied,) = order.enter(payload)
        pieces[step] = shift_expert(tied, 0, step)

    def start_inner(number):
        rows_of_inner[number] = [gather_start(pieces[step], 1) for step in chunks[number]]
        rows_of_core[number] = [gather_start(pieces[step], 2) for step in chunks[number]]

    def start_core(number):
        for along, across in zip(rows_of_inner[number], rows_of_core[number]):
            sent = [gather_start(value, 2) for value in along[1:]]
            across[:] = [[value] + [other[index] for other in sent] for index, value in enumerate(across)]

    def partial_sums(number):
        (across,) = order.enter(rows_of_core[number])
        parts = [
            value for index in range(core) for piece in across for value in piece[index]
        ]
        before, base = tables(number)
        slots = before.shape[0] // rows * most
        picked[number] = project(parts, mask, before, base, slots, gate_w, up_w, down_w)
        own, sent = picked[number][5:]
        order.leave(sent)
        sums[number] = (own, exchange(sent))

    def finish_chunk(number):
        own, arrived = order.enter(*sums[number])
        x_rows, grad, term, weight, pick = picked[number][:5]
        pieces_here = len(chunks[number])
        results = finish(
            own, arrived, grad, weight, pick, route_cols, gate_w, up_w, down_w, core * pieces_here
        )
        ends[number] = results[:3]
        back = results[3:]
        order.leave(*back)
        moving[number] = [
            (
                back[index],
                [
                    shift_expert(back[step * pieces_here + index], 2, -step)
                    for step in range(1, core)
                ],
            )
            for index in range(pieces_here)
        ]

    def next_inner(number):
        add = merge_between if 0 < number < last else merge
        for index in range(len(chunks[number])):
            mine, arrived = order.enter(*moving[number][index])
            mine, *others = add([mine] + arrived, inner)
            order.leave(mine, *others)
            moving[number][index] = (
                mine,
                [shift_expert(other, 1, -step) for step, other in enumerate(others, 1)],
            )

    def next_outer(number):
        for index, step in enumerate(chunks[number]):
            mine, arrived = order.enter(*moving[number][index])
            (total,) = merge([mine] + arrived, 1)
            if step:
                total = total.astype(BF)
            order.leave(total)
            finals[step] = shift_expert(total, 0, -step) if step else total

    start_inner(0)
    for step in chunks[1] if last else []:
        start_outer(step)
    (rows_of_inner[0],) = order.enter(rows_of_inner[0])
    start_core(0)
    if last:
        tied, rows_of_core[0] = order.enter([pieces[step] for step in chunks[1]], rows_of_core[0])
        pieces.update(zip(chunks[1], tied))
        start_inner(1)
    partial_sums(0)
    if last:
        (rows_of_inner[1],) = order.enter(rows_of_inner[1])
        start_core(1)
        for number in range(2, last + 1):
            for step in chunks[number]:
                start_outer(step)
        partial_sums(1)
    for number in range(last + 1):
        later = number + 2
        if later <= last:
            arrived, tied = order.enter(sums[number][1], [pieces[step] for step in chunks[later]])
            sums[number] = (sums[number][0], arrived)
            pieces.update(zip(chunks[later], tied))
            start_inner(later)
        finish_chunk(number)
        if later <= last:
            (rows_of_inner[later],) = order.enter(rows_of_inner[later])
            start_core(later)
            partial_sums(later)
        if 0 < number == last:
            for earlier in range(last):
                next_outer(earlier)
        next_inner(number)

    def rows_of(table, index):
        return [table[number][index] for number in range(last + 1)]

    def joined(values):
        return jnp.concatenate(values, axis=0)

    hidden_all, out_all = order.enter(rows_of(ends, 0), rows_of(picked, 2))
    down_grad = dot_tn(joined(hidden_all), joined(out_all)).astype(BF)[None]
    order.leave(down_grad)
    next_outer(last)
    x_all, gate_all, up_all = order.enter(
        rows_of(picked, 0), rows_of(ends, 1), rows_of(ends, 2)
    )
    x_all = joined(x_all)
    gate_grad = dot_tn(x_all, joined(gate_all)).astype(BF)[None]
    up_grad = dot_tn(x_all, joined(up_all)).astype(BF)[None]
    order.leave(gate_grad, up_grad)
    (arrived,) = order.enter([finals[step] for step in range(outer)])
    final = add_all(arrived[0].astype(F32), arrived[1:]).astype(BF)
    parts = swap_groups([final[g * rows : (g + 1) * rows] for g in range(groups)])
    mixed = jnp.concatenate([value[:, :part] for value in parts], axis=1)
    tokens_grad = jnp.concatenate([value[:, part + extra :] for value in parts], axis=1)
    route_table = jnp.zeros((), F32)
    for value in parts:
        for number in range(3):
            start = part + number * experts
            route_table = route_table + value[:, start : start + experts].astype(F32)
    route_grad = jnp.sum(jnp.where(chosen, route_table[:, None, :], 0.0), axis=2)
    return (mixed, tokens_grad, route_grad, gate_grad, up_grad, down_grad)


def solution(mesh):
    return jax.shard_map(
        per_device,
        mesh=mesh,
        in_specs=(
            P(("dp", "expert"), None),
            P(("dp", "expert"), None),
            P(("dp", "expert"), None),
            P(("dp", "expert"), None),
            P("expert", "dp", None),
            P("expert", "dp", None),
            P("expert", None, "dp"),
        ),
        out_specs=(
            P(("dp", "expert"), None),
            P(("dp", "expert"), None),
            P(("dp", "expert"), None),
            P("expert", "dp", None),
            P("expert", "dp", None),
            P("expert", None, "dp"),
        ),
        check_vma=False,
    )
```

```python
import jax
import jax.numpy as jnp
from jax import lax
from jax.experimental import pallas as pl
from jax.experimental.pallas import tpu as pltpu
from jax.sharding import PartitionSpec as P

BF = jnp.bfloat16
F32 = jnp.float32


def silu_parts(pre_act):
    sigmoid_val = jax.nn.sigmoid(pre_act)
    return (pre_act * sigmoid_val, sigmoid_val * (1.0 + pre_act * (1.0 - sigmoid_val)))


def dot_nn(first, second):
    return lax.dot_general(first, second, (((1,), (0,)), ((), ())), preferred_element_type=F32)


def dot_nt(first, second):
    return lax.dot_general(first, second, (((1,), (1,)), ((), ())), preferred_element_type=F32)


def dot_tn(first, second):
    return lax.dot_general(first, second, (((0,), (0,)), ((), ())), preferred_element_type=F32)


def shift_dp(value, step):
    groups = lax.axis_size("dp")
    return lax.ppermute(value, "dp", [(i, (i + step) % groups) for i in range(groups)])


def choose(parts, index):
    picked = parts[0]
    for number in range(1, len(parts)):
        picked = jnp.where(index == number, parts[number], picked)
    return picked


def swap_groups(parts):
    groups = len(parts)
    mine = lax.axis_index("dp")
    by_step = [choose(parts, mine)]
    for step in range(1, groups):
        by_step.append(shift_dp(choose(parts, (mine + step) % groups), step))
    return [choose(by_step, (mine - group) % groups) for group in range(groups)]


def exchange(sent):
    return [shift_dp(sent, step) for step in range(1, lax.axis_size("dp"))]


def add_all(total, arrived):
    for value in arrived:
        total = total + value.astype(F32)
    return total


class Order:
    def __init__(self):
        self.last = []

    def enter(self, *values):
        flat, tree = jax.tree.flatten(values)
        tied = lax.optimization_barrier(tuple(flat) + tuple(self.last))[: len(flat)]
        return jax.tree.unflatten(tree, tied)

    def leave(self, *values):
        self.last = list(values)


def factors(experts):
    core = 2 if experts % 2 == 0 else 1
    rest = experts // core
    inner = 1
    while rest % (inner * 2) == 0 and (inner * 2) ** 2 <= rest:
        inner = inner * 2
    return (rest // inner, inner, core)


def shift_expert(value, level, step):
    dims = factors(lax.axis_size("expert"))
    stride = 1
    for dim in dims[level + 1 :]:
        stride = stride * dim
    size = dims[level]
    pairs = []
    for source in range(lax.axis_size("expert")):
        place = source // stride % size
        pairs.append((source, source + ((place + step) % size - place) * stride))
    return lax.ppermute(value, "expert", pairs)


def shift_both(value, outer_step, inner_step):
    outer, inner, core = factors(lax.axis_size("expert"))
    pairs = []
    for source in range(outer * inner * core):
        place_outer, place_inner = source // (inner * core), source // core % inner
        target = (place_outer + outer_step) % outer * inner + (place_inner + inner_step) % inner
        pairs.append((source, target * core + source % core))
    return lax.ppermute(value, "expert", pairs)


def level_size(level):
    return factors(lax.axis_size("expert"))[level]


def gather_start(piece, level):
    return [piece] + [shift_expert(piece, level, step) for step in range(1, level_size(level))]


def three_pieces(value):
    high = lax.reduce_precision(value, 8, 7)
    rest = value - high
    mid = lax.reduce_precision(rest, 8, 7)
    return [high.astype(BF), mid.astype(BF), (rest - mid).astype(BF)]


def stacked_rows(values):
    return jnp.concatenate(values, axis=0) if len(values) > 1 else values[0]


def project_body(number_parts, part, *refs):
    mask_ref, order_ref, base_ref = refs[:3]
    part_refs = refs[3 : 3 + number_parts]
    gate_ref, up_ref, down_ref = refs[3 + number_parts : 6 + number_parts]
    x_ref, grad_ref, term_ref, weight_ref, pick_ref, own_ref, sent_ref = refs[6 + number_parts :]

    @pl.when(pl.program_id(0) == 0)
    def _():
        slots = x_ref.shape[0]
        arrived = stacked_rows([ref[...] for ref in part_refs])
        count = arrived.shape[0]
        mask = mask_ref[...]
        weight = dot_nt(mask, arrived[:, 2 * part :])
        live = weight > 0.0
        place = dot_nn(jnp.where(live, 1.0, 0.0).astype(BF), order_ref[...])
        slot = jnp.where(live, place - 1.0 + base_ref[...], -1.0)[:1]
        index = lax.broadcasted_iota(jnp.int32, (slots, count), 0).astype(F32)
        pick = jnp.where(index == slot, 1.0, 0.0).astype(BF)
        pick_ref[...] = pick
        x_ref[...] = dot_nn(pick, arrived[:, :part]).astype(BF)
        grad = dot_nn(pick, arrived[:, part : 2 * part])
        grad_ref[...] = grad.astype(BF)
        chosen = dot_nn(pick, arrived[:, 2 * part :]) * mask[:1].astype(F32)
        weight_rows = jnp.sum(chosen, axis=1, keepdims=True)
        weight_ref[...] = jnp.broadcast_to(weight_rows, weight_ref.shape)
        term_ref[...] = (weight_rows * grad).astype(BF)

    x_rows = x_ref[...]
    values = (
        dot_nn(x_rows, gate_ref[...]),
        dot_nn(x_rows, up_ref[...]),
        dot_nt(term_ref[...], down_ref[...]),
    )
    for number, value in enumerate(values):
        own_ref[number] = value
        sent_ref[number] = value.astype(BF)


def project(parts, mask, order, base, slots, gate_w, up_w, down_w):
    part, hidden = gate_w.shape
    tile = min(256, hidden)
    count = sum(value.shape[0] for value in parts)
    whole = lambda shape: pl.BlockSpec(shape, lambda j: (0,) * len(shape))
    columns = lambda rows: pl.BlockSpec((rows, tile), lambda j: (0, j))
    stacked = pl.BlockSpec((3, slots, tile), lambda j: (0, 0, j))
    row_out = jax.ShapeDtypeStruct((slots, part), BF)
    return pl.pallas_call(
        lambda *refs: project_body(len(parts), part, *refs),
        grid=(hidden // tile,),
        in_specs=[whole(mask.shape), whole(order.shape), whole(base.shape)]
        + [whole(value.shape) for value in parts]
        + [columns(part), columns(part), pl.BlockSpec((tile, part), lambda j: (j, 0))],
        out_specs=[whole((slots, part))] * 3
        + [whole((slots, 128)), whole((slots, count)), stacked, stacked],
        out_shape=[row_out] * 3
        + [
            jax.ShapeDtypeStruct((slots, 128), F32),
            jax.ShapeDtypeStruct((slots, count), BF),
            jax.ShapeDtypeStruct((3, slots, hidden), F32),
            jax.ShapeDtypeStruct((3, slots, hidden), BF),
        ],
        compiler_params=pltpu.CompilerParams(vmem_limit_bytes=56 * 2**20),
        name="project",
    )(mask, order, base, *parts, gate_w, up_w, down_w)


def merge(values, pieces):
    total = add_all(values[0].astype(F32), values[1:])
    rows = total.shape[0] // pieces
    parts = [total[number * rows : (number + 1) * rows] for number in range(pieces)]
    return parts[:1] + [part.astype(BF) for part in parts[1:]]


def merge_between(values, pieces):
    rows, wide = values[0].shape
    rows = rows // pieces
    kinds = [F32] + [BF] * (pieces - 1)

    def body(*refs):
        for number in range(pieces):
            here = slice(number * rows, (number + 1) * rows)
            total = add_all(refs[0][here].astype(F32), [ref[here] for ref in refs[1 : len(values)]])
            refs[len(values) + number][...] = total.astype(kinds[number])

    return pl.pallas_call(
        body,
        out_shape=[jax.ShapeDtypeStruct((rows, wide), kind) for kind in kinds],
        compiler_params=pltpu.CompilerParams(vmem_limit_bytes=56 * 2**20),
        name="merge",
    )(*values)


def finish_body(number_sent, number_parts, *refs):
    own_ref = refs[0]
    sent_refs = refs[1 : 1 + number_sent]
    grad_ref, weight_ref, pick_ref, route_ref, gate_ref, up_ref, down_ref = refs[
        1 + number_sent : 8 + number_sent
    ]
    hidden_ref, gate_term_ref, up_term_ref = refs[8 + number_sent : 11 + number_sent]
    back_refs = refs[11 + number_sent : 11 + number_sent + number_parts]
    out_acc, in_acc = refs[11 + number_sent + number_parts :]
    step = pl.program_id(0)
    gate_pre, up_pre, hidden_grad = (
        add_all(own_ref[number], [ref[number] for ref in sent_refs]) for number in range(3)
    )
    act_val, act_slope = silu_parts(gate_pre)
    hidden = (act_val * up_pre).astype(BF)
    gate_term = (hidden_grad * up_pre * act_slope).astype(BF)
    up_term = (hidden_grad * act_val).astype(BF)
    hidden_ref[...] = hidden
    gate_term_ref[...] = gate_term
    up_term_ref[...] = up_term
    out_part = dot_nn(hidden, down_ref[...])
    in_part = dot_nt(gate_term, gate_ref[...]) + dot_nt(up_term, up_ref[...])

    @pl.when(step == 0)
    def _():
        out_acc[...] = out_part
        in_acc[...] = in_part

    @pl.when(step > 0)
    def _():
        out_acc[...] += out_part
        in_acc[...] += in_part

    @pl.when(step == pl.num_programs(0) - 1)
    def _():
        part = out_acc.shape[1]
        extra = route_ref.shape[1]
        expert_out = out_acc[...].astype(BF).astype(F32)
        rest = jnp.sum(grad_ref[...].astype(F32) * expert_out, axis=1, keepdims=True)
        route = jnp.zeros((rest.shape[0], extra), F32)
        for number in range(3):
            piece = rest.astype(BF).astype(F32)
            route = route + piece * route_ref[number : number + 1]
            rest = rest - piece
        pick = pick_ref[...]
        weighted = (weight_ref[:, :1] * expert_out).astype(BF)
        backs = (
            dot_tn(pick, weighted).astype(BF),
            dot_tn(pick, route.astype(BF)).astype(BF),
            dot_tn(pick, in_acc[...].astype(BF)).astype(BF),
        )
        rows = back_refs[0].shape[0]
        for number, ref in enumerate(back_refs):
            here = slice(number * rows, (number + 1) * rows)
            ref[:, :part] = backs[0][here]
            ref[:, part : part + extra] = backs[1][here]
            ref[:, part + extra :] = backs[2][here]


def finish(own, sent, grad, weight, pick, route, gate_w, up_w, down_w, number_parts):
    part, hidden = gate_w.shape
    tile = min(256, hidden)
    slots, count = pick.shape
    rows = count // number_parts
    wide = 2 * part + route.shape[1]
    whole = lambda shape: pl.BlockSpec(shape, lambda j: (0,) * len(shape))
    columns = lambda size: pl.BlockSpec((size, tile), lambda j: (0, j))
    stacked = pl.BlockSpec((3, slots, tile), lambda j: (0, 0, j))
    return pl.pallas_call(
        lambda *refs: finish_body(len(sent), number_parts, *refs),
        grid=(hidden // tile,),
        in_specs=[stacked] * (1 + len(sent))
        + [whole(value.shape) for value in (grad, weight, pick, route)]
        + [columns(part), columns(part), pl.BlockSpec((tile, part), lambda j: (j, 0))],
        out_specs=[columns(slots)] * 3 + [whole((rows, wide))] * number_parts,
        out_shape=[jax.ShapeDtypeStruct((slots, hidden), BF)] * 3
        + [jax.ShapeDtypeStruct((rows, wide), BF)] * number_parts,
        scratch_shapes=[pltpu.VMEM((slots, part), F32), pltpu.VMEM((slots, part), F32)],
        compiler_params=pltpu.CompilerParams(vmem_limit_bytes=56 * 2**20),
        name="finish",
    )(own, *sent, grad, weight, pick, route, gate_w, up_w, down_w)


def per_device(tokens, expert_ids, route_weights, out_grad, gate_weight, up_weight, down_weight):
    experts = lax.axis_size("expert")
    groups = lax.axis_size("dp")
    my_expert = lax.axis_index("expert")
    outer, inner, core = factors(experts)
    rows, width = tokens.shape
    hidden_width = gate_weight.shape[2]
    choices = expert_ids.shape[1]
    part = width // groups
    most = min(rows, 3 * rows * choices // (2 * experts))
    extra = -(-3 * experts // 128) * 128
    gate_w, up_w, down_w = gate_weight[0], up_weight[0], down_weight[0]

    chosen = expert_ids[:, :, None] == jnp.arange(experts, dtype=jnp.int32)[None, None, :]
    weight_table = jnp.sum(jnp.where(chosen, route_weights[:, :, None], 0.0), axis=1)
    weight_cols = jnp.concatenate(
        three_pieces(weight_table) + [jnp.zeros((rows, extra - 3 * experts), BF)], axis=1
    )
    payload = jnp.concatenate(
        swap_groups(
            [
                jnp.concatenate(
                    [
                        tokens[:, g * part : (g + 1) * part],
                        out_grad[:, g * part : (g + 1) * part],
                        weight_cols,
                    ],
                    axis=1,
                )
                for g in range(groups)
            ]
        ),
        axis=0,
    )

    column = jnp.arange(extra, dtype=jnp.int32)[None, :]
    mask = jnp.broadcast_to(
        (column % experts == my_expert) & (column < 3 * experts), (8, extra)
    ).astype(BF)
    route_cols = (
        column == jnp.arange(8, dtype=jnp.int32)[:, None] * experts + my_expert
    ) & (jnp.arange(8)[:, None] < 3)
    route_cols = route_cols.astype(F32)
    last = outer - 1
    count = inner * core * groups * rows
    slots = inner * core * groups * most
    token = jnp.arange(count, dtype=jnp.int32)
    block = token // rows
    before = (block[:, None] == block[None, :]) & (token[:, None] <= token[None, :])
    tables = (mask, before.astype(BF), jnp.broadcast_to((block * most).astype(F32)[None], (8, count)))
    order = Order()
    pieces, around, picked, sums, ends = {}, {}, {}, {}, {}
    moving, finals = {}, {}

    def start_pieces(number):
        (tied,) = order.enter(payload)
        pieces[number] = [shift_both(tied, number, step) for step in range(inner)]

    def start_core(number):
        (mine,) = order.enter(pieces[number])
        order.leave(*mine)
        around[number] = [gather_start(value, 2) for value in mine]

    def partial_sums(number):
        (across,) = order.enter(around[number])
        parts = [piece[index] for index in range(core) for piece in across]
        picked[number] = project(parts, *tables, slots, gate_w, up_w, down_w)
        own, sent = picked[number][5:]
        order.leave(sent)
        sums[number] = (own, exchange(sent))

    def finish_chunk(number):
        own, arrived = order.enter(*sums[number])
        x_rows, grad, term, weight, pick = picked[number][:5]
        results = finish(
            own, arrived, grad, weight, pick, route_cols, gate_w, up_w, down_w, core
        )
        ends[number] = results[:3]
        back = results[3:]
        order.leave(*back)
        moving[number] = (
            back[0],
            [shift_expert(back[step], 2, -step) for step in range(1, core)],
        )

    def next_inner(number):
        mine, arrived = order.enter(*moving[number])
        mine, *others = (merge if number == last else merge_between)([mine] + arrived, inner)
        order.leave(mine, *others)
        moving[number] = (
            mine,
            [shift_expert(other, 1, -step) for step, other in enumerate(others, 1)],
        )

    def next_outer(number):
        mine, arrived = order.enter(*moving[number])
        (total,) = merge([mine] + arrived, 1)
        if number:
            total = total.astype(BF)
        order.leave(total)
        finals[number] = shift_expert(total, 0, -number) if number else total

    own_rows = gather_start(payload, 1)
    own_across = gather_start(payload, 2)
    if last:
        pieces[1] = [shift_both(payload, 1, step) for step in range(inner)]
    own_rows, tables = order.enter(own_rows, tables)
    order.leave(*own_rows)
    around[0] = [own_across] + [gather_start(value, 2) for value in own_rows[1:]]
    partial_sums(0)
    if last:
        start_core(1)
        if last > 1:
            start_pieces(2)
        partial_sums(1)
    for number in range(last + 1):
        later = number + 2
        finish_chunk(number)
        if later <= last:
            start_core(later)
            if later < last:
                start_pieces(later + 1)
            partial_sums(later)
        if number < last:
            next_inner(number)
    for number in range(1, last):
        next_outer(number)
    next_inner(last)
    if last > 0:
        next_outer(0)

    def rows_of(table, index):
        return [table[number][index] for number in range(last + 1)]

    def joined(values):
        return jnp.concatenate(values, axis=0)

    hidden_all, out_all = order.enter(rows_of(ends, 0), rows_of(picked, 2))
    down_grad = dot_tn(joined(hidden_all), joined(out_all)).astype(BF)[None]
    order.leave(down_grad)
    next_outer(last)
    x_all, gate_all, up_all = order.enter(
        rows_of(picked, 0), rows_of(ends, 1), rows_of(ends, 2)
    )
    x_all = joined(x_all)
    gate_grad = dot_tn(x_all, joined(gate_all)).astype(BF)[None]
    up_grad = dot_tn(x_all, joined(up_all)).astype(BF)[None]
    order.leave(gate_grad, up_grad)
    (arrived,) = order.enter([finals[step] for step in range(outer)])
    final = add_all(arrived[0].astype(F32), arrived[1:]).astype(BF)
    parts = swap_groups([final[g * rows : (g + 1) * rows] for g in range(groups)])
    mixed = jnp.concatenate([value[:, :part] for value in parts], axis=1)
    tokens_grad = jnp.concatenate([value[:, part + extra :] for value in parts], axis=1)
    route_table = jnp.zeros((), F32)
    for value in parts:
        for number in range(3):
            start = part + number * experts
            route_table = route_table + value[:, start : start + experts].astype(F32)
    route_grad = jnp.sum(jnp.where(chosen, route_table[:, None, :], 0.0), axis=2)
    return (mixed, tokens_grad, route_grad, gate_grad, up_grad, down_grad)


def solution(mesh):
    return jax.shard_map(
        per_device,
        mesh=mesh,
        in_specs=(
            P(("dp", "expert"), None),
            P(("dp", "expert"), None),
            P(("dp", "expert"), None),
            P(("dp", "expert"), None),
            P("expert", "dp", None),
            P("expert", "dp", None),
            P("expert", None, "dp"),
        ),
        out_specs=(
            P(("dp", "expert"), None),
            P(("dp", "expert"), None),
            P(("dp", "expert"), None),
            P("expert", "dp", None),
            P("expert", "dp", None),
            P("expert", None, "dp"),
        ),
        check_vma=False,
    )
```

```python
import jax
import jax.numpy as jnp
from jax import lax
from jax.experimental import pallas as pl
from jax.experimental.pallas import tpu as pltpu
from jax.sharding import PartitionSpec as P

BF = jnp.bfloat16
F32 = jnp.float32


def silu_parts(pre_act):
    sigmoid_val = jax.nn.sigmoid(pre_act)
    return (pre_act * sigmoid_val, sigmoid_val * (1.0 + pre_act * (1.0 - sigmoid_val)))


def dot_nn(first, second):
    return lax.dot_general(first, second, (((1,), (0,)), ((), ())), preferred_element_type=F32)


def dot_nt(first, second):
    return lax.dot_general(first, second, (((1,), (1,)), ((), ())), preferred_element_type=F32)


def dot_tn(first, second):
    return lax.dot_general(first, second, (((0,), (0,)), ((), ())), preferred_element_type=F32)


def shift_dp(value, step):
    groups = lax.axis_size("dp")
    return lax.ppermute(value, "dp", [(i, (i + step) % groups) for i in range(groups)])


def choose(parts, index):
    picked = parts[0]
    for number in range(1, len(parts)):
        picked = jnp.where(index == number, parts[number], picked)
    return picked


def swap_groups(parts):
    groups = len(parts)
    mine = lax.axis_index("dp")
    by_step = [choose(parts, mine)]
    for step in range(1, groups):
        by_step.append(shift_dp(choose(parts, (mine + step) % groups), step))
    return [choose(by_step, (mine - group) % groups) for group in range(groups)]


def exchange(sent):
    return [shift_dp(sent, step) for step in range(1, lax.axis_size("dp"))]


def add_all(total, arrived):
    for value in arrived:
        total = total + value.astype(F32)
    return total


class Order:
    def __init__(self):
        self.last = []

    def enter(self, *values):
        flat, tree = jax.tree.flatten(values)
        tied = lax.optimization_barrier(tuple(flat) + tuple(self.last))[: len(flat)]
        return jax.tree.unflatten(tree, tied)

    def leave(self, *values):
        self.last = list(values)


def factors(experts):
    core = 2 if experts % 2 == 0 else 1
    rest = experts // core
    inner = 1
    while rest % (inner * 2) == 0 and (inner * 2) ** 2 <= rest:
        inner = inner * 2
    return (rest // inner, inner, core)


def shift_expert(value, level, step):
    dims = factors(lax.axis_size("expert"))
    stride = 1
    for dim in dims[level + 1 :]:
        stride = stride * dim
    size = dims[level]
    pairs = []
    for source in range(lax.axis_size("expert")):
        place = source // stride % size
        pairs.append((source, source + ((place + step) % size - place) * stride))
    return lax.ppermute(value, "expert", pairs)


def level_size(level):
    return factors(lax.axis_size("expert"))[level]


def gather_start(piece, level):
    return [piece] + [shift_expert(piece, level, step) for step in range(1, level_size(level))]


def three_pieces(value):
    high = lax.reduce_precision(value, 8, 7)
    rest = value - high
    mid = lax.reduce_precision(rest, 8, 7)
    return [high.astype(BF), mid.astype(BF), (rest - mid).astype(BF)]


def stacked_rows(values):
    return jnp.concatenate(values, axis=0) if len(values) > 1 else values[0]


def project_body(number_parts, part, *refs):
    mask_ref, order_ref, base_ref = refs[:3]
    part_refs = refs[3 : 3 + number_parts]
    gate_ref, up_ref, down_ref = refs[3 + number_parts : 6 + number_parts]
    x_ref, grad_ref, term_ref, weight_ref, pick_ref, own_ref, sent_ref = refs[6 + number_parts :]

    @pl.when(pl.program_id(0) == 0)
    def _():
        slots = x_ref.shape[0]
        arrived = stacked_rows([ref[...] for ref in part_refs])
        count = arrived.shape[0]
        mask = mask_ref[...]
        weight = dot_nt(mask, arrived[:, 2 * part :])
        live = weight > 0.0
        place = dot_nn(jnp.where(live, 1.0, 0.0).astype(BF), order_ref[...])
        slot = jnp.where(live, place - 1.0 + base_ref[...], -1.0)[:1]
        index = lax.broadcasted_iota(jnp.int32, (slots, count), 0).astype(F32)
        pick = jnp.where(index == slot, 1.0, 0.0).astype(BF)
        pick_ref[...] = pick
        x_ref[...] = dot_nn(pick, arrived[:, :part]).astype(BF)
        grad = dot_nn(pick, arrived[:, part : 2 * part])
        grad_ref[...] = grad.astype(BF)
        chosen = dot_nn(pick, arrived[:, 2 * part :]) * mask[:1].astype(F32)
        weight_rows = jnp.sum(chosen, axis=1, keepdims=True)
        weight_ref[...] = jnp.broadcast_to(weight_rows, weight_ref.shape)
        term_ref[...] = (weight_rows * grad).astype(BF)

    x_rows = x_ref[...]
    values = (
        dot_nn(x_rows, gate_ref[...]),
        dot_nn(x_rows, up_ref[...]),
        dot_nt(term_ref[...], down_ref[...]),
    )
    for number, value in enumerate(values):
        own_ref[number] = value
        sent_ref[number] = value.astype(BF)


def project(parts, mask, order, base, slots, gate_w, up_w, down_w):
    part, hidden = gate_w.shape
    tile = min(256, hidden)
    count = sum(value.shape[0] for value in parts)
    whole = lambda shape: pl.BlockSpec(shape, lambda j: (0,) * len(shape))
    columns = lambda rows: pl.BlockSpec((rows, tile), lambda j: (0, j))
    stacked = pl.BlockSpec((3, slots, tile), lambda j: (0, 0, j))
    row_out = jax.ShapeDtypeStruct((slots, part), BF)
    return pl.pallas_call(
        lambda *refs: project_body(len(parts), part, *refs),
        grid=(hidden // tile,),
        in_specs=[whole(mask.shape), whole(order.shape), whole(base.shape)]
        + [whole(value.shape) for value in parts]
        + [columns(part), columns(part), pl.BlockSpec((tile, part), lambda j: (j, 0))],
        out_specs=[whole((slots, part))] * 3
        + [whole((slots, 128)), whole((slots, count)), stacked, stacked],
        out_shape=[row_out] * 3
        + [
            jax.ShapeDtypeStruct((slots, 128), F32),
            jax.ShapeDtypeStruct((slots, count), BF),
            jax.ShapeDtypeStruct((3, slots, hidden), F32),
            jax.ShapeDtypeStruct((3, slots, hidden), BF),
        ],
        compiler_params=pltpu.CompilerParams(vmem_limit_bytes=56 * 2**20),
        name="project",
    )(mask, order, base, *parts, gate_w, up_w, down_w)


def merge(values, pieces):
    total = add_all(values[0].astype(F32), values[1:])
    rows = total.shape[0] // pieces
    parts = [total[number * rows : (number + 1) * rows] for number in range(pieces)]
    return parts[:1] + [part.astype(BF) for part in parts[1:]]


def merge_between(values, pieces):
    rows, wide = values[0].shape
    rows = rows // pieces
    kinds = [F32] + [BF] * (pieces - 1)

    def body(*refs):
        for number in range(pieces):
            here = slice(number * rows, (number + 1) * rows)
            total = add_all(refs[0][here].astype(F32), [ref[here] for ref in refs[1 : len(values)]])
            refs[len(values) + number][...] = total.astype(kinds[number])

    return pl.pallas_call(
        body,
        out_shape=[jax.ShapeDtypeStruct((rows, wide), kind) for kind in kinds],
        compiler_params=pltpu.CompilerParams(vmem_limit_bytes=56 * 2**20),
        name="merge",
    )(*values)


def finish_body(number_sent, number_parts, *refs):
    own_ref = refs[0]
    sent_refs = refs[1 : 1 + number_sent]
    grad_ref, weight_ref, pick_ref, route_ref, gate_ref, up_ref, down_ref = refs[
        1 + number_sent : 8 + number_sent
    ]
    hidden_ref, gate_term_ref, up_term_ref = refs[8 + number_sent : 11 + number_sent]
    back_refs = refs[11 + number_sent : 11 + number_sent + number_parts]
    out_acc, in_acc = refs[11 + number_sent + number_parts :]
    step = pl.program_id(0)
    gate_pre, up_pre, hidden_grad = (
        add_all(own_ref[number], [ref[number] for ref in sent_refs]) for number in range(3)
    )
    act_val, act_slope = silu_parts(gate_pre)
    hidden = (act_val * up_pre).astype(BF)
    gate_term = (hidden_grad * up_pre * act_slope).astype(BF)
    up_term = (hidden_grad * act_val).astype(BF)
    hidden_ref[...] = hidden
    gate_term_ref[...] = gate_term
    up_term_ref[...] = up_term
    out_part = dot_nn(hidden, down_ref[...])
    in_part = dot_nt(gate_term, gate_ref[...]) + dot_nt(up_term, up_ref[...])

    @pl.when(step == 0)
    def _():
        out_acc[...] = out_part
        in_acc[...] = in_part

    @pl.when(step > 0)
    def _():
        out_acc[...] += out_part
        in_acc[...] += in_part

    @pl.when(step == pl.num_programs(0) - 1)
    def _():
        part = out_acc.shape[1]
        extra = route_ref.shape[1]
        expert_out = out_acc[...].astype(BF).astype(F32)
        rest = jnp.sum(grad_ref[...].astype(F32) * expert_out, axis=1, keepdims=True)
        route = jnp.zeros((rest.shape[0], extra), F32)
        for number in range(3):
            piece = rest.astype(BF).astype(F32)
            route = route + piece * route_ref[number : number + 1]
            rest = rest - piece
        pick = pick_ref[...]
        weighted = (weight_ref[:, :1] * expert_out).astype(BF)
        backs = (
            dot_tn(pick, weighted).astype(BF),
            dot_tn(pick, route.astype(BF)).astype(BF),
            dot_tn(pick, in_acc[...].astype(BF)).astype(BF),
        )
        rows = back_refs[0].shape[0]
        for number, ref in enumerate(back_refs):
            here = slice(number * rows, (number + 1) * rows)
            ref[:, :part] = backs[0][here]
            ref[:, part : part + extra] = backs[1][here]
            ref[:, part + extra :] = backs[2][here]


def finish(own, sent, grad, weight, pick, route, gate_w, up_w, down_w, number_parts):
    part, hidden = gate_w.shape
    tile = min(256, hidden)
    slots, count = pick.shape
    rows = count // number_parts
    wide = 2 * part + route.shape[1]
    whole = lambda shape: pl.BlockSpec(shape, lambda j: (0,) * len(shape))
    columns = lambda size: pl.BlockSpec((size, tile), lambda j: (0, j))
    stacked = pl.BlockSpec((3, slots, tile), lambda j: (0, 0, j))
    return pl.pallas_call(
        lambda *refs: finish_body(len(sent), number_parts, *refs),
        grid=(hidden // tile,),
        in_specs=[stacked] * (1 + len(sent))
        + [whole(value.shape) for value in (grad, weight, pick, route)]
        + [columns(part), columns(part), pl.BlockSpec((tile, part), lambda j: (j, 0))],
        out_specs=[columns(slots)] * 3 + [whole((rows, wide))] * number_parts,
        out_shape=[jax.ShapeDtypeStruct((slots, hidden), BF)] * 3
        + [jax.ShapeDtypeStruct((rows, wide), BF)] * number_parts,
        scratch_shapes=[pltpu.VMEM((slots, part), F32), pltpu.VMEM((slots, part), F32)],
        compiler_params=pltpu.CompilerParams(vmem_limit_bytes=56 * 2**20),
        name="finish",
    )(own, *sent, grad, weight, pick, route, gate_w, up_w, down_w)


def per_device(tokens, expert_ids, route_weights, out_grad, gate_weight, up_weight, down_weight):
    experts = lax.axis_size("expert")
    groups = lax.axis_size("dp")
    my_expert = lax.axis_index("expert")
    outer, inner, core = factors(experts)
    rows, width = tokens.shape
    hidden_width = gate_weight.shape[2]
    choices = expert_ids.shape[1]
    part = width // groups
    most = min(rows, 3 * rows * choices // (2 * experts))
    extra = -(-3 * experts // 128) * 128
    gate_w, up_w, down_w = gate_weight[0], up_weight[0], down_weight[0]

    chosen = expert_ids[:, :, None] == jnp.arange(experts, dtype=jnp.int32)[None, None, :]
    weight_table = jnp.sum(jnp.where(chosen, route_weights[:, :, None], 0.0), axis=1)
    weight_cols = jnp.concatenate(
        three_pieces(weight_table) + [jnp.zeros((rows, extra - 3 * experts), BF)], axis=1
    )
    payload = jnp.concatenate(
        swap_groups(
            [
                jnp.concatenate(
                    [
                        tokens[:, g * part : (g + 1) * part],
                        out_grad[:, g * part : (g + 1) * part],
                        weight_cols,
                    ],
                    axis=1,
                )
                for g in range(groups)
            ]
        ),
        axis=0,
    )

    column = jnp.arange(extra, dtype=jnp.int32)[None, :]
    mask = jnp.broadcast_to(
        (column % experts == my_expert) & (column < 3 * experts), (8, extra)
    ).astype(BF)
    route_cols = (
        column == jnp.arange(8, dtype=jnp.int32)[:, None] * experts + my_expert
    ) & (jnp.arange(8)[:, None] < 3)
    route_cols = route_cols.astype(F32)
    last = outer - 1
    count = inner * core * groups * rows
    slots = inner * core * groups * most
    token = jnp.arange(count, dtype=jnp.int32)
    block = token // rows
    before = (block[:, None] == block[None, :]) & (token[:, None] <= token[None, :])
    tables = (mask, before.astype(BF), jnp.broadcast_to((block * most).astype(F32)[None], (8, count)))
    order = Order()
    pieces, along, around, picked, sums, ends = {0: payload}, {}, {}, {}, {}, {}
    moving, finals, held = {}, {}, {}

    def start_outer(number):
        if number < outer:
            (tied,) = order.enter(payload)
            pieces[number] = shift_expert(tied, 0, number)

    def start_inner(number):
        (mine,) = order.enter(pieces[number])
        along[number] = gather_start(mine, 1)
        around[number] = [gather_start(mine, 2)]

    def start_back(number):
        mine, others = held[number]
        (others,) = order.enter(others)
        moving[number] = (
            mine,
            [shift_expert(other, 1, -step) for step, other in enumerate(others, 1)],
        )

    def start_core(number):
        (mine,) = order.enter(along[number])
        order.leave(*mine)
        around[number] = around[number] + [gather_start(value, 2) for value in mine[1:]]

    def partial_sums(number):
        across, tied = order.enter(around[number], pieces.get(2) if number == 1 else None)
        if number == 1 and number + 1 < outer:
            pieces[number + 1] = tied
        parts = [piece[index] for index in range(core) for piece in across]
        picked[number] = project(parts, *tables, slots, gate_w, up_w, down_w)
        own, sent = picked[number][5:]
        order.leave(sent)
        sums[number] = (own, exchange(sent))

    def finish_chunk(number):
        own, arrived = order.enter(*sums[number])
        if number + 2 <= last:
            order.leave(*arrived)
            start_inner(number + 2)
        x_rows, grad, term, weight, pick = picked[number][:5]
        results = finish(
            own, arrived, grad, weight, pick, route_cols, gate_w, up_w, down_w, core
        )
        ends[number] = results[:3]
        back = results[3:]
        order.leave(*back)
        moving[number] = (
            back[0],
            [shift_expert(back[step], 2, -step) for step in range(1, core)],
        )

    def next_inner(number):
        mine, arrived = order.enter(*moving[number])
        mine, *others = (merge if number == last else merge_between)([mine] + arrived, inner)
        order.leave(mine, *others)
        held[number] = (mine, others)
        if number or not last:
            start_back(number)

    def next_outer(number):
        mine, arrived = order.enter(*moving[number])
        (total,) = merge([mine] + arrived, 1)
        if number:
            total = total.astype(BF)
        order.leave(total)
        finals[number] = shift_expert(total, 0, -number) if number else total

    start_inner(0)
    start_outer(1)
    along[0], pieces, tables = order.enter(along[0], pieces, tables)
    order.leave(*along[0])
    start_core(0)
    if last:
        start_inner(1)
    start_outer(2)
    partial_sums(0)
    if last:
        start_core(1)
        partial_sums(1)
        start_outer(3)
    for number in range(last + 1):
        finish_chunk(number)
        if number + 2 <= last:
            start_core(number + 2)
            partial_sums(number + 2)
            if number:
                start_outer(number + 3)
        if number < last:
            next_inner(number)
    for number in range(1, last):
        next_outer(number)
    next_inner(last)

    def rows_of(table, index):
        return [table[number][index] for number in range(last + 1)]

    def joined(values):
        return jnp.concatenate(values, axis=0)

    hidden_all, out_all = order.enter(rows_of(ends, 0), rows_of(picked, 2))
    down_grad = dot_tn(joined(hidden_all), joined(out_all)).astype(BF)[None]
    order.leave(down_grad)
    next_outer(last)
    if last:
        start_back(0)
    x_all, gate_all, up_all = order.enter(
        rows_of(picked, 0), rows_of(ends, 1), rows_of(ends, 2)
    )
    x_all = joined(x_all)
    gate_grad = dot_tn(x_all, joined(gate_all)).astype(BF)[None]
    up_grad = dot_tn(x_all, joined(up_all)).astype(BF)[None]
    order.leave(gate_grad, up_grad)
    if last:
        next_outer(0)
    (arrived,) = order.enter([finals[step] for step in range(outer)])
    final = add_all(arrived[0].astype(F32), arrived[1:]).astype(BF)
    parts = swap_groups([final[g * rows : (g + 1) * rows] for g in range(groups)])
    mixed = jnp.concatenate([value[:, :part] for value in parts], axis=1)
    tokens_grad = jnp.concatenate([value[:, part + extra :] for value in parts], axis=1)
    route_table = jnp.zeros((), F32)
    for value in parts:
        for number in range(3):
            start = part + number * experts
            route_table = route_table + value[:, start : start + experts].astype(F32)
    route_grad = jnp.sum(jnp.where(chosen, route_table[:, None, :], 0.0), axis=2)
    return (mixed, tokens_grad, route_grad, gate_grad, up_grad, down_grad)


def solution(mesh):
    return jax.shard_map(
        per_device,
        mesh=mesh,
        in_specs=(
            P(("dp", "expert"), None),
            P(("dp", "expert"), None),
            P(("dp", "expert"), None),
            P(("dp", "expert"), None),
            P("expert", "dp", None),
            P("expert", "dp", None),
            P("expert", None, "dp"),
        ),
        out_specs=(
            P(("dp", "expert"), None),
            P(("dp", "expert"), None),
            P(("dp", "expert"), None),
            P("expert", "dp", None),
            P("expert", "dp", None),
            P("expert", None, "dp"),
        ),
        check_vma=False,
    )
```

```python
import jax
import jax.numpy as jnp
from jax import lax
from jax.experimental import pallas as pl
from jax.experimental.pallas import tpu as pltpu
from jax.sharding import PartitionSpec as P

BF = jnp.bfloat16
F32 = jnp.float32


def silu_parts(pre_act):
    sigmoid_val = jax.nn.sigmoid(pre_act)
    return (pre_act * sigmoid_val, sigmoid_val * (1.0 + pre_act * (1.0 - sigmoid_val)))


def dot_nn(first, second):
    return lax.dot_general(first, second, (((1,), (0,)), ((), ())), preferred_element_type=F32)


def dot_nt(first, second):
    return lax.dot_general(first, second, (((1,), (1,)), ((), ())), preferred_element_type=F32)


def dot_tn(first, second):
    return lax.dot_general(first, second, (((0,), (0,)), ((), ())), preferred_element_type=F32)


def shift_dp(value, step):
    groups = lax.axis_size("dp")
    return lax.ppermute(value, "dp", [(i, (i + step) % groups) for i in range(groups)])


def choose(parts, index):
    picked = parts[0]
    for number in range(1, len(parts)):
        picked = jnp.where(index == number, parts[number], picked)
    return picked


def swap_groups(parts):
    groups = len(parts)
    mine = lax.axis_index("dp")
    by_step = [choose(parts, mine)]
    for step in range(1, groups):
        by_step.append(shift_dp(choose(parts, (mine + step) % groups), step))
    return [choose(by_step, (mine - group) % groups) for group in range(groups)]


def exchange(sent):
    return [shift_dp(sent, step) for step in range(1, lax.axis_size("dp"))]


def add_all(total, arrived):
    for value in arrived:
        total = total + value.astype(F32)
    return total


class Order:
    def __init__(self):
        self.last = []

    def enter(self, *values):
        flat, tree = jax.tree.flatten(values)
        tied = lax.optimization_barrier(tuple(flat) + tuple(self.last))[: len(flat)]
        return jax.tree.unflatten(tree, tied)

    def leave(self, *values):
        self.last = list(values)


def factors(experts):
    core = 2 if experts % 2 == 0 else 1
    rest = experts // core
    inner = 1
    while rest % (inner * 2) == 0 and (inner * 2) ** 2 <= rest:
        inner = inner * 2
    return (rest // inner, inner, core)


def shift_expert(value, level, step):
    dims = factors(lax.axis_size("expert"))
    stride = 1
    for dim in dims[level + 1 :]:
        stride = stride * dim
    size = dims[level]
    pairs = []
    for source in range(lax.axis_size("expert")):
        place = source // stride % size
        pairs.append((source, source + ((place + step) % size - place) * stride))
    return lax.ppermute(value, "expert", pairs)


def level_size(level):
    return factors(lax.axis_size("expert"))[level]


def gather_start(piece, level):
    return [piece] + [shift_expert(piece, level, step) for step in range(1, level_size(level))]


def three_pieces(value):
    high = lax.reduce_precision(value, 8, 7)
    rest = value - high
    mid = lax.reduce_precision(rest, 8, 7)
    return [high.astype(BF), mid.astype(BF), (rest - mid).astype(BF)]


def stacked_rows(values):
    return jnp.concatenate(values, axis=0) if len(values) > 1 else values[0]


def project_body(number_parts, part, *refs):
    mask_ref, order_ref, base_ref = refs[:3]
    part_refs = refs[3 : 3 + number_parts]
    gate_ref, up_ref, down_ref = refs[3 + number_parts : 6 + number_parts]
    x_ref, grad_ref, term_ref, weight_ref, pick_ref, own_ref, sent_ref = refs[6 + number_parts :]

    @pl.when(pl.program_id(0) == 0)
    def _():
        slots = x_ref.shape[0]
        arrived = stacked_rows([ref[...] for ref in part_refs])
        count = arrived.shape[0]
        mask = mask_ref[...]
        weight = dot_nt(mask, arrived[:, 2 * part :])
        live = weight > 0.0
        place = dot_nn(jnp.where(live, 1.0, 0.0).astype(BF), order_ref[...])
        slot = jnp.where(live, place - 1.0 + base_ref[...], -1.0)[:1]
        index = lax.broadcasted_iota(jnp.int32, (slots, count), 0).astype(F32)
        pick = jnp.where(index == slot, 1.0, 0.0).astype(BF)
        pick_ref[...] = pick
        x_ref[...] = dot_nn(pick, arrived[:, :part]).astype(BF)
        grad = dot_nn(pick, arrived[:, part : 2 * part])
        grad_ref[...] = grad.astype(BF)
        chosen = dot_nn(pick, arrived[:, 2 * part :]) * mask[:1].astype(F32)
        weight_rows = jnp.sum(chosen, axis=1, keepdims=True)
        weight_ref[...] = jnp.broadcast_to(weight_rows, weight_ref.shape)
        term_ref[...] = (weight_rows * grad).astype(BF)

    x_rows = x_ref[...]
    values = (
        dot_nn(x_rows, gate_ref[...]),
        dot_nn(x_rows, up_ref[...]),
        dot_nt(term_ref[...], down_ref[...]),
    )
    for number, value in enumerate(values):
        own_ref[number] = value
        sent_ref[number] = value.astype(BF)


def project(parts, mask, order, base, slots, gate_w, up_w, down_w):
    part, hidden = gate_w.shape
    tile = min(256, hidden)
    count = sum(value.shape[0] for value in parts)
    whole = lambda shape: pl.BlockSpec(shape, lambda j: (0,) * len(shape))
    columns = lambda rows: pl.BlockSpec((rows, tile), lambda j: (0, j))
    stacked = pl.BlockSpec((3, slots, tile), lambda j: (0, 0, j))
    row_out = jax.ShapeDtypeStruct((slots, part), BF)
    return pl.pallas_call(
        lambda *refs: project_body(len(parts), part, *refs),
        grid=(hidden // tile,),
        in_specs=[whole(mask.shape), whole(order.shape), whole(base.shape)]
        + [whole(value.shape) for value in parts]
        + [columns(part), columns(part), pl.BlockSpec((tile, part), lambda j: (j, 0))],
        out_specs=[whole((slots, part))] * 3
        + [whole((slots, 128)), whole((slots, count)), stacked, stacked],
        out_shape=[row_out] * 3
        + [
            jax.ShapeDtypeStruct((slots, 128), F32),
            jax.ShapeDtypeStruct((slots, count), BF),
            jax.ShapeDtypeStruct((3, slots, hidden), F32),
            jax.ShapeDtypeStruct((3, slots, hidden), BF),
        ],
        compiler_params=pltpu.CompilerParams(vmem_limit_bytes=56 * 2**20),
        name="project",
    )(mask, order, base, *parts, gate_w, up_w, down_w)


def merge(values, pieces):
    total = add_all(values[0].astype(F32), values[1:])
    rows = total.shape[0] // pieces
    parts = [total[number * rows : (number + 1) * rows] for number in range(pieces)]
    return parts[:1] + [part.astype(BF) for part in parts[1:]]


def merge_between(values, pieces):
    rows, wide = values[0].shape
    rows = rows // pieces
    kinds = [F32] + [BF] * (pieces - 1)

    def body(*refs):
        for number in range(pieces):
            here = slice(number * rows, (number + 1) * rows)
            total = add_all(refs[0][here].astype(F32), [ref[here] for ref in refs[1 : len(values)]])
            refs[len(values) + number][...] = total.astype(kinds[number])

    return pl.pallas_call(
        body,
        out_shape=[jax.ShapeDtypeStruct((rows, wide), kind) for kind in kinds],
        compiler_params=pltpu.CompilerParams(vmem_limit_bytes=56 * 2**20),
        name="merge",
    )(*values)


def finish_body(number_sent, number_parts, *refs):
    own_ref = refs[0]
    sent_refs = refs[1 : 1 + number_sent]
    grad_ref, weight_ref, pick_ref, route_ref, gate_ref, up_ref, down_ref = refs[
        1 + number_sent : 8 + number_sent
    ]
    hidden_ref, gate_term_ref, up_term_ref = refs[8 + number_sent : 11 + number_sent]
    back_refs = refs[11 + number_sent : 11 + number_sent + number_parts]
    out_acc, in_acc = refs[11 + number_sent + number_parts :]
    step = pl.program_id(0)
    gate_pre, up_pre, hidden_grad = (
        add_all(own_ref[number], [ref[number] for ref in sent_refs]) for number in range(3)
    )
    act_val, act_slope = silu_parts(gate_pre)
    hidden = (act_val * up_pre).astype(BF)
    gate_term = (hidden_grad * up_pre * act_slope).astype(BF)
    up_term = (hidden_grad * act_val).astype(BF)
    hidden_ref[...] = hidden
    gate_term_ref[...] = gate_term
    up_term_ref[...] = up_term
    out_part = dot_nn(hidden, down_ref[...])
    in_part = dot_nt(gate_term, gate_ref[...]) + dot_nt(up_term, up_ref[...])

    @pl.when(step == 0)
    def _():
        out_acc[...] = out_part
        in_acc[...] = in_part

    @pl.when(step > 0)
    def _():
        out_acc[...] += out_part
        in_acc[...] += in_part

    @pl.when(step == pl.num_programs(0) - 1)
    def _():
        part = out_acc.shape[1]
        extra = route_ref.shape[1]
        expert_out = out_acc[...].astype(BF).astype(F32)
        rest = jnp.sum(grad_ref[...].astype(F32) * expert_out, axis=1, keepdims=True)
        route = jnp.zeros((rest.shape[0], extra), F32)
        for number in range(3):
            piece = rest.astype(BF).astype(F32)
            route = route + piece * route_ref[number : number + 1]
            rest = rest - piece
        pick = pick_ref[...]
        weighted = (weight_ref[:, :1] * expert_out).astype(BF)
        backs = (
            dot_tn(pick, weighted).astype(BF),
            dot_tn(pick, route.astype(BF)).astype(BF),
            dot_tn(pick, in_acc[...].astype(BF)).astype(BF),
        )
        rows = back_refs[0].shape[0]
        for number, ref in enumerate(back_refs):
            here = slice(number * rows, (number + 1) * rows)
            ref[:, :part] = backs[0][here]
            ref[:, part : part + extra] = backs[1][here]
            ref[:, part + extra :] = backs[2][here]


def finish(own, sent, grad, weight, pick, route, gate_w, up_w, down_w, number_parts):
    part, hidden = gate_w.shape
    tile = min(256, hidden)
    slots, count = pick.shape
    rows = count // number_parts
    wide = 2 * part + route.shape[1]
    whole = lambda shape: pl.BlockSpec(shape, lambda j: (0,) * len(shape))
    columns = lambda size: pl.BlockSpec((size, tile), lambda j: (0, j))
    stacked = pl.BlockSpec((3, slots, tile), lambda j: (0, 0, j))
    return pl.pallas_call(
        lambda *refs: finish_body(len(sent), number_parts, *refs),
        grid=(hidden // tile,),
        in_specs=[stacked] * (1 + len(sent))
        + [whole(value.shape) for value in (grad, weight, pick, route)]
        + [columns(part), columns(part), pl.BlockSpec((tile, part), lambda j: (j, 0))],
        out_specs=[columns(slots)] * 3 + [whole((rows, wide))] * number_parts,
        out_shape=[jax.ShapeDtypeStruct((slots, hidden), BF)] * 3
        + [jax.ShapeDtypeStruct((rows, wide), BF)] * number_parts,
        scratch_shapes=[pltpu.VMEM((slots, part), F32), pltpu.VMEM((slots, part), F32)],
        compiler_params=pltpu.CompilerParams(vmem_limit_bytes=56 * 2**20),
        name="finish",
    )(own, *sent, grad, weight, pick, route, gate_w, up_w, down_w)


def finish_and_project(left, parts, mask, order, base, slots, gate_w, up_w, down_w, number_parts):
    own, sent, grad, weight, pick, route = left
    part, hidden = gate_w.shape
    tile = min(256, hidden)
    count = sum(value.shape[0] for value in parts)
    rows = pick.shape[1] // number_parts
    wide = 2 * part + route.shape[1]
    whole = lambda shape: pl.BlockSpec(shape, lambda j: (0,) * len(shape))
    columns = lambda size: pl.BlockSpec((size, tile), lambda j: (0, j))
    stacked = pl.BlockSpec((3, slots, tile), lambda j: (0, 0, j))
    first = 3 + len(parts)
    second = first + 5 + len(sent)
    weights = second + 3

    def body(*refs):
        outs = refs[weights : weights + 7]
        ends = refs[weights + 7 :]
        finish_body(len(sent), number_parts, *refs[first:weights], *ends)
        project_body(len(parts), part, *refs[:first], *refs[second:weights], *outs)

    results = pl.pallas_call(
        body,
        grid=(hidden // tile,),
        in_specs=[whole(value.shape) for value in (mask, order, base, *parts)]
        + [stacked] * (1 + len(sent))
        + [whole(value.shape) for value in (grad, weight, pick, route)]
        + [columns(part), columns(part), pl.BlockSpec((tile, part), lambda j: (j, 0))],
        out_specs=[whole((slots, part))] * 3
        + [whole((slots, 128)), whole((slots, count)), stacked, stacked]
        + [columns(slots)] * 3
        + [whole((rows, wide))] * number_parts,
        out_shape=[jax.ShapeDtypeStruct((slots, part), BF)] * 3
        + [
            jax.ShapeDtypeStruct((slots, 128), F32),
            jax.ShapeDtypeStruct((slots, count), BF),
            jax.ShapeDtypeStruct((3, slots, hidden), F32),
            jax.ShapeDtypeStruct((3, slots, hidden), BF),
        ]
        + [jax.ShapeDtypeStruct((slots, hidden), BF)] * 3
        + [jax.ShapeDtypeStruct((rows, wide), BF)] * number_parts,
        scratch_shapes=[pltpu.VMEM((slots, part), F32), pltpu.VMEM((slots, part), F32)],
        compiler_params=pltpu.CompilerParams(vmem_limit_bytes=56 * 2**20),
        name="step",
    )(mask, order, base, *parts, own, *sent, grad, weight, pick, route, gate_w, up_w, down_w)
    return results[:7], results[7:]


def per_device(tokens, expert_ids, route_weights, out_grad, gate_weight, up_weight, down_weight):
    experts = lax.axis_size("expert")
    groups = lax.axis_size("dp")
    my_expert = lax.axis_index("expert")
    outer, inner, core = factors(experts)
    rows, width = tokens.shape
    hidden_width = gate_weight.shape[2]
    choices = expert_ids.shape[1]
    part = width // groups
    most = min(rows, 3 * rows * choices // (2 * experts))
    extra = -(-3 * experts // 128) * 128
    gate_w, up_w, down_w = gate_weight[0], up_weight[0], down_weight[0]

    chosen = expert_ids[:, :, None] == jnp.arange(experts, dtype=jnp.int32)[None, None, :]
    weight_table = jnp.sum(jnp.where(chosen, route_weights[:, :, None], 0.0), axis=1)
    weight_cols = jnp.concatenate(
        three_pieces(weight_table) + [jnp.zeros((rows, extra - 3 * experts), BF)], axis=1
    )
    payload = jnp.concatenate(
        swap_groups(
            [
                jnp.concatenate(
                    [
                        tokens[:, g * part : (g + 1) * part],
                        out_grad[:, g * part : (g + 1) * part],
                        weight_cols,
                    ],
                    axis=1,
                )
                for g in range(groups)
            ]
        ),
        axis=0,
    )

    column = jnp.arange(extra, dtype=jnp.int32)[None, :]
    mask = jnp.broadcast_to(
        (column % experts == my_expert) & (column < 3 * experts), (8, extra)
    ).astype(BF)
    route_cols = (
        column == jnp.arange(8, dtype=jnp.int32)[:, None] * experts + my_expert
    ) & (jnp.arange(8)[:, None] < 3)
    route_cols = route_cols.astype(F32)
    last = outer - 1
    count = inner * core * groups * rows
    slots = inner * core * groups * most
    token = jnp.arange(count, dtype=jnp.int32)
    block = token // rows
    before = (block[:, None] == block[None, :]) & (token[:, None] <= token[None, :])
    tables = (mask, before.astype(BF), jnp.broadcast_to((block * most).astype(F32)[None], (8, count)))
    order = Order()
    pieces, along, around, picked, sums, ends = {0: payload}, {}, {}, {}, {}, {}
    moving, finals, held = {}, {}, {}

    def start_outer(number):
        if number < outer:
            (tied,) = order.enter(payload)
            pieces[number] = shift_expert(tied, 0, number)

    def start_inner(number):
        (mine,) = order.enter(pieces[number])
        along[number] = gather_start(mine, 1)
        around[number] = [] if number else [gather_start(mine, 2)]

    def start_back(number):
        mine, others = held[number]
        (others,) = order.enter(others)
        moving[number] = (
            mine,
            [shift_expert(other, 1, -step) for step, other in enumerate(others, 1)],
        )

    def start_core(number):
        (mine,) = order.enter(along[number])
        order.leave(*mine)
        around[number] = around[number] + [
            gather_start(value, 2) for value in (mine if number else mine[1:])
        ]

    def ready_parts(across):
        return [piece[index] for index in range(core) for piece in across]

    def partial_sums(number):
        across, tied = order.enter(around[number], pieces.get(2) if number == 1 else None)
        if number == 1 and outer > 2:
            pieces[2] = tied
            if outer > 3:
                late, _ = lax.optimization_barrier((payload, tied))
                pieces[3] = shift_expert(late, 0, 3)
        projected(
            number, project(ready_parts(across), *tables, slots, gate_w, up_w, down_w)
        )
        order.leave(picked[number][6])

    def projected(number, results):
        picked[number] = results
        own, sent = results[5:]
        sums[number] = (own, exchange(sent))

    def finished(number, results):
        ends[number] = results[:3]
        back = results[3:]
        moving[number] = (
            back[0],
            [shift_expert(back[step], 2, -step) for step in range(1, core)],
        )

    def finish_chunk(number, later=None):
        own, arrived, across = order.enter(*sums[number], around.get(later))
        x_rows, grad, term, weight, pick = picked[number][:5]
        left = (own, arrived, grad, weight, pick, route_cols)
        if later is None:
            results = finish(*left, gate_w, up_w, down_w, core)
            order.leave(*results[3:])
            finished(number, results)
        else:
            made, results = finish_and_project(
                left, ready_parts(across), *tables, slots, gate_w, up_w, down_w, core
            )
            order.leave(made[6], *results[3:])
            projected(later, made)
            finished(number, results)

    def next_inner(number):
        mine, arrived = order.enter(*moving[number])
        mine, *others = (merge_between if 0 < number < last else merge)([mine] + arrived, inner)
        order.leave(mine, *others)
        held[number] = (mine, others)
        if number or not last:
            start_back(number)

    def next_outer(number):
        mine, arrived = order.enter(*moving[number])
        (total,) = merge([mine] + arrived, 1)
        if number:
            total = total.astype(BF)
        order.leave(total)
        finals[number] = shift_expert(total, 0, -number) if number else total

    pieces[0], tables = order.enter(payload, tables)
    payload = pieces[0]
    start_inner(0)
    start_outer(1)
    along[0], pieces = order.enter(along[0], pieces)
    order.leave(*along[0])
    start_core(0)
    if last:
        start_inner(1)
    start_outer(2)
    partial_sums(0)
    if last:
        start_core(1)
        partial_sums(1)
    if last > 1:
        start_inner(2)
        if last > 2:
            start_inner(3)
        start_core(2)
    for number in range(last + 1):
        later = number + 2
        if later <= last:
            finish_chunk(number, later)
            if later < last:
                if later > 2:
                    start_inner(later + 1)
                start_core(later + 1)
                start_outer(later + 2)
        else:
            finish_chunk(number)
        if 0 < number < last:
            next_inner(number)
    for number in range(1, last):
        next_outer(number)
    next_inner(last)

    def rows_of(table, index):
        return [table[number][index] for number in range(last + 1)]

    def joined(values):
        return jnp.concatenate(values, axis=0)

    hidden_all, out_all = order.enter(rows_of(ends, 0), rows_of(picked, 2))
    down_grad = dot_tn(joined(hidden_all), joined(out_all)).astype(BF)[None]
    order.leave(down_grad)
    next_outer(last)
    if last:
        next_inner(0)
        start_back(0)
    x_all, gate_all, up_all = order.enter(
        rows_of(picked, 0), rows_of(ends, 1), rows_of(ends, 2)
    )
    x_all = joined(x_all)
    gate_grad = dot_tn(x_all, joined(gate_all)).astype(BF)[None]
    up_grad = dot_tn(x_all, joined(up_all)).astype(BF)[None]
    order.leave(gate_grad, up_grad)
    if last:
        next_outer(0)
    (arrived,) = order.enter(list(finals.values()))
    final = add_all(arrived[0].astype(F32), arrived[1:]).astype(BF)
    parts = swap_groups([final[g * rows : (g + 1) * rows] for g in range(groups)])
    mixed = jnp.concatenate([value[:, :part] for value in parts], axis=1)
    tokens_grad = jnp.concatenate([value[:, part + extra :] for value in parts], axis=1)
    route_table = jnp.zeros((), F32)
    for value in parts:
        for number in range(3):
            start = part + number * experts
            route_table = route_table + value[:, start : start + experts].astype(F32)
    route_grad = jnp.sum(jnp.where(chosen, route_table[:, None, :], 0.0), axis=2)
    return (mixed, tokens_grad, route_grad, gate_grad, up_grad, down_grad)


def solution(mesh):
    return jax.shard_map(
        per_device,
        mesh=mesh,
        in_specs=(
            P(("dp", "expert"), None),
            P(("dp", "expert"), None),
            P(("dp", "expert"), None),
            P(("dp", "expert"), None),
            P("expert", "dp", None),
            P("expert", "dp", None),
            P("expert", None, "dp"),
        ),
        out_specs=(
            P(("dp", "expert"), None),
            P(("dp", "expert"), None),
            P(("dp", "expert"), None),
            P("expert", "dp", None),
            P("expert", "dp", None),
            P("expert", None, "dp"),
        ),
        check_vma=False,
    )
```

```python
import jax
import jax.numpy as jnp
from jax import lax
from jax.experimental import pallas as pl
from jax.experimental.pallas import tpu as pltpu
from jax.sharding import PartitionSpec as P

BF = jnp.bfloat16
F32 = jnp.float32


def silu_parts(pre_act):
    sigmoid_val = jax.nn.sigmoid(pre_act)
    return (pre_act * sigmoid_val, sigmoid_val * (1.0 + pre_act * (1.0 - sigmoid_val)))


def dot_nn(first, second):
    return lax.dot_general(first, second, (((1,), (0,)), ((), ())), preferred_element_type=F32)


def dot_nt(first, second):
    return lax.dot_general(first, second, (((1,), (1,)), ((), ())), preferred_element_type=F32)


def dot_tn(first, second):
    return lax.dot_general(first, second, (((0,), (0,)), ((), ())), preferred_element_type=F32)


def shift_dp(value, step):
    groups = lax.axis_size("dp")
    return lax.ppermute(value, "dp", [(i, (i + step) % groups) for i in range(groups)])


def choose(parts, index):
    picked = parts[0]
    for number in range(1, len(parts)):
        picked = jnp.where(index == number, parts[number], picked)
    return picked


def swap_groups(parts):
    groups = len(parts)
    mine = lax.axis_index("dp")
    by_step = [choose(parts, mine)]
    for step in range(1, groups):
        by_step.append(shift_dp(choose(parts, (mine + step) % groups), step))
    return [choose(by_step, (mine - group) % groups) for group in range(groups)]


def exchange(sent):
    return [shift_dp(sent, step) for step in range(1, lax.axis_size("dp"))]


def add_all(total, arrived):
    for value in arrived:
        total = total + value.astype(F32)
    return total


class Order:
    def __init__(self):
        self.last = []

    def enter(self, *values):
        flat, tree = jax.tree.flatten(values)
        tied = lax.optimization_barrier(tuple(flat) + tuple(self.last))[: len(flat)]
        return jax.tree.unflatten(tree, tied)

    def leave(self, *values):
        self.last = list(values)


def factors(experts):
    core = 2 if experts % 2 == 0 else 1
    rest = experts // core
    inner = 1
    while rest % (inner * 2) == 0 and (inner * 2) ** 2 <= rest:
        inner = inner * 2
    return (rest // inner, inner, core)


def shift_expert(value, level, step):
    dims = factors(lax.axis_size("expert"))
    stride = 1
    for dim in dims[level + 1 :]:
        stride = stride * dim
    size = dims[level]
    pairs = []
    for source in range(lax.axis_size("expert")):
        place = source // stride % size
        pairs.append((source, source + ((place + step) % size - place) * stride))
    return lax.ppermute(value, "expert", pairs)


def level_size(level):
    return factors(lax.axis_size("expert"))[level]


def gather_start(piece, level):
    return [piece] + [shift_expert(piece, level, step) for step in range(1, level_size(level))]


def three_pieces(value):
    high = lax.reduce_precision(value, 8, 7)
    rest = value - high
    mid = lax.reduce_precision(rest, 8, 7)
    return [high.astype(BF), mid.astype(BF), (rest - mid).astype(BF)]


def stacked_rows(values):
    return jnp.concatenate(values, axis=0) if len(values) > 1 else values[0]


def project_body(number_parts, part, *refs):
    mask_ref, order_ref, base_ref = refs[:3]
    part_refs = refs[3 : 3 + number_parts]
    gate_ref, up_ref, down_ref = refs[3 + number_parts : 6 + number_parts]
    x_ref, grad_ref, term_ref, weight_ref, pick_ref, own_ref, sent_ref = refs[6 + number_parts :]

    @pl.when(pl.program_id(0) == 0)
    def _():
        slots = x_ref.shape[0]
        arrived = stacked_rows([ref[...] for ref in part_refs])
        count = arrived.shape[0]
        mask = mask_ref[...]
        weight = dot_nt(mask, arrived[:, 2 * part :])
        live = weight > 0.0
        place = dot_nn(jnp.where(live, 1.0, 0.0).astype(BF), order_ref[...])
        slot = jnp.where(live, place - 1.0 + base_ref[...], -1.0)[:1]
        index = lax.broadcasted_iota(jnp.int32, (slots, count), 0).astype(F32)
        pick = jnp.where(index == slot, 1.0, 0.0).astype(BF)
        pick_ref[...] = pick
        x_ref[...] = dot_nn(pick, arrived[:, :part]).astype(BF)
        grad = dot_nn(pick, arrived[:, part : 2 * part])
        grad_ref[...] = grad.astype(BF)
        chosen = dot_nn(pick, arrived[:, 2 * part :]) * mask[:1].astype(F32)
        weight_rows = jnp.sum(chosen, axis=1, keepdims=True)
        weight_ref[...] = jnp.broadcast_to(weight_rows, weight_ref.shape)
        term_ref[...] = (weight_rows * grad).astype(BF)

    x_rows = x_ref[...]
    values = (
        dot_nn(x_rows, gate_ref[...]),
        dot_nn(x_rows, up_ref[...]),
        dot_nt(term_ref[...], down_ref[...]),
    )
    for number, value in enumerate(values):
        own_ref[number] = value
        sent_ref[number] = value.astype(BF)


def project(parts, mask, order, base, slots, gate_w, up_w, down_w):
    part, hidden = gate_w.shape
    tile = min(256, hidden)
    count = sum(value.shape[0] for value in parts)
    whole = lambda shape: pl.BlockSpec(shape, lambda j: (0,) * len(shape))
    columns = lambda rows: pl.BlockSpec((rows, tile), lambda j: (0, j))
    stacked = pl.BlockSpec((3, slots, tile), lambda j: (0, 0, j))
    row_out = jax.ShapeDtypeStruct((slots, part), BF)
    return pl.pallas_call(
        lambda *refs: project_body(len(parts), part, *refs),
        grid=(hidden // tile,),
        in_specs=[whole(mask.shape), whole(order.shape), whole(base.shape)]
        + [whole(value.shape) for value in parts]
        + [columns(part), columns(part), pl.BlockSpec((tile, part), lambda j: (j, 0))],
        out_specs=[whole((slots, part))] * 3
        + [whole((slots, 128)), whole((slots, count)), stacked, stacked],
        out_shape=[row_out] * 3
        + [
            jax.ShapeDtypeStruct((slots, 128), F32),
            jax.ShapeDtypeStruct((slots, count), BF),
            jax.ShapeDtypeStruct((3, slots, hidden), F32),
            jax.ShapeDtypeStruct((3, slots, hidden), BF),
        ],
        compiler_params=pltpu.CompilerParams(vmem_limit_bytes=56 * 2**20),
        name="project",
    )(mask, order, base, *parts, gate_w, up_w, down_w)


def merge(values, pieces):
    total = add_all(values[0].astype(F32), values[1:])
    rows = total.shape[0] // pieces
    parts = [total[number * rows : (number + 1) * rows] for number in range(pieces)]
    return parts[:1] + [part.astype(BF) for part in parts[1:]]


def merge_between(groups, kinds):
    sizes = [len(group) for group in groups]

    def body(*refs):
        start = 0
        for size, out in zip(sizes, refs[sum(sizes) :]):
            total = add_all(refs[start][...].astype(F32), [ref[...] for ref in refs[start + 1 : start + size]])
            out[...] = total.astype(out.dtype)
            start += size

    return pl.pallas_call(
        body,
        out_shape=[
            jax.ShapeDtypeStruct(group[0].shape, kind) for group, kind in zip(groups, kinds)
        ],
        compiler_params=pltpu.CompilerParams(vmem_limit_bytes=56 * 2**20),
        name="merge",
    )(*[value for group in groups for value in group])


def finish_body(number_sent, number_parts, *refs):
    own_ref = refs[0]
    sent_refs = refs[1 : 1 + number_sent]
    grad_ref, weight_ref, pick_ref, route_ref, gate_ref, up_ref, down_ref = refs[
        1 + number_sent : 8 + number_sent
    ]
    hidden_ref, gate_term_ref, up_term_ref = refs[8 + number_sent : 11 + number_sent]
    back_refs = refs[11 + number_sent : 11 + number_sent + number_parts]
    out_acc, in_acc = refs[11 + number_sent + number_parts :]
    step = pl.program_id(0)
    gate_pre, up_pre, hidden_grad = (
        add_all(own_ref[number], [ref[number] for ref in sent_refs]) for number in range(3)
    )
    act_val, act_slope = silu_parts(gate_pre)
    hidden = (act_val * up_pre).astype(BF)
    gate_term = (hidden_grad * up_pre * act_slope).astype(BF)
    up_term = (hidden_grad * act_val).astype(BF)
    hidden_ref[...] = hidden
    gate_term_ref[...] = gate_term
    up_term_ref[...] = up_term
    out_part = dot_nn(hidden, down_ref[...])
    in_part = dot_nt(gate_term, gate_ref[...]) + dot_nt(up_term, up_ref[...])

    @pl.when(step == 0)
    def _():
        out_acc[...] = out_part
        in_acc[...] = in_part

    @pl.when(step > 0)
    def _():
        out_acc[...] += out_part
        in_acc[...] += in_part

    @pl.when(step == pl.num_programs(0) - 1)
    def _():
        part = out_acc.shape[1]
        extra = route_ref.shape[1]
        expert_out = out_acc[...].astype(BF).astype(F32)
        rest = jnp.sum(grad_ref[...].astype(F32) * expert_out, axis=1, keepdims=True)
        route = jnp.zeros((rest.shape[0], extra), F32)
        for number in range(3):
            piece = rest.astype(BF).astype(F32)
            route = route + piece * route_ref[number : number + 1]
            rest = rest - piece
        pick = pick_ref[...]
        weighted = (weight_ref[:, :1] * expert_out).astype(BF)
        backs = (
            dot_tn(pick, weighted).astype(BF),
            dot_tn(pick, route.astype(BF)).astype(BF),
            dot_tn(pick, in_acc[...].astype(BF)).astype(BF),
        )
        rows = back_refs[0].shape[0]
        for number, ref in enumerate(back_refs):
            here = slice(number * rows, (number + 1) * rows)
            ref[:, :part] = backs[0][here]
            ref[:, part : part + extra] = backs[1][here]
            ref[:, part + extra :] = backs[2][here]


def finish(own, sent, grad, weight, pick, route, gate_w, up_w, down_w, number_parts):
    part, hidden = gate_w.shape
    tile = min(256, hidden)
    slots, count = pick.shape
    rows = count // number_parts
    wide = 2 * part + route.shape[1]
    whole = lambda shape: pl.BlockSpec(shape, lambda j: (0,) * len(shape))
    columns = lambda size: pl.BlockSpec((size, tile), lambda j: (0, j))
    stacked = pl.BlockSpec((3, slots, tile), lambda j: (0, 0, j))
    return pl.pallas_call(
        lambda *refs: finish_body(len(sent), number_parts, *refs),
        grid=(hidden // tile,),
        in_specs=[stacked] * (1 + len(sent))
        + [whole(value.shape) for value in (grad, weight, pick, route)]
        + [columns(part), columns(part), pl.BlockSpec((tile, part), lambda j: (j, 0))],
        out_specs=[columns(slots)] * 3 + [whole((rows, wide))] * number_parts,
        out_shape=[jax.ShapeDtypeStruct((slots, hidden), BF)] * 3
        + [jax.ShapeDtypeStruct((rows, wide), BF)] * number_parts,
        scratch_shapes=[pltpu.VMEM((slots, part), F32), pltpu.VMEM((slots, part), F32)],
        compiler_params=pltpu.CompilerParams(vmem_limit_bytes=56 * 2**20),
        name="finish",
    )(own, *sent, grad, weight, pick, route, gate_w, up_w, down_w)


def finish_and_project(left, parts, mask, order, base, slots, gate_w, up_w, down_w, number_parts):
    own, sent, grad, weight, pick, route = left
    part, hidden = gate_w.shape
    tile = min(256, hidden)
    count = sum(value.shape[0] for value in parts)
    rows = pick.shape[1] // number_parts
    wide = 2 * part + route.shape[1]
    whole = lambda shape: pl.BlockSpec(shape, lambda j: (0,) * len(shape))
    columns = lambda size: pl.BlockSpec((size, tile), lambda j: (0, j))
    stacked = pl.BlockSpec((3, slots, tile), lambda j: (0, 0, j))
    first = 3 + len(parts)
    second = first + 5 + len(sent)
    weights = second + 3

    def body(*refs):
        outs = refs[weights : weights + 7]
        ends = refs[weights + 7 :]
        finish_body(len(sent), number_parts, *refs[first:weights], *ends)
        project_body(len(parts), part, *refs[:first], *refs[second:weights], *outs)

    results = pl.pallas_call(
        body,
        grid=(hidden // tile,),
        in_specs=[whole(value.shape) for value in (mask, order, base, *parts)]
        + [stacked] * (1 + len(sent))
        + [whole(value.shape) for value in (grad, weight, pick, route)]
        + [columns(part), columns(part), pl.BlockSpec((tile, part), lambda j: (j, 0))],
        out_specs=[whole((slots, part))] * 3
        + [whole((slots, 128)), whole((slots, count)), stacked, stacked]
        + [columns(slots)] * 3
        + [whole((rows, wide))] * number_parts,
        out_shape=[jax.ShapeDtypeStruct((slots, part), BF)] * 3
        + [
            jax.ShapeDtypeStruct((slots, 128), F32),
            jax.ShapeDtypeStruct((slots, count), BF),
            jax.ShapeDtypeStruct((3, slots, hidden), F32),
            jax.ShapeDtypeStruct((3, slots, hidden), BF),
        ]
        + [jax.ShapeDtypeStruct((slots, hidden), BF)] * 3
        + [jax.ShapeDtypeStruct((rows, wide), BF)] * number_parts,
        scratch_shapes=[pltpu.VMEM((slots, part), F32), pltpu.VMEM((slots, part), F32)],
        compiler_params=pltpu.CompilerParams(vmem_limit_bytes=56 * 2**20),
        name="step",
    )(mask, order, base, *parts, own, *sent, grad, weight, pick, route, gate_w, up_w, down_w)
    return results[:7], results[7:]


def per_device(tokens, expert_ids, route_weights, out_grad, gate_weight, up_weight, down_weight):
    experts = lax.axis_size("expert")
    groups = lax.axis_size("dp")
    my_expert = lax.axis_index("expert")
    outer, inner, core = factors(experts)
    rows, width = tokens.shape
    hidden_width = gate_weight.shape[2]
    choices = expert_ids.shape[1]
    part = width // groups
    most = min(rows, 3 * rows * choices // (2 * experts))
    extra = -(-3 * experts // 128) * 128
    gate_w, up_w, down_w = gate_weight[0], up_weight[0], down_weight[0]

    chosen = expert_ids[:, :, None] == jnp.arange(experts, dtype=jnp.int32)[None, None, :]
    weight_table = jnp.sum(jnp.where(chosen, route_weights[:, :, None], 0.0), axis=1)
    weight_cols = jnp.concatenate(
        three_pieces(weight_table) + [jnp.zeros((rows, extra - 3 * experts), BF)], axis=1
    )
    payload = jnp.concatenate(
        swap_groups(
            [
                jnp.concatenate(
                    [
                        tokens[:, g * part : (g + 1) * part],
                        out_grad[:, g * part : (g + 1) * part],
                        weight_cols,
                    ],
                    axis=1,
                )
                for g in range(groups)
            ]
        ),
        axis=0,
    )

    column = jnp.arange(extra, dtype=jnp.int32)[None, :]
    mask = jnp.broadcast_to(
        (column % experts == my_expert) & (column < 3 * experts), (8, extra)
    ).astype(BF)
    route_cols = (
        column == jnp.arange(8, dtype=jnp.int32)[:, None] * experts + my_expert
    ) & (jnp.arange(8)[:, None] < 3)
    route_cols = route_cols.astype(F32)
    last = outer - 1
    count = inner * core * groups * rows
    slots = inner * core * groups * most
    token = jnp.arange(count, dtype=jnp.int32)
    block = token // rows
    before = (block[:, None] == block[None, :]) & (token[:, None] <= token[None, :])
    tables = (mask, before.astype(BF), jnp.broadcast_to((block * most).astype(F32)[None], (8, count)))
    order = Order()
    pieces, along, around, picked, sums, ends = {0: payload}, {}, {}, {}, {}, {}
    moving, finals, held = {}, {}, {}

    def start_outer(number):
        if number < outer:
            (tied,) = order.enter(payload)
            pieces[number] = shift_expert(tied, 0, number)

    def start_inner(number):
        (mine,) = order.enter(pieces[number])
        along[number] = gather_start(mine, 1)
        around[number] = [] if number else [gather_start(mine, 2)]

    def add_up(numbers):
        if len(numbers):
            (arrived,) = order.enter([finals.pop(number) for number in numbers])
            total = add_all(arrived[0].astype(F32), arrived[1:])
            order.leave(total)
            finals[numbers[0]] = total

    def start_back(number):
        mine, others = held[number]
        (others,) = order.enter(others)
        moving[number] = (
            mine,
            [shift_expert(other, 1, -step) for step, other in enumerate(others, 1)],
        )

    def start_core(number):
        (mine,) = order.enter(along[number])
        order.leave(*mine)
        around[number] = around[number] + [
            gather_start(value, 2) for value in (mine if number else mine[1:])
        ]

    def cuts_of(number):
        return inner if 0 < number < last else 1

    def ready_parts(across):
        return [piece[index] for index in range(core) for piece in across]

    def partial_sums(number):
        across, tied = order.enter(around[number], pieces.get(2) if number == 1 else None)
        if number == 1 and outer > 2:
            pieces[2] = tied
            if outer > 3:
                late, _ = lax.optimization_barrier((payload, tied))
                pieces[3] = shift_expert(late, 0, 3)
            along[2] = gather_start(tied, 1)
            around[2] = []
        projected(
            number, project(ready_parts(across), *tables, slots, gate_w, up_w, down_w)
        )
        order.leave(picked[number][6])

    def projected(number, results):
        picked[number] = results
        own, sent = results[5:]
        sums[number] = (own, exchange(sent))

    def finished(number, results):
        ends[number] = results[:3]
        back = results[3:]
        cuts = len(back) // core
        moving[number] = [
            (
                back[cut],
                [shift_expert(back[step * cuts + cut], 2, -step) for step in range(1, core)],
            )
            for cut in range(cuts)
        ]

    def finish_chunk(number, later=None):
        own, arrived, across = order.enter(*sums[number], around.get(later))
        if number == last:
            order.leave(*arrived)
            for earlier in range(1, number - 1):
                next_outer(earlier)
            own, arrived = order.enter(own, arrived)
        x_rows, grad, term, weight, pick = picked[number][:5]
        left = (own, arrived, grad, weight, pick, route_cols)
        if later is None:
            results = finish(*left, gate_w, up_w, down_w, core * cuts_of(number))
            order.leave(*results[3:])
            finished(number, results)
        else:
            made, results = finish_and_project(
                left, ready_parts(across), *tables, slots, gate_w, up_w, down_w, core * cuts_of(number)
            )
            order.leave(made[6], *results[3:])
            projected(later, made)
            finished(number, results)

    def next_inner(number):
        (cuts,) = order.enter(moving[number])
        if len(cuts) == inner:
            groups_here = [[mine] + arrived for mine, arrived in cuts]
            mine, *others = merge_between(groups_here, [F32] + [BF] * (inner - 1))
        else:
            mine, *others = merge([cuts[0][0]] + cuts[0][1], inner)
        order.leave(mine, *others)
        held[number] = (mine, others)
        if number or not last:
            start_back(number)

    def next_outer(number):
        mine, arrived = order.enter(*moving[number])
        (total,) = merge([mine] + arrived, 1)
        if number:
            total = total.astype(BF)
        order.leave(total)
        finals[number] = shift_expert(total, 0, -number) if number else total

    pieces[0], tables = order.enter(payload, tables)
    payload = pieces[0]
    start_inner(0)
    start_outer(1)
    along[0], pieces = order.enter(along[0], pieces)
    order.leave(*along[0])
    start_core(0)
    if last:
        start_inner(1)
    start_outer(2)
    partial_sums(0)
    if last:
        start_core(1)
        partial_sums(1)
    if last > 1:
        if last > 2:
            start_inner(3)
        start_core(2)
    for number in range(last + 1):
        later = number + 2
        if later <= last:
            finish_chunk(number, later)
            if later < last:
                if later > 2:
                    start_inner(later + 1)
                start_core(later + 1)
                start_outer(later + 2)
        else:
            finish_chunk(number)
        if 0 < number < last:
            next_inner(number)
    add_up(range(1, last - 1))
    if last > 1:
        next_outer(last - 1)
    next_inner(last)

    def rows_of(table, index):
        return [table[number][index] for number in range(last + 1)]

    def joined(values):
        return jnp.concatenate(values, axis=0)

    hidden_all, out_all = order.enter(rows_of(ends, 0), rows_of(picked, 2))
    down_grad = dot_tn(joined(hidden_all), joined(out_all)).astype(BF)[None]
    order.leave(down_grad)
    next_outer(last)
    if last:
        next_inner(0)
        start_back(0)
    x_all, gate_all, up_all = order.enter(
        rows_of(picked, 0), rows_of(ends, 1), rows_of(ends, 2)
    )
    x_all = joined(x_all)
    gate_grad = dot_tn(x_all, joined(gate_all)).astype(BF)[None]
    up_grad = dot_tn(x_all, joined(up_all)).astype(BF)[None]
    order.leave(gate_grad, up_grad)
    if last:
        next_outer(0)
    (arrived,) = order.enter(list(finals.values()))
    final = add_all(arrived[0].astype(F32), arrived[1:]).astype(BF)
    parts = swap_groups([final[g * rows : (g + 1) * rows] for g in range(groups)])
    mixed = jnp.concatenate([value[:, :part] for value in parts], axis=1)
    tokens_grad = jnp.concatenate([value[:, part + extra :] for value in parts], axis=1)
    route_table = jnp.zeros((), F32)
    for value in parts:
        for number in range(3):
            start = part + number * experts
            route_table = route_table + value[:, start : start + experts].astype(F32)
    route_grad = jnp.sum(jnp.where(chosen, route_table[:, None, :], 0.0), axis=2)
    return (mixed, tokens_grad, route_grad, gate_grad, up_grad, down_grad)


def solution(mesh):
    return jax.shard_map(
        per_device,
        mesh=mesh,
        in_specs=(
            P(("dp", "expert"), None),
            P(("dp", "expert"), None),
            P(("dp", "expert"), None),
            P(("dp", "expert"), None),
            P("expert", "dp", None),
            P("expert", "dp", None),
            P("expert", None, "dp"),
        ),
        out_specs=(
            P(("dp", "expert"), None),
            P(("dp", "expert"), None),
            P(("dp", "expert"), None),
            P("expert", "dp", None),
            P("expert", "dp", None),
            P("expert", None, "dp"),
        ),
        check_vma=False,
    )
```

```python
import jax
import jax.numpy as jnp
import numpy as np
from jax import lax
from jax.experimental import pallas as pl
from jax.experimental.pallas import tpu as pltpu
from jax.sharding import PartitionSpec as P

BF = jnp.bfloat16
F32 = jnp.float32


def silu_parts(pre_act):
    sigmoid_val = jax.nn.sigmoid(pre_act)
    return (pre_act * sigmoid_val, sigmoid_val * (1.0 + pre_act * (1.0 - sigmoid_val)))


def dot_nn(first, second):
    return lax.dot_general(first, second, (((1,), (0,)), ((), ())), preferred_element_type=F32)


def dot_nt(first, second):
    return lax.dot_general(first, second, (((1,), (1,)), ((), ())), preferred_element_type=F32)


def dot_tn(first, second):
    return lax.dot_general(first, second, (((0,), (0,)), ((), ())), preferred_element_type=F32)


def shift_dp(value, step):
    groups = lax.axis_size("dp")
    return lax.ppermute(value, "dp", [(i, (i + step) % groups) for i in range(groups)])


def choose(parts, index):
    picked = parts[0]
    for number in range(1, len(parts)):
        picked = jnp.where(index == number, parts[number], picked)
    return picked


def swap_groups(parts):
    groups = len(parts)
    mine = lax.axis_index("dp")
    by_step = [choose(parts, mine)]
    for step in range(1, groups):
        by_step.append(shift_dp(choose(parts, (mine + step) % groups), step))
    return [choose(by_step, (mine - group) % groups) for group in range(groups)]


def exchange(sent):
    return [shift_dp(sent, step) for step in range(1, lax.axis_size("dp"))]


def add_all(total, arrived):
    for value in arrived:
        total = total + value.astype(F32)
    return total


class Order:
    def __init__(self):
        self.last = []

    def enter(self, *values):
        flat, tree = jax.tree.flatten(values)
        tied = lax.optimization_barrier(tuple(flat) + tuple(self.last))[: len(flat)]
        return jax.tree.unflatten(tree, tied)

    def leave(self, *values):
        self.last = list(values)


def factors(experts):
    core = 2 if experts % 2 == 0 else 1
    rest = experts // core
    inner = 1
    while rest % (inner * 2) == 0 and (inner * 2) ** 2 <= rest:
        inner = inner * 2
    return (rest // inner, inner, core)


def shift_expert(value, level, step):
    dims = factors(lax.axis_size("expert"))
    stride = 1
    for dim in dims[level + 1 :]:
        stride = stride * dim
    size = dims[level]
    pairs = []
    for source in range(lax.axis_size("expert")):
        place = source // stride % size
        pairs.append((source, source + ((place + step) % size - place) * stride))
    return lax.ppermute(value, "expert", pairs)


def shift_to_owner(value, dp_step, outer_step):
    groups, experts = lax.axis_size("dp"), lax.axis_size("expert")
    outer, inner, core = factors(experts)
    pairs = []
    for group in range(groups):
        for source in range(experts):
            place = source // (inner * core)
            target = source + ((place + outer_step) % outer - place) * inner * core
            pairs.append((group * experts + source, (group + dp_step) % groups * experts + target))
    return lax.ppermute(value, ("dp", "expert"), pairs)


def level_size(level):
    return factors(lax.axis_size("expert"))[level]


def gather_start(piece, level):
    return [piece] + [shift_expert(piece, level, step) for step in range(1, level_size(level))]


def three_pieces(value):
    high = lax.reduce_precision(value, 8, 7)
    rest = value - high
    mid = lax.reduce_precision(rest, 8, 7)
    return [high.astype(BF), mid.astype(BF), (rest - mid).astype(BF)]


def stacked_rows(values):
    return jnp.concatenate(values, axis=0) if len(values) > 1 else values[0]


def project_body(number_parts, part, experts, *refs):
    mask_ref, order_ref, base_ref = refs[:3]
    part_refs = refs[3 : 3 + number_parts]
    gate_ref, up_ref, down_ref = refs[3 + number_parts : 6 + number_parts]
    x_ref, grad_ref, term_ref, weight_ref, pick_ref, own_ref, sent_ref = refs[6 + number_parts :]

    @pl.when(pl.program_id(0) == 0)
    def _():
        slots = x_ref.shape[0]
        arrived = stacked_rows([ref[...] for ref in part_refs])
        count = arrived.shape[0]
        column = lax.broadcasted_iota(jnp.int32, (8, arrived.shape[1] - 2 * part), 1)
        expert = mask_ref[0, 0]
        mask = jnp.zeros(column.shape, F32)
        for number in range(3):
            mask = mask + jnp.where(column == number * experts + expert, 1.0, 0.0)
        mask = mask.astype(BF)
        weight = dot_nt(mask, arrived[:, 2 * part :])
        live = weight > 0.0
        place = dot_nn(jnp.where(live, 1.0, 0.0).astype(BF), order_ref[...])
        slot = jnp.where(live, place - 1.0 + base_ref[...], -1.0)[:1]
        index = lax.broadcasted_iota(jnp.int32, (slots, count), 0).astype(F32)
        pick = jnp.where(index == slot, 1.0, 0.0).astype(BF)
        pick_ref[...] = pick
        x_ref[...] = dot_nn(pick, arrived[:, :part]).astype(BF)
        grad = dot_nn(pick, arrived[:, part : 2 * part])
        grad_ref[...] = grad.astype(BF)
        chosen = dot_nn(pick, arrived[:, 2 * part :]) * mask[:1].astype(F32)
        weight_rows = jnp.sum(chosen, axis=1, keepdims=True)
        weight_ref[...] = jnp.broadcast_to(weight_rows, weight_ref.shape)
        term_ref[...] = (weight_rows * grad).astype(BF)

    x_rows = x_ref[...]
    values = (
        dot_nn(x_rows, gate_ref[...]),
        dot_nn(x_rows, up_ref[...]),
        dot_nt(term_ref[...], down_ref[...]),
    )
    for number, value in enumerate(values):
        own_ref[number] = value
        sent_ref[number] = value.astype(BF)


def project(parts, mask, order, base, slots, gate_w, up_w, down_w):
    experts = lax.axis_size("expert")
    part, hidden = gate_w.shape
    tile = min(256, hidden)
    count = sum(value.shape[0] for value in parts)
    whole = lambda shape: pl.BlockSpec(shape, lambda j: (0,) * len(shape))
    columns = lambda rows: pl.BlockSpec((rows, tile), lambda j: (0, j))
    stacked = pl.BlockSpec((3, slots, tile), lambda j: (0, 0, j))
    row_out = jax.ShapeDtypeStruct((slots, part), BF)
    return pl.pallas_call(
        lambda *refs: project_body(len(parts), part, experts, *refs),
        grid=(hidden // tile,),
        in_specs=[pl.BlockSpec(memory_space=pltpu.SMEM), whole(order.shape), whole(base.shape)]
        + [whole(value.shape) for value in parts]
        + [columns(part), columns(part), pl.BlockSpec((tile, part), lambda j: (j, 0))],
        out_specs=[whole((slots, part))] * 3
        + [whole((slots, 128)), whole((slots, count)), stacked, stacked],
        out_shape=[row_out] * 3
        + [
            jax.ShapeDtypeStruct((slots, 128), F32),
            jax.ShapeDtypeStruct((slots, count), BF),
            jax.ShapeDtypeStruct((3, slots, hidden), F32),
            jax.ShapeDtypeStruct((3, slots, hidden), BF),
        ],
        compiler_params=pltpu.CompilerParams(vmem_limit_bytes=56 * 2**20),
        name="project",
    )(mask, order, base, *parts, gate_w, up_w, down_w)


def merge(values, pieces):
    total = add_all(values[0].astype(F32), values[1:])
    rows = total.shape[0] // pieces
    parts = [total[number * rows : (number + 1) * rows] for number in range(pieces)]
    return parts[:1] + [part.astype(BF) for part in parts[1:]]


def merge_between(groups, kinds):
    sizes = [len(group) for group in groups]

    def body(*refs):
        start = 0
        for size, out in zip(sizes, refs[sum(sizes) :]):
            total = add_all(refs[start][...].astype(F32), [ref[...] for ref in refs[start + 1 : start + size]])
            out[...] = total.astype(out.dtype)
            start += size

    return pl.pallas_call(
        body,
        out_shape=[
            jax.ShapeDtypeStruct(group[0].shape, kind) for group, kind in zip(groups, kinds)
        ],
        compiler_params=pltpu.CompilerParams(vmem_limit_bytes=56 * 2**20),
        name="merge",
    )(*[value for group in groups for value in group])


def finish_body(number_sent, number_parts, *refs):
    own_ref = refs[0]
    sent_refs = refs[1 : 1 + number_sent]
    grad_ref, weight_ref, pick_ref, route_ref, gate_ref, up_ref, down_ref = refs[
        1 + number_sent : 8 + number_sent
    ]
    hidden_ref, gate_term_ref, up_term_ref = refs[8 + number_sent : 11 + number_sent]
    back_refs = refs[11 + number_sent : 11 + number_sent + number_parts]
    out_acc, in_acc = refs[11 + number_sent + number_parts :]
    step = pl.program_id(0)
    gate_pre, up_pre, hidden_grad = (
        add_all(own_ref[number], [ref[number] for ref in sent_refs]) for number in range(3)
    )
    act_val, act_slope = silu_parts(gate_pre)
    hidden = (act_val * up_pre).astype(BF)
    gate_term = (hidden_grad * up_pre * act_slope).astype(BF)
    up_term = (hidden_grad * act_val).astype(BF)
    hidden_ref[...] = hidden
    gate_term_ref[...] = gate_term
    up_term_ref[...] = up_term
    out_part = dot_nn(hidden, down_ref[...])
    in_part = dot_nt(gate_term, gate_ref[...]) + dot_nt(up_term, up_ref[...])

    @pl.when(step == 0)
    def _():
        out_acc[...] = out_part
        in_acc[...] = in_part

    @pl.when(step > 0)
    def _():
        out_acc[...] += out_part
        in_acc[...] += in_part

    @pl.when(step == pl.num_programs(0) - 1)
    def _():
        part = out_acc.shape[1]
        extra = route_ref.shape[1]
        expert_out = out_acc[...].astype(BF).astype(F32)
        rest = jnp.sum(grad_ref[...].astype(F32) * expert_out, axis=1, keepdims=True)
        route = jnp.zeros((rest.shape[0], extra), F32)
        for number in range(3):
            piece = rest.astype(BF).astype(F32)
            route = route + piece * route_ref[number : number + 1]
            rest = rest - piece
        pick = pick_ref[...]
        weighted = (weight_ref[:, :1] * expert_out).astype(BF)
        backs = (
            dot_tn(pick, weighted).astype(BF),
            dot_tn(pick, route.astype(BF)).astype(BF),
            dot_tn(pick, in_acc[...].astype(BF)).astype(BF),
        )
        rows = back_refs[0].shape[0]
        for number, ref in enumerate(back_refs):
            here = slice(number * rows, (number + 1) * rows)
            ref[:, :part] = backs[0][here]
            ref[:, part : part + extra] = backs[1][here]
            ref[:, part + extra :] = backs[2][here]


def finish(own, sent, grad, weight, pick, route, gate_w, up_w, down_w, number_parts):
    part, hidden = gate_w.shape
    tile = min(256, hidden)
    slots, count = pick.shape
    rows = count // number_parts
    wide = 2 * part + route.shape[1]
    whole = lambda shape: pl.BlockSpec(shape, lambda j: (0,) * len(shape))
    columns = lambda size: pl.BlockSpec((size, tile), lambda j: (0, j))
    stacked = pl.BlockSpec((3, slots, tile), lambda j: (0, 0, j))
    return pl.pallas_call(
        lambda *refs: finish_body(len(sent), number_parts, *refs),
        grid=(hidden // tile,),
        in_specs=[stacked] * (1 + len(sent))
        + [whole(value.shape) for value in (grad, weight, pick, route)]
        + [columns(part), columns(part), pl.BlockSpec((tile, part), lambda j: (j, 0))],
        out_specs=[columns(slots)] * 3 + [whole((rows, wide))] * number_parts,
        out_shape=[jax.ShapeDtypeStruct((slots, hidden), BF)] * 3
        + [jax.ShapeDtypeStruct((rows, wide), BF)] * number_parts,
        scratch_shapes=[pltpu.VMEM((slots, part), F32), pltpu.VMEM((slots, part), F32)],
        compiler_params=pltpu.CompilerParams(vmem_limit_bytes=56 * 2**20),
        name="finish",
    )(own, *sent, grad, weight, pick, route, gate_w, up_w, down_w)


def finish_and_project(left, parts, mask, order, base, slots, gate_w, up_w, down_w, number_parts):
    own, sent, grad, weight, pick, route = left
    experts = lax.axis_size("expert")
    part, hidden = gate_w.shape
    tile = min(256, hidden)
    count = sum(value.shape[0] for value in parts)
    rows = pick.shape[1] // number_parts
    wide = 2 * part + route.shape[1]
    whole = lambda shape: pl.BlockSpec(shape, lambda j: (0,) * len(shape))
    columns = lambda size: pl.BlockSpec((size, tile), lambda j: (0, j))
    stacked = pl.BlockSpec((3, slots, tile), lambda j: (0, 0, j))
    first = 3 + len(parts)
    second = first + 5 + len(sent)
    weights = second + 3

    def body(*refs):
        outs = refs[weights : weights + 7]
        ends = refs[weights + 7 :]
        finish_body(len(sent), number_parts, *refs[first:weights], *ends)
        project_body(len(parts), part, experts, *refs[:first], *refs[second:weights], *outs)

    results = pl.pallas_call(
        body,
        grid=(hidden // tile,),
        in_specs=[pl.BlockSpec(memory_space=pltpu.SMEM)]
        + [whole(value.shape) for value in (order, base, *parts)]
        + [stacked] * (1 + len(sent))
        + [whole(value.shape) for value in (grad, weight, pick, route)]
        + [columns(part), columns(part), pl.BlockSpec((tile, part), lambda j: (j, 0))],
        out_specs=[whole((slots, part))] * 3
        + [whole((slots, 128)), whole((slots, count)), stacked, stacked]
        + [columns(slots)] * 3
        + [whole((rows, wide))] * number_parts,
        out_shape=[jax.ShapeDtypeStruct((slots, part), BF)] * 3
        + [
            jax.ShapeDtypeStruct((slots, 128), F32),
            jax.ShapeDtypeStruct((slots, count), BF),
            jax.ShapeDtypeStruct((3, slots, hidden), F32),
            jax.ShapeDtypeStruct((3, slots, hidden), BF),
        ]
        + [jax.ShapeDtypeStruct((slots, hidden), BF)] * 3
        + [jax.ShapeDtypeStruct((rows, wide), BF)] * number_parts,
        scratch_shapes=[pltpu.VMEM((slots, part), F32), pltpu.VMEM((slots, part), F32)],
        compiler_params=pltpu.CompilerParams(vmem_limit_bytes=56 * 2**20),
        name="step",
    )(mask, order, base, *parts, own, *sent, grad, weight, pick, route, gate_w, up_w, down_w)
    return results[:7], results[7:]


def per_device(tokens, expert_ids, route_weights, out_grad, gate_weight, up_weight, down_weight):
    experts = lax.axis_size("expert")
    groups = lax.axis_size("dp")
    my_expert = lax.axis_index("expert")
    mine_dp = lax.axis_index("dp")
    outer, inner, core = factors(experts)
    rows, width = tokens.shape
    hidden_width = gate_weight.shape[2]
    choices = expert_ids.shape[1]
    part = width // groups
    most = min(rows, 3 * rows * choices // (2 * experts))
    extra = -(-3 * experts // 128) * 128
    gate_w, up_w, down_w = gate_weight[0], up_weight[0], down_weight[0]

    chosen = expert_ids[:, :, None] == jnp.arange(experts, dtype=jnp.int32)[None, None, :]
    weight_table = jnp.sum(jnp.where(chosen, route_weights[:, :, None], 0.0), axis=1)
    weight_cols = jnp.concatenate(
        three_pieces(weight_table) + [jnp.zeros((rows, extra - 3 * experts), BF)], axis=1
    )
    payload = jnp.concatenate(
        swap_groups(
            [
                jnp.concatenate(
                    [
                        tokens[:, g * part : (g + 1) * part],
                        out_grad[:, g * part : (g + 1) * part],
                        weight_cols,
                    ],
                    axis=1,
                )
                for g in range(groups)
            ]
        ),
        axis=0,
    )

    column = jnp.arange(extra, dtype=jnp.int32)[None, :]
    route_cols = (
        column == jnp.arange(8, dtype=jnp.int32)[:, None] * experts + my_expert
    ) & (jnp.arange(8)[:, None] < 3)
    route_cols = route_cols.astype(F32)
    last = outer - 1
    count = inner * core * groups * rows
    slots = inner * core * groups * most
    token = np.arange(count)
    block = token // rows
    before = (block[:, None] == block[None, :]) & (token[:, None] <= token[None, :])
    base = np.tile((block * most).astype(np.float32)[None], (8, 1))
    tables = (
        my_expert.astype(jnp.int32).reshape(1, 1),
        jnp.asarray(before.astype(np.float32), BF),
        jnp.asarray(base),
    )
    order = Order()
    pieces, along, around, picked, sums, ends = {0: payload}, {}, {}, {}, {}, {}
    moving, finals, held = {}, {}, {}

    def start_outer(number):
        if number < outer:
            (tied,) = order.enter(payload)
            pieces[number] = shift_expert(tied, 0, number)

    def start_inner(number):
        (mine,) = order.enter(pieces[number])
        along[number] = gather_start(mine, 1)
        around[number] = [] if number else [gather_start(mine, 2)]

    def add_up(numbers):
        if len(numbers):
            (arrived,) = order.enter([finals.pop(number) for number in numbers])
            total = add_all(arrived[0].astype(F32), arrived[1:])
            order.leave(total)
            finals[numbers[0]] = total

    def start_back(number):
        mine, others = held[number]
        (others,) = order.enter(others)
        moving[number] = (
            mine,
            [shift_expert(other, 1, -step) for step, other in enumerate(others, 1)],
        )

    def start_core(number):
        (mine,) = order.enter(along[number])
        order.leave(*mine)
        around[number] = around[number] + [
            gather_start(value, 2) for value in (mine if number else mine[1:])
        ]

    def cuts_of(number):
        return inner if 0 < number < last else 1

    def ready_parts(across):
        return [piece[index] for index in range(core) for piece in across]

    def partial_sums(number):
        across, tied = order.enter(around[number], pieces.get(2) if number == 1 else None)
        if number == 1 and outer > 2:
            pieces[2] = tied
            if outer > 3:
                late, _ = lax.optimization_barrier((payload, tied))
                pieces[3] = shift_expert(late, 0, 3)
            along[2] = gather_start(tied, 1)
            around[2] = []
        projected(
            number, project(ready_parts(across), *tables, slots, gate_w, up_w, down_w)
        )
        order.leave(picked[number][6])

    def projected(number, results):
        picked[number] = results
        own, sent = results[5:]
        sums[number] = (own, exchange(sent))

    def finished(number, results):
        ends[number] = results[:3]
        back = results[3:]
        cuts = len(back) // core
        moving[number] = [
            (
                back[cut],
                [shift_expert(back[step * cuts + cut], 2, -step) for step in range(1, core)],
            )
            for cut in range(cuts)
        ]

    def finish_chunk(number, later=None):
        own, arrived, across = order.enter(*sums[number], around.get(later))
        if number == last:
            order.leave(*arrived)
            for earlier in range(1, number - 1):
                next_outer(earlier)
            own, arrived = order.enter(own, arrived)
        x_rows, grad, term, weight, pick = picked[number][:5]
        left = (own, arrived, grad, weight, pick, route_cols)
        if later is None:
            results = finish(*left, gate_w, up_w, down_w, core * cuts_of(number))
            order.leave(*results[3:])
            finished(number, results)
        else:
            made, results = finish_and_project(
                left, ready_parts(across), *tables, slots, gate_w, up_w, down_w, core * cuts_of(number)
            )
            order.leave(made[6], *results[3:])
            projected(later, made)
            finished(number, results)

    def next_inner(number):
        (cuts,) = order.enter(moving[number])
        if len(cuts) == inner:
            groups_here = [[mine] + arrived for mine, arrived in cuts]
            mine, *others = merge_between(groups_here, [F32] + [BF] * (inner - 1))
        else:
            mine, *others = merge([cuts[0][0]] + cuts[0][1], inner)
        order.leave(mine, *others)
        held[number] = (mine, others)
        if number or not last:
            start_back(number)

    def next_outer(number):
        mine, arrived = order.enter(*moving[number])
        (total,) = merge([mine] + arrived, 1)
        if number and number == last:
            total = total.astype(BF)
            order.leave(total)
            parts = [total[g * rows : (g + 1) * rows] for g in range(groups)]
            finals[number] = [
                shift_to_owner(choose(parts, (mine_dp + step) % groups), step, -number)
                for step in range(groups)
            ]
            return
        if number:
            total = total.astype(BF)
        order.leave(total)
        finals[number] = shift_expert(total, 0, -number) if number else total

    pieces[0], tables = order.enter(payload, tables)
    payload = pieces[0]
    start_inner(0)
    start_outer(1)
    along[0], pieces = order.enter(along[0], pieces)
    order.leave(*along[0])
    start_core(0)
    if last:
        start_inner(1)
    start_outer(2)
    partial_sums(0)
    if last:
        start_core(1)
        partial_sums(1)
    if last > 1:
        if last > 2:
            start_inner(3)
        start_core(2)
    for number in range(last + 1):
        later = number + 2
        if later <= last:
            finish_chunk(number, later)
            if later < last:
                if later > 2:
                    start_inner(later + 1)
                start_core(later + 1)
                start_outer(later + 2)
        else:
            finish_chunk(number)
        if 0 < number < last:
            next_inner(number)
    add_up(range(1, last - 1))
    if last > 1:
        next_outer(last - 1)
    next_inner(last)

    def rows_of(table, index):
        return [table[number][index] for number in range(last + 1)]

    def joined(values):
        return jnp.concatenate(values, axis=0)

    hidden_all, out_all = order.enter(rows_of(ends, 0), rows_of(picked, 2))
    down_grad = dot_tn(joined(hidden_all), joined(out_all)).astype(BF)[None]
    order.leave(down_grad)
    next_outer(last)
    if last:
        next_inner(0)
        start_back(0)
    x_all, gate_all = order.enter(rows_of(picked, 0), rows_of(ends, 1))
    x_all = joined(x_all)
    gate_grad = dot_tn(x_all, joined(gate_all)).astype(BF)[None]
    order.leave(gate_grad)
    if last:
        next_outer(0)
    straight = finals.pop(last) if last else None
    (arrived,) = order.enter(list(finals.values()))
    total = add_all(arrived[0].astype(F32), arrived[1:])
    sums_here = [total[g * rows : (g + 1) * rows] for g in range(groups)]
    by_step = [choose(sums_here, mine_dp)]
    for step in range(1, groups):
        by_step.append(shift_dp(choose(sums_here, (mine_dp + step) % groups).astype(BF), step))
    order.leave(total)
    x_all, up_all = order.enter(x_all, rows_of(ends, 2))
    up_grad = dot_tn(x_all, joined(up_all)).astype(BF)[None]
    order.leave(up_grad)
    if last:
        by_step, straight = order.enter(by_step, straight)
        by_step = [value.astype(F32) + add.astype(F32) for value, add in zip(by_step, straight)]
    by_step = [value.astype(BF) for value in by_step]
    parts = [choose(by_step, (mine_dp - g) % groups) for g in range(groups)]
    mixed = jnp.concatenate([value[:, :part] for value in parts], axis=1)
    tokens_grad = jnp.concatenate([value[:, part + extra :] for value in parts], axis=1)
    route_table = jnp.zeros((), F32)
    for value in parts:
        for number in range(3):
            start = part + number * experts
            route_table = route_table + value[:, start : start + experts].astype(F32)
    route_grad = jnp.sum(jnp.where(chosen, route_table[:, None, :], 0.0), axis=2)
    return (mixed, tokens_grad, route_grad, gate_grad, up_grad, down_grad)


def solution(mesh):
    return jax.shard_map(
        per_device,
        mesh=mesh,
        in_specs=(
            P(("dp", "expert"), None),
            P(("dp", "expert"), None),
            P(("dp", "expert"), None),
            P(("dp", "expert"), None),
            P("expert", "dp", None),
            P("expert", "dp", None),
            P("expert", None, "dp"),
        ),
        out_specs=(
            P(("dp", "expert"), None),
            P(("dp", "expert"), None),
            P(("dp", "expert"), None),
            P("expert", "dp", None),
            P("expert", "dp", None),
            P("expert", None, "dp"),
        ),
        check_vma=False,
    )
```

```python
import jax
import jax.numpy as jnp
import numpy as np
from jax import lax
from jax.experimental import pallas as pl
from jax.experimental.pallas import tpu as pltpu
from jax.sharding import PartitionSpec as P

BF = jnp.bfloat16
F32 = jnp.float32


def silu_parts(pre_act):
    sigmoid_val = jax.nn.sigmoid(pre_act)
    return (pre_act * sigmoid_val, sigmoid_val * (1.0 + pre_act * (1.0 - sigmoid_val)))


def dot_nn(first, second):
    return lax.dot_general(first, second, (((1,), (0,)), ((), ())), preferred_element_type=F32)


def dot_nt(first, second):
    return lax.dot_general(first, second, (((1,), (1,)), ((), ())), preferred_element_type=F32)


def dot_tn(first, second):
    return lax.dot_general(first, second, (((0,), (0,)), ((), ())), preferred_element_type=F32)


def shift_dp(value, step):
    groups = lax.axis_size("dp")
    return lax.ppermute(value, "dp", [(i, (i + step) % groups) for i in range(groups)])


def choose(parts, index):
    picked = parts[0]
    for number in range(1, len(parts)):
        picked = jnp.where(index == number, parts[number], picked)
    return picked


def swap_groups(parts):
    groups = len(parts)
    mine = lax.axis_index("dp")
    by_step = [choose(parts, mine)]
    for step in range(1, groups):
        by_step.append(shift_dp(choose(parts, (mine + step) % groups), step))
    return [choose(by_step, (mine - group) % groups) for group in range(groups)]


def exchange(sent):
    return [shift_dp(sent, step) for step in range(1, lax.axis_size("dp"))]


def add_all(total, arrived):
    for value in arrived:
        total = total + value.astype(F32)
    return total


class Order:
    def __init__(self):
        self.last = []

    def enter(self, *values):
        flat, tree = jax.tree.flatten(values)
        tied = lax.optimization_barrier(tuple(flat) + tuple(self.last))[: len(flat)]
        return jax.tree.unflatten(tree, tied)

    def leave(self, *values):
        self.last = list(values)


def factors(experts):
    core = 2 if experts % 2 == 0 else 1
    rest = experts // core
    inner = 1
    while rest % (inner * 2) == 0 and (inner * 2) ** 2 <= rest:
        inner = inner * 2
    return (rest // inner, inner, core)


def shift_expert(value, level, step):
    dims = factors(lax.axis_size("expert"))
    stride = 1
    for dim in dims[level + 1 :]:
        stride = stride * dim
    size = dims[level]
    pairs = []
    for source in range(lax.axis_size("expert")):
        place = source // stride % size
        pairs.append((source, source + ((place + step) % size - place) * stride))
    return lax.ppermute(value, "expert", pairs)


def shift_to_owner(value, dp_step, outer_step):
    groups, experts = lax.axis_size("dp"), lax.axis_size("expert")
    outer, inner, core = factors(experts)
    pairs = []
    for group in range(groups):
        for source in range(experts):
            place = source // (inner * core)
            target = source + ((place + outer_step) % outer - place) * inner * core
            pairs.append((group * experts + source, (group + dp_step) % groups * experts + target))
    return lax.ppermute(value, ("dp", "expert"), pairs)


def level_size(level):
    return factors(lax.axis_size("expert"))[level]


def gather_start(piece, level):
    return [piece] + [shift_expert(piece, level, step) for step in range(1, level_size(level))]


def three_pieces(value):
    high = lax.reduce_precision(value, 8, 7)
    rest = value - high
    mid = lax.reduce_precision(rest, 8, 7)
    return [high.astype(BF), mid.astype(BF), (rest - mid).astype(BF)]


def stacked_rows(values):
    return jnp.concatenate(values, axis=0) if len(values) > 1 else values[0]


def project_body(number_parts, part, experts, *refs):
    mask_ref, order_ref, base_ref = refs[:3]
    part_refs = refs[3 : 3 + number_parts]
    gate_ref, up_ref, down_ref = refs[3 + number_parts : 6 + number_parts]
    x_ref, grad_ref, term_ref, weight_ref, pick_ref, own_ref, sent_ref = refs[6 + number_parts :]

    @pl.when(pl.program_id(0) == 0)
    def _():
        slots = x_ref.shape[0]
        arrived = stacked_rows([ref[...] for ref in part_refs])
        count = arrived.shape[0]
        column = lax.broadcasted_iota(jnp.int32, (8, arrived.shape[1] - 2 * part), 1)
        expert = mask_ref[0, 0]
        mask = jnp.zeros(column.shape, F32)
        for number in range(3):
            mask = mask + jnp.where(column == number * experts + expert, 1.0, 0.0)
        mask = mask.astype(BF)
        weight = dot_nt(mask, arrived[:, 2 * part :])
        live = weight > 0.0
        place = dot_nn(jnp.where(live, 1.0, 0.0).astype(BF), order_ref[...])
        slot = jnp.where(live, place - 1.0 + base_ref[...], -1.0)[:1]
        index = lax.broadcasted_iota(jnp.int32, (slots, count), 0).astype(F32)
        pick = jnp.where(index == slot, 1.0, 0.0).astype(BF)
        pick_ref[...] = pick
        x_ref[...] = dot_nn(pick, arrived[:, :part]).astype(BF)
        grad = dot_nn(pick, arrived[:, part : 2 * part])
        grad_ref[...] = grad.astype(BF)
        chosen = dot_nn(pick, arrived[:, 2 * part :]) * mask[:1].astype(F32)
        weight_rows = jnp.sum(chosen, axis=1, keepdims=True)
        weight_ref[...] = jnp.broadcast_to(weight_rows, weight_ref.shape)
        term_ref[...] = (weight_rows * grad).astype(BF)

    x_rows = x_ref[...]
    values = (
        dot_nn(x_rows, gate_ref[...]),
        dot_nn(x_rows, up_ref[...]),
        dot_nt(term_ref[...], down_ref[...]),
    )
    for number, value in enumerate(values):
        own_ref[number] = value
        sent_ref[number] = value.astype(BF)


def project(parts, mask, order, base, slots, gate_w, up_w, down_w):
    experts = lax.axis_size("expert")
    part, hidden = gate_w.shape
    tile = min(256, hidden)
    count = sum(value.shape[0] for value in parts)
    whole = lambda shape: pl.BlockSpec(shape, lambda j: (0,) * len(shape))
    columns = lambda rows: pl.BlockSpec((rows, tile), lambda j: (0, j))
    stacked = pl.BlockSpec((3, slots, tile), lambda j: (0, 0, j))
    row_out = jax.ShapeDtypeStruct((slots, part), BF)
    return pl.pallas_call(
        lambda *refs: project_body(len(parts), part, experts, *refs),
        grid=(hidden // tile,),
        in_specs=[pl.BlockSpec(memory_space=pltpu.SMEM), whole(order.shape), whole(base.shape)]
        + [whole(value.shape) for value in parts]
        + [columns(part), columns(part), pl.BlockSpec((tile, part), lambda j: (j, 0))],
        out_specs=[whole((slots, part))] * 3
        + [whole((slots, 128)), whole((slots, count)), stacked, stacked],
        out_shape=[row_out] * 3
        + [
            jax.ShapeDtypeStruct((slots, 128), F32),
            jax.ShapeDtypeStruct((slots, count), BF),
            jax.ShapeDtypeStruct((3, slots, hidden), F32),
            jax.ShapeDtypeStruct((3, slots, hidden), BF),
        ],
        compiler_params=pltpu.CompilerParams(vmem_limit_bytes=56 * 2**20),
        name="project",
    )(mask, order, base, *parts, gate_w, up_w, down_w)


def merge(values, pieces):
    total = add_all(values[0].astype(F32), values[1:])
    rows = total.shape[0] // pieces
    parts = [total[number * rows : (number + 1) * rows] for number in range(pieces)]
    return parts[:1] + [part.astype(BF) for part in parts[1:]]


def merge_between(groups, kinds):
    sizes = [len(group) for group in groups]

    def body(*refs):
        start = 0
        for size, out in zip(sizes, refs[sum(sizes) :]):
            total = add_all(refs[start][...].astype(F32), [ref[...] for ref in refs[start + 1 : start + size]])
            out[...] = total.astype(out.dtype)
            start += size

    return pl.pallas_call(
        body,
        out_shape=[
            jax.ShapeDtypeStruct(group[0].shape, kind) for group, kind in zip(groups, kinds)
        ],
        compiler_params=pltpu.CompilerParams(vmem_limit_bytes=56 * 2**20),
        name="merge",
    )(*[value for group in groups for value in group])


def finish_body(number_sent, number_parts, *refs):
    own_ref = refs[0]
    sent_refs = refs[1 : 1 + number_sent]
    grad_ref, weight_ref, pick_ref, route_ref, gate_ref, up_ref, down_ref = refs[
        1 + number_sent : 8 + number_sent
    ]
    hidden_ref, gate_term_ref, up_term_ref = refs[8 + number_sent : 11 + number_sent]
    back_refs = refs[11 + number_sent : 11 + number_sent + number_parts]
    out_acc, in_acc = refs[11 + number_sent + number_parts :]
    step = pl.program_id(0)
    gate_pre, up_pre, hidden_grad = (
        add_all(own_ref[number], [ref[number] for ref in sent_refs]) for number in range(3)
    )
    act_val, act_slope = silu_parts(gate_pre)
    hidden = (act_val * up_pre).astype(BF)
    gate_term = (hidden_grad * up_pre * act_slope).astype(BF)
    up_term = (hidden_grad * act_val).astype(BF)
    hidden_ref[...] = hidden
    gate_term_ref[...] = gate_term
    up_term_ref[...] = up_term
    out_part = dot_nn(hidden, down_ref[...])
    in_part = dot_nt(gate_term, gate_ref[...]) + dot_nt(up_term, up_ref[...])

    @pl.when(step == 0)
    def _():
        out_acc[...] = out_part
        in_acc[...] = in_part

    @pl.when(step > 0)
    def _():
        out_acc[...] += out_part
        in_acc[...] += in_part

    @pl.when(step == pl.num_programs(0) - 1)
    def _():
        part = out_acc.shape[1]
        extra = route_ref.shape[1]
        expert_out = out_acc[...].astype(BF).astype(F32)
        rest = jnp.sum(grad_ref[...].astype(F32) * expert_out, axis=1, keepdims=True)
        route = jnp.zeros((rest.shape[0], extra), F32)
        for number in range(3):
            piece = rest.astype(BF).astype(F32)
            route = route + piece * route_ref[number : number + 1]
            rest = rest - piece
        pick = pick_ref[...]
        weighted = (weight_ref[:, :1] * expert_out).astype(BF)
        backs = (
            dot_tn(pick, weighted).astype(BF),
            dot_tn(pick, route.astype(BF)).astype(BF),
            dot_tn(pick, in_acc[...].astype(BF)).astype(BF),
        )
        rows = back_refs[0].shape[0]
        for number, ref in enumerate(back_refs):
            here = slice(number * rows, (number + 1) * rows)
            ref[:, :part] = backs[0][here]
            ref[:, part : part + extra] = backs[1][here]
            ref[:, part + extra :] = backs[2][here]


def finish(own, sent, grad, weight, pick, route, gate_w, up_w, down_w, number_parts):
    part, hidden = gate_w.shape
    tile = min(256, hidden)
    slots, count = pick.shape
    rows = count // number_parts
    wide = 2 * part + route.shape[1]
    whole = lambda shape: pl.BlockSpec(shape, lambda j: (0,) * len(shape))
    columns = lambda size: pl.BlockSpec((size, tile), lambda j: (0, j))
    stacked = pl.BlockSpec((3, slots, tile), lambda j: (0, 0, j))
    return pl.pallas_call(
        lambda *refs: finish_body(len(sent), number_parts, *refs),
        grid=(hidden // tile,),
        in_specs=[stacked] * (1 + len(sent))
        + [whole(value.shape) for value in (grad, weight, pick, route)]
        + [columns(part), columns(part), pl.BlockSpec((tile, part), lambda j: (j, 0))],
        out_specs=[columns(slots)] * 3 + [whole((rows, wide))] * number_parts,
        out_shape=[jax.ShapeDtypeStruct((slots, hidden), BF)] * 3
        + [jax.ShapeDtypeStruct((rows, wide), BF)] * number_parts,
        scratch_shapes=[pltpu.VMEM((slots, part), F32), pltpu.VMEM((slots, part), F32)],
        compiler_params=pltpu.CompilerParams(vmem_limit_bytes=56 * 2**20),
        name="finish",
    )(own, *sent, grad, weight, pick, route, gate_w, up_w, down_w)


def finish_and_project(left, parts, mask, order, base, slots, gate_w, up_w, down_w, number_parts):
    own, sent, grad, weight, pick, route = left
    experts = lax.axis_size("expert")
    part, hidden = gate_w.shape
    tile = min(256, hidden)
    count = sum(value.shape[0] for value in parts)
    rows = pick.shape[1] // number_parts
    wide = 2 * part + route.shape[1]
    whole = lambda shape: pl.BlockSpec(shape, lambda j: (0,) * len(shape))
    columns = lambda size: pl.BlockSpec((size, tile), lambda j: (0, j))
    stacked = pl.BlockSpec((3, slots, tile), lambda j: (0, 0, j))
    first = 3 + len(parts)
    second = first + 5 + len(sent)
    weights = second + 3

    def body(*refs):
        outs = refs[weights : weights + 7]
        ends = refs[weights + 7 :]
        finish_body(len(sent), number_parts, *refs[first:weights], *ends)
        project_body(len(parts), part, experts, *refs[:first], *refs[second:weights], *outs)

    results = pl.pallas_call(
        body,
        grid=(hidden // tile,),
        in_specs=[pl.BlockSpec(memory_space=pltpu.SMEM)]
        + [whole(value.shape) for value in (order, base, *parts)]
        + [stacked] * (1 + len(sent))
        + [whole(value.shape) for value in (grad, weight, pick, route)]
        + [columns(part), columns(part), pl.BlockSpec((tile, part), lambda j: (j, 0))],
        out_specs=[whole((slots, part))] * 3
        + [whole((slots, 128)), whole((slots, count)), stacked, stacked]
        + [columns(slots)] * 3
        + [whole((rows, wide))] * number_parts,
        out_shape=[jax.ShapeDtypeStruct((slots, part), BF)] * 3
        + [
            jax.ShapeDtypeStruct((slots, 128), F32),
            jax.ShapeDtypeStruct((slots, count), BF),
            jax.ShapeDtypeStruct((3, slots, hidden), F32),
            jax.ShapeDtypeStruct((3, slots, hidden), BF),
        ]
        + [jax.ShapeDtypeStruct((slots, hidden), BF)] * 3
        + [jax.ShapeDtypeStruct((rows, wide), BF)] * number_parts,
        scratch_shapes=[pltpu.VMEM((slots, part), F32), pltpu.VMEM((slots, part), F32)],
        compiler_params=pltpu.CompilerParams(vmem_limit_bytes=56 * 2**20),
        name="step",
    )(mask, order, base, *parts, own, *sent, grad, weight, pick, route, gate_w, up_w, down_w)
    return results[:7], results[7:]


def per_device(tokens, expert_ids, route_weights, out_grad, gate_weight, up_weight, down_weight):
    experts = lax.axis_size("expert")
    groups = lax.axis_size("dp")
    my_expert = lax.axis_index("expert")
    mine_dp = lax.axis_index("dp")
    outer, inner, core = factors(experts)
    rows, width = tokens.shape
    hidden_width = gate_weight.shape[2]
    choices = expert_ids.shape[1]
    part = width // groups
    most = min(rows, 3 * rows * choices // (2 * experts))
    extra = -(-3 * experts // 128) * 128
    gate_w, up_w, down_w = gate_weight[0], up_weight[0], down_weight[0]

    chosen = expert_ids[:, :, None] == jnp.arange(experts, dtype=jnp.int32)[None, None, :]
    weight_table = jnp.sum(jnp.where(chosen, route_weights[:, :, None], 0.0), axis=1)
    weight_cols = jnp.concatenate(
        three_pieces(weight_table) + [jnp.zeros((rows, extra - 3 * experts), BF)], axis=1
    )
    payload = jnp.concatenate(
        swap_groups(
            [
                jnp.concatenate(
                    [
                        tokens[:, g * part : (g + 1) * part],
                        out_grad[:, g * part : (g + 1) * part],
                        weight_cols,
                    ],
                    axis=1,
                )
                for g in range(groups)
            ]
        ),
        axis=0,
    )

    column = jnp.arange(extra, dtype=jnp.int32)[None, :]
    route_cols = (
        column == jnp.arange(8, dtype=jnp.int32)[:, None] * experts + my_expert
    ) & (jnp.arange(8)[:, None] < 3)
    route_cols = route_cols.astype(F32)
    last = outer - 1
    count = inner * core * groups * rows
    slots = inner * core * groups * most
    token = np.arange(count)
    block = token // rows
    before = (block[:, None] == block[None, :]) & (token[:, None] <= token[None, :])
    base = np.tile((block * most).astype(np.float32)[None], (8, 1))
    tables = (
        my_expert.astype(jnp.int32).reshape(1, 1),
        jnp.asarray(before.astype(np.float32), BF),
        jnp.asarray(base),
    )
    order = Order()
    pieces, along, around, picked, sums, ends = {0: payload}, {}, {}, {}, {}, {}
    moving, finals, held = {}, {}, {}

    def start_outer(number):
        if number < outer:
            (tied,) = order.enter(payload)
            pieces[number] = shift_expert(tied, 0, number)

    def start_inner(number):
        (mine,) = order.enter(pieces[number])
        along[number] = gather_start(mine, 1)
        around[number] = [] if number else [gather_start(mine, 2)]

    def add_up(numbers):
        if len(numbers):
            (arrived,) = order.enter([finals.pop(number) for number in numbers])
            total = add_all(arrived[0].astype(F32), arrived[1:])
            order.leave(total)
            finals[numbers[0]] = total

    def start_back(number):
        mine, others = held[number]
        (others,) = order.enter(others)
        moving[number] = (
            mine,
            [shift_expert(other, 1, -step) for step, other in enumerate(others, 1)],
        )

    def start_core(number):
        (mine,) = order.enter(along[number])
        order.leave(*mine)
        around[number] = around[number] + [
            gather_start(value, 2) for value in (mine if number else mine[1:])
        ]

    def cuts_of(number):
        return inner if number < last else 1

    def ready_parts(across):
        return [piece[index] for index in range(core) for piece in across]

    def partial_sums(number):
        across, tied = order.enter(around[number], pieces.get(2) if number == 1 else None)
        if number == 1 and outer > 2:
            pieces[2] = tied
            if outer > 3:
                late, _ = lax.optimization_barrier((payload, tied))
                pieces[3] = shift_expert(late, 0, 3)
            along[2] = gather_start(tied, 1)
            around[2] = []
        projected(
            number, project(ready_parts(across), *tables, slots, gate_w, up_w, down_w)
        )
        order.leave(picked[number][6])

    def projected(number, results):
        picked[number] = results
        own, sent = results[5:]
        sums[number] = (own, exchange(sent))

    def finished(number, results):
        ends[number] = results[:3]
        back = results[3:]
        cuts = len(back) // core
        moving[number] = [
            (
                back[cut],
                [shift_expert(back[step * cuts + cut], 2, -step) for step in range(1, core)],
            )
            for cut in range(cuts)
        ]

    def finish_chunk(number, later=None):
        own, arrived, across = order.enter(*sums[number], around.get(later))
        if number == last:
            order.leave(*arrived)
            for earlier in range(1, number - 1):
                next_outer(earlier)
            own, arrived = order.enter(own, arrived)
        x_rows, grad, term, weight, pick = picked[number][:5]
        left = (own, arrived, grad, weight, pick, route_cols)
        if later is None:
            results = finish(*left, gate_w, up_w, down_w, core * cuts_of(number))
            order.leave(*results[3:])
            finished(number, results)
        else:
            made, results = finish_and_project(
                left, ready_parts(across), *tables, slots, gate_w, up_w, down_w, core * cuts_of(number)
            )
            order.leave(made[6], *results[3:])
            projected(later, made)
            finished(number, results)

    def next_inner(number):
        (cuts,) = order.enter(moving[number])
        if len(cuts) == inner:
            groups_here = [[mine] + arrived for mine, arrived in cuts]
            mine, *others = merge_between(groups_here, [F32] + [BF] * (inner - 1))
        else:
            mine, *others = merge([cuts[0][0]] + cuts[0][1], inner)
        order.leave(mine, *others)
        held[number] = (mine, others)
        start_back(number)

    def next_outer(number):
        mine, arrived = order.enter(*moving[number])
        (total,) = merge([mine] + arrived, 1)
        if number and number == last:
            total = total.astype(BF)
            order.leave(total)
            parts = [total[g * rows : (g + 1) * rows] for g in range(groups)]
            finals[number] = [
                shift_to_owner(choose(parts, (mine_dp + step) % groups), step, -number)
                for step in range(groups)
            ]
            return
        if number:
            total = total.astype(BF)
        order.leave(total)
        finals[number] = shift_expert(total, 0, -number) if number else total

    pieces[0], tables = order.enter(payload, tables)
    payload = pieces[0]
    start_inner(0)
    start_outer(1)
    along[0], pieces = order.enter(along[0], pieces)
    order.leave(*along[0])
    start_core(0)
    if last:
        start_inner(1)
    start_outer(2)
    partial_sums(0)
    if last:
        start_core(1)
        partial_sums(1)
    if last > 1:
        if last > 2:
            start_inner(3)
        start_core(2)
    for number in range(last + 1):
        later = number + 2
        if later <= last:
            finish_chunk(number, later)
            if later < last:
                if later > 2:
                    start_inner(later + 1)
                start_core(later + 1)
                start_outer(later + 2)
        else:
            finish_chunk(number)
        if 0 < number == last - 1:
            next_outer(0)
        if number < last:
            next_inner(number)
    add_up(range(1, last - 1))
    if last > 1:
        next_outer(last - 1)
    next_inner(last)

    def rows_of(table, index):
        return [table[number][index] for number in range(last + 1)]

    def joined(values):
        return jnp.concatenate(values, axis=0)

    hidden_all, out_all = order.enter(rows_of(ends, 0), rows_of(picked, 2))
    down_grad = dot_tn(joined(hidden_all), joined(out_all)).astype(BF)[None]
    order.leave(down_grad)
    next_outer(last)
    x_all, gate_all = order.enter(rows_of(picked, 0), rows_of(ends, 1))
    x_all = joined(x_all)
    gate_grad = dot_tn(x_all, joined(gate_all)).astype(BF)[None]
    order.leave(gate_grad)
    straight = finals.pop(last) if last else None
    (arrived,) = order.enter(list(finals.values()))
    total = add_all(arrived[0].astype(F32), arrived[1:])
    sums_here = [total[g * rows : (g + 1) * rows] for g in range(groups)]
    by_step = [choose(sums_here, mine_dp)]
    for step in range(1, groups):
        by_step.append(shift_dp(choose(sums_here, (mine_dp + step) % groups).astype(BF), step))
    order.leave(total)
    x_all, up_all = order.enter(x_all, rows_of(ends, 2))
    up_grad = dot_tn(x_all, joined(up_all)).astype(BF)[None]
    order.leave(up_grad)
    if last:
        by_step, straight = order.enter(by_step, straight)
        by_step = [value.astype(F32) + add.astype(F32) for value, add in zip(by_step, straight)]
    by_step = [value.astype(BF) for value in by_step]
    parts = [choose(by_step, (mine_dp - g) % groups) for g in range(groups)]
    mixed = jnp.concatenate([value[:, :part] for value in parts], axis=1)
    tokens_grad = jnp.concatenate([value[:, part + extra :] for value in parts], axis=1)
    route_table = jnp.zeros((), F32)
    for value in parts:
        for number in range(3):
            start = part + number * experts
            route_table = route_table + value[:, start : start + experts].astype(F32)
    route_grad = jnp.sum(jnp.where(chosen, route_table[:, None, :], 0.0), axis=2)
    return (mixed, tokens_grad, route_grad, gate_grad, up_grad, down_grad)


def solution(mesh):
    return jax.shard_map(
        per_device,
        mesh=mesh,
        in_specs=(
            P(("dp", "expert"), None),
            P(("dp", "expert"), None),
            P(("dp", "expert"), None),
            P(("dp", "expert"), None),
            P("expert", "dp", None),
            P("expert", "dp", None),
            P("expert", None, "dp"),
        ),
        out_specs=(
            P(("dp", "expert"), None),
            P(("dp", "expert"), None),
            P(("dp", "expert"), None),
            P("expert", "dp", None),
            P("expert", "dp", None),
            P("expert", None, "dp"),
        ),
        check_vma=False,
    )
```

```python
import jax
import jax.numpy as jnp
import numpy as np
from jax import lax
from jax.experimental import pallas as pl
from jax.experimental.pallas import tpu as pltpu
from jax.sharding import PartitionSpec as P

BF = jnp.bfloat16
F32 = jnp.float32


def silu_parts(pre_act):
    sigmoid_val = jax.nn.sigmoid(pre_act)
    return (pre_act * sigmoid_val, sigmoid_val * (1.0 + pre_act * (1.0 - sigmoid_val)))


def dot_nn(first, second):
    return lax.dot_general(first, second, (((1,), (0,)), ((), ())), preferred_element_type=F32)


def dot_nt(first, second):
    return lax.dot_general(first, second, (((1,), (1,)), ((), ())), preferred_element_type=F32)


def dot_tn(first, second):
    return lax.dot_general(first, second, (((0,), (0,)), ((), ())), preferred_element_type=F32)


def shift_dp(value, step):
    groups = lax.axis_size("dp")
    return lax.ppermute(value, "dp", [(i, (i + step) % groups) for i in range(groups)])


def choose(parts, index):
    picked = parts[0]
    for number in range(1, len(parts)):
        picked = jnp.where(index == number, parts[number], picked)
    return picked


def swap_groups(parts):
    groups = len(parts)
    mine = lax.axis_index("dp")
    by_step = [choose(parts, mine)]
    for step in range(1, groups):
        by_step.append(shift_dp(choose(parts, (mine + step) % groups), step))
    return [choose(by_step, (mine - group) % groups) for group in range(groups)]


def exchange(sent):
    return [shift_dp(sent, step) for step in range(1, lax.axis_size("dp"))]


def add_all(total, arrived):
    for value in arrived:
        total = total + value.astype(F32)
    return total


class Order:
    def __init__(self):
        self.last = []

    def enter(self, *values):
        flat, tree = jax.tree.flatten(values)
        tied = lax.optimization_barrier(tuple(flat) + tuple(self.last))[: len(flat)]
        return jax.tree.unflatten(tree, tied)

    def leave(self, *values):
        self.last = list(values)


def factors(experts):
    core = 2 if experts % 2 == 0 else 1
    rest = experts // core
    inner = 1
    while rest % (inner * 2) == 0 and (inner * 2) ** 2 <= rest:
        inner = inner * 2
    return (rest // inner, inner, core)


def shift_expert(value, level, step):
    dims = factors(lax.axis_size("expert"))
    stride = 1
    for dim in dims[level + 1 :]:
        stride = stride * dim
    size = dims[level]
    pairs = []
    for source in range(lax.axis_size("expert")):
        place = source // stride % size
        pairs.append((source, source + ((place + step) % size - place) * stride))
    return lax.ppermute(value, "expert", pairs)


def shift_to_owner(value, dp_step, outer_step):
    groups, experts = lax.axis_size("dp"), lax.axis_size("expert")
    outer, inner, core = factors(experts)
    pairs = []
    for group in range(groups):
        for source in range(experts):
            place = source // (inner * core)
            target = source + ((place + outer_step) % outer - place) * inner * core
            pairs.append((group * experts + source, (group + dp_step) % groups * experts + target))
    return lax.ppermute(value, ("dp", "expert"), pairs)


def level_size(level):
    return factors(lax.axis_size("expert"))[level]


def gather_start(piece, level):
    return [piece] + [shift_expert(piece, level, step) for step in range(1, level_size(level))]


def three_pieces(value):
    high = lax.reduce_precision(value, 8, 7)
    rest = value - high
    mid = lax.reduce_precision(rest, 8, 7)
    return [high.astype(BF), mid.astype(BF), (rest - mid).astype(BF)]


def stacked_rows(values):
    return jnp.concatenate(values, axis=0) if len(values) > 1 else values[0]


def project_body(number_parts, part, experts, *refs):
    mask_ref, order_ref, base_ref = refs[:3]
    part_refs = refs[3 : 3 + number_parts]
    gate_ref, up_ref, down_ref = refs[3 + number_parts : 6 + number_parts]
    x_ref, grad_ref, term_ref, weight_ref, pick_ref, own_ref, sent_ref = refs[6 + number_parts :]

    @pl.when(pl.program_id(0) == 0)
    def _():
        slots = x_ref.shape[0]
        arrived = stacked_rows([ref[...] for ref in part_refs])
        count = arrived.shape[0]
        column = lax.broadcasted_iota(jnp.int32, (8, arrived.shape[1] - 2 * part), 1)
        expert = mask_ref[0, 0]
        mask = jnp.zeros(column.shape, F32)
        for number in range(3):
            mask = mask + jnp.where(column == number * experts + expert, 1.0, 0.0)
        mask = mask.astype(BF)
        weight = dot_nt(mask, arrived[:, 2 * part :])
        live = weight > 0.0
        place = dot_nn(jnp.where(live, 1.0, 0.0).astype(BF), order_ref[...])
        slot = jnp.where(live, place - 1.0 + base_ref[...], -1.0)[:1]
        index = lax.broadcasted_iota(jnp.int32, (slots, count), 0).astype(F32)
        pick = jnp.where(index == slot, 1.0, 0.0).astype(BF)
        pick_ref[...] = pick
        x_ref[...] = dot_nn(pick, arrived[:, :part]).astype(BF)
        grad = dot_nn(pick, arrived[:, part : 2 * part])
        grad_ref[...] = grad.astype(BF)
        chosen = dot_nn(pick, arrived[:, 2 * part :]) * mask[:1].astype(F32)
        weight_rows = jnp.sum(chosen, axis=1, keepdims=True)
        weight_ref[...] = jnp.broadcast_to(weight_rows, weight_ref.shape)
        term_ref[...] = (weight_rows * grad).astype(BF)

    x_rows = x_ref[...]
    values = (
        dot_nn(x_rows, gate_ref[...]),
        dot_nn(x_rows, up_ref[...]),
        dot_nt(term_ref[...], down_ref[...]),
    )
    for number, value in enumerate(values):
        own_ref[number] = value
        sent_ref[number] = value.astype(BF)


def project(parts, mask, order, base, slots, gate_w, up_w, down_w):
    experts = lax.axis_size("expert")
    part, hidden = gate_w.shape
    tile = min(256, hidden)
    count = sum(value.shape[0] for value in parts)
    whole = lambda shape: pl.BlockSpec(shape, lambda j: (0,) * len(shape))
    columns = lambda rows: pl.BlockSpec((rows, tile), lambda j: (0, j))
    stacked = pl.BlockSpec((3, slots, tile), lambda j: (0, 0, j))
    row_out = jax.ShapeDtypeStruct((slots, part), BF)
    return pl.pallas_call(
        lambda *refs: project_body(len(parts), part, experts, *refs),
        grid=(hidden // tile,),
        in_specs=[pl.BlockSpec(memory_space=pltpu.SMEM), whole(order.shape), whole(base.shape)]
        + [whole(value.shape) for value in parts]
        + [columns(part), columns(part), pl.BlockSpec((tile, part), lambda j: (j, 0))],
        out_specs=[whole((slots, part))] * 3
        + [whole((slots, 128)), whole((slots, count)), stacked, stacked],
        out_shape=[row_out] * 3
        + [
            jax.ShapeDtypeStruct((slots, 128), F32),
            jax.ShapeDtypeStruct((slots, count), BF),
            jax.ShapeDtypeStruct((3, slots, hidden), F32),
            jax.ShapeDtypeStruct((3, slots, hidden), BF),
        ],
        compiler_params=pltpu.CompilerParams(vmem_limit_bytes=56 * 2**20),
        name="project",
    )(mask, order, base, *parts, gate_w, up_w, down_w)


def merge(values, pieces):
    total = add_all(values[0].astype(F32), values[1:])
    rows = total.shape[0] // pieces
    parts = [total[number * rows : (number + 1) * rows] for number in range(pieces)]
    return parts[:1] + [part.astype(BF) for part in parts[1:]]


def merge_between(groups, kinds):
    sizes = [len(group) for group in groups]

    def body(*refs):
        start = 0
        for size, out in zip(sizes, refs[sum(sizes) :]):
            total = add_all(refs[start][...].astype(F32), [ref[...] for ref in refs[start + 1 : start + size]])
            out[...] = total.astype(out.dtype)
            start += size

    return pl.pallas_call(
        body,
        out_shape=[
            jax.ShapeDtypeStruct(group[0].shape, kind) for group, kind in zip(groups, kinds)
        ],
        compiler_params=pltpu.CompilerParams(vmem_limit_bytes=56 * 2**20),
        name="merge",
    )(*[value for group in groups for value in group])


def finish_body(number_sent, number_parts, *refs):
    own_ref = refs[0]
    sent_refs = refs[1 : 1 + number_sent]
    grad_ref, weight_ref, pick_ref, route_ref, gate_ref, up_ref, down_ref = refs[
        1 + number_sent : 8 + number_sent
    ]
    hidden_ref, gate_term_ref, up_term_ref = refs[8 + number_sent : 11 + number_sent]
    back_refs = refs[11 + number_sent : 11 + number_sent + number_parts]
    out_acc, in_acc = refs[11 + number_sent + number_parts :]
    step = pl.program_id(0)
    gate_pre, up_pre, hidden_grad = (
        add_all(own_ref[number], [ref[number] for ref in sent_refs]) for number in range(3)
    )
    act_val, act_slope = silu_parts(gate_pre)
    hidden = (act_val * up_pre).astype(BF)
    gate_term = (hidden_grad * up_pre * act_slope).astype(BF)
    up_term = (hidden_grad * act_val).astype(BF)
    hidden_ref[...] = hidden
    gate_term_ref[...] = gate_term
    up_term_ref[...] = up_term
    out_part = dot_nn(hidden, down_ref[...])
    in_part = dot_nt(gate_term, gate_ref[...]) + dot_nt(up_term, up_ref[...])

    @pl.when(step == 0)
    def _():
        out_acc[...] = out_part
        in_acc[...] = in_part

    @pl.when(step > 0)
    def _():
        out_acc[...] += out_part
        in_acc[...] += in_part

    @pl.when(step == pl.num_programs(0) - 1)
    def _():
        part = out_acc.shape[1]
        extra = route_ref.shape[1]
        expert_out = out_acc[...].astype(BF).astype(F32)
        rest = jnp.sum(grad_ref[...].astype(F32) * expert_out, axis=1, keepdims=True)
        route = jnp.zeros((rest.shape[0], extra), F32)
        for number in range(3):
            piece = rest.astype(BF).astype(F32)
            route = route + piece * route_ref[number : number + 1]
            rest = rest - piece
        pick = pick_ref[...]
        weighted = (weight_ref[:, :1] * expert_out).astype(BF)
        backs = (
            dot_tn(pick, weighted).astype(BF),
            dot_tn(pick, route.astype(BF)).astype(BF),
            dot_tn(pick, in_acc[...].astype(BF)).astype(BF),
        )
        rows = back_refs[0].shape[0]
        for number, ref in enumerate(back_refs):
            here = slice(number * rows, (number + 1) * rows)
            ref[:, :part] = backs[0][here]
            ref[:, part : part + extra] = backs[1][here]
            ref[:, part + extra :] = backs[2][here]


def finish(own, sent, grad, weight, pick, route, gate_w, up_w, down_w, number_parts):
    part, hidden = gate_w.shape
    tile = min(256, hidden)
    slots, count = pick.shape
    rows = count // number_parts
    wide = 2 * part + route.shape[1]
    whole = lambda shape: pl.BlockSpec(shape, lambda j: (0,) * len(shape))
    columns = lambda size: pl.BlockSpec((size, tile), lambda j: (0, j))
    stacked = pl.BlockSpec((3, slots, tile), lambda j: (0, 0, j))
    return pl.pallas_call(
        lambda *refs: finish_body(len(sent), number_parts, *refs),
        grid=(hidden // tile,),
        in_specs=[stacked] * (1 + len(sent))
        + [whole(value.shape) for value in (grad, weight, pick, route)]
        + [columns(part), columns(part), pl.BlockSpec((tile, part), lambda j: (j, 0))],
        out_specs=[columns(slots)] * 3 + [whole((rows, wide))] * number_parts,
        out_shape=[jax.ShapeDtypeStruct((slots, hidden), BF)] * 3
        + [jax.ShapeDtypeStruct((rows, wide), BF)] * number_parts,
        scratch_shapes=[pltpu.VMEM((slots, part), F32), pltpu.VMEM((slots, part), F32)],
        compiler_params=pltpu.CompilerParams(vmem_limit_bytes=56 * 2**20),
        name="finish",
    )(own, *sent, grad, weight, pick, route, gate_w, up_w, down_w)


def finish_and_project(left, parts, mask, order, base, slots, gate_w, up_w, down_w, number_parts):
    own, sent, grad, weight, pick, route = left
    experts = lax.axis_size("expert")
    part, hidden = gate_w.shape
    tile = min(256, hidden)
    count = sum(value.shape[0] for value in parts)
    rows = pick.shape[1] // number_parts
    wide = 2 * part + route.shape[1]
    whole = lambda shape: pl.BlockSpec(shape, lambda j: (0,) * len(shape))
    columns = lambda size: pl.BlockSpec((size, tile), lambda j: (0, j))
    stacked = pl.BlockSpec((3, slots, tile), lambda j: (0, 0, j))
    first = 3 + len(parts)
    second = first + 5 + len(sent)
    weights = second + 3

    def body(*refs):
        outs = refs[weights : weights + 7]
        ends = refs[weights + 7 :]
        finish_body(len(sent), number_parts, *refs[first:weights], *ends)
        project_body(len(parts), part, experts, *refs[:first], *refs[second:weights], *outs)

    results = pl.pallas_call(
        body,
        grid=(hidden // tile,),
        in_specs=[pl.BlockSpec(memory_space=pltpu.SMEM)]
        + [whole(value.shape) for value in (order, base, *parts)]
        + [stacked] * (1 + len(sent))
        + [whole(value.shape) for value in (grad, weight, pick, route)]
        + [columns(part), columns(part), pl.BlockSpec((tile, part), lambda j: (j, 0))],
        out_specs=[whole((slots, part))] * 3
        + [whole((slots, 128)), whole((slots, count)), stacked, stacked]
        + [columns(slots)] * 3
        + [whole((rows, wide))] * number_parts,
        out_shape=[jax.ShapeDtypeStruct((slots, part), BF)] * 3
        + [
            jax.ShapeDtypeStruct((slots, 128), F32),
            jax.ShapeDtypeStruct((slots, count), BF),
            jax.ShapeDtypeStruct((3, slots, hidden), F32),
            jax.ShapeDtypeStruct((3, slots, hidden), BF),
        ]
        + [jax.ShapeDtypeStruct((slots, hidden), BF)] * 3
        + [jax.ShapeDtypeStruct((rows, wide), BF)] * number_parts,
        scratch_shapes=[pltpu.VMEM((slots, part), F32), pltpu.VMEM((slots, part), F32)],
        compiler_params=pltpu.CompilerParams(vmem_limit_bytes=56 * 2**20),
        name="step",
    )(mask, order, base, *parts, own, *sent, grad, weight, pick, route, gate_w, up_w, down_w)
    return results[:7], results[7:]


def per_device(tokens, expert_ids, route_weights, out_grad, gate_weight, up_weight, down_weight):
    experts = lax.axis_size("expert")
    groups = lax.axis_size("dp")
    my_expert = lax.axis_index("expert")
    mine_dp = lax.axis_index("dp")
    outer, inner, core = factors(experts)
    rows, width = tokens.shape
    hidden_width = gate_weight.shape[2]
    choices = expert_ids.shape[1]
    part = width // groups
    most = min(rows, 3 * rows * choices // (2 * experts))
    extra = -(-3 * experts // 128) * 128
    gate_w, up_w, down_w = gate_weight[0], up_weight[0], down_weight[0]

    chosen = expert_ids[:, :, None] == jnp.arange(experts, dtype=jnp.int32)[None, None, :]
    weight_table = jnp.sum(jnp.where(chosen, route_weights[:, :, None], 0.0), axis=1)
    weight_cols = jnp.concatenate(
        three_pieces(weight_table) + [jnp.zeros((rows, extra - 3 * experts), BF)], axis=1
    )
    payload = jnp.concatenate(
        swap_groups(
            [
                jnp.concatenate(
                    [
                        tokens[:, g * part : (g + 1) * part],
                        out_grad[:, g * part : (g + 1) * part],
                        weight_cols,
                    ],
                    axis=1,
                )
                for g in range(groups)
            ]
        ),
        axis=0,
    )

    column = jnp.arange(extra, dtype=jnp.int32)[None, :]
    route_cols = (
        column == jnp.arange(8, dtype=jnp.int32)[:, None] * experts + my_expert
    ) & (jnp.arange(8)[:, None] < 3)
    route_cols = route_cols.astype(F32)
    last = outer - 1
    count = inner * core * groups * rows
    slots = inner * core * groups * most
    token = np.arange(count)
    block = token // rows
    before = (block[:, None] == block[None, :]) & (token[:, None] <= token[None, :])
    base = np.tile((block * most).astype(np.float32)[None], (8, 1))
    tables = (
        my_expert.astype(jnp.int32).reshape(1, 1),
        jnp.asarray(before.astype(np.float32), BF),
        jnp.asarray(base),
    )
    order = Order()
    pieces, along, around, picked, sums, ends = {0: payload}, {}, {}, {}, {}, {}
    moving, finals, held = {}, {}, {}

    def start_outer(number):
        if number < outer:
            (tied,) = order.enter(payload)
            pieces[number] = shift_expert(tied, 0, number)

    def start_inner(number):
        (mine,) = order.enter(pieces[number])
        along[number] = gather_start(mine, 1)
        around[number] = [] if number else [gather_start(mine, 2)]

    def add_up(numbers):
        if len(numbers):
            (arrived,) = order.enter([finals.pop(number) for number in numbers])
            total = add_all(arrived[0].astype(F32), arrived[1:])
            order.leave(total)
            finals[numbers[0]] = total

    def start_back(number):
        mine, others = held[number]
        (others,) = order.enter(others)
        moving[number] = (
            mine,
            [shift_expert(other, 1, -step) for step, other in enumerate(others, 1)],
        )

    def start_core(number):
        (mine,) = order.enter(along[number])
        order.leave(*mine)
        around[number] = around[number] + [
            gather_start(value, 2) for value in (mine if number else mine[1:])
        ]

    def cuts_of(number):
        return inner if number < last else 1

    def ready_parts(across):
        return [piece[index] for index in range(core) for piece in across]

    def partial_sums(number):
        across, tied = order.enter(around[number], pieces.get(2) if number == 1 else None)
        if number == 1 and outer > 2:
            pieces[2] = tied
            if outer > 3:
                late, _ = lax.optimization_barrier((payload, tied))
                pieces[3] = shift_expert(late, 0, 3)
            along[2] = gather_start(tied, 1)
            around[2] = []
        projected(
            number, project(ready_parts(across), *tables, slots, gate_w, up_w, down_w)
        )
        order.leave(picked[number][6])

    def projected(number, results):
        picked[number] = results
        own, sent = results[5:]
        sums[number] = (own, exchange(sent))

    def finished(number, results):
        ends[number] = results[:3]
        back = results[3:]
        cuts = len(back) // core
        moving[number] = [
            (
                back[cut],
                [shift_expert(back[step * cuts + cut], 2, -step) for step in range(1, core)],
            )
            for cut in range(cuts)
        ]

    def finish_chunk(number, later=None):
        own, arrived, across = order.enter(*sums[number], around.get(later))
        if number == last:
            order.leave(*arrived)
            for earlier in range(1, number - 1):
                next_outer(earlier)
            own, arrived = order.enter(own, arrived)
        x_rows, grad, term, weight, pick = picked[number][:5]
        left = (own, arrived, grad, weight, pick, route_cols)
        if later is None:
            results = finish(*left, gate_w, up_w, down_w, core * cuts_of(number))
            order.leave(*results[3:])
            finished(number, results)
        else:
            made, results = finish_and_project(
                left, ready_parts(across), *tables, slots, gate_w, up_w, down_w, core * cuts_of(number)
            )
            order.leave(made[6], *results[3:])
            projected(later, made)
            finished(number, results)

    def next_inner(number):
        (cuts,) = order.enter(moving[number])
        if len(cuts) == inner:
            groups_here = [[mine] + arrived for mine, arrived in cuts]
            mine, *others = merge_between(groups_here, [F32] + [BF] * (inner - 1))
        else:
            mine, *others = merge([cuts[0][0]] + cuts[0][1], inner)
        order.leave(mine, *others)
        held[number] = (mine, others)
        start_back(number)

    def next_outer(number):
        mine, arrived = order.enter(*moving[number])
        (total,) = merge([mine] + arrived, 1)
        if number and number >= last - 1:
            total = total.astype(BF)
            order.leave(total)
            parts = [total[g * rows : (g + 1) * rows] for g in range(groups)]
            finals[number] = [
                shift_to_owner(choose(parts, (mine_dp + step) % groups), step, -number)
                for step in range(groups)
            ]
            return
        if number:
            total = total.astype(BF)
        order.leave(total)
        finals[number] = shift_expert(total, 0, -number) if number else total

    pieces[0], tables = order.enter(payload, tables)
    payload = pieces[0]
    start_inner(0)
    start_outer(1)
    along[0], pieces = order.enter(along[0], pieces)
    order.leave(*along[0])
    start_core(0)
    if last:
        start_inner(1)
    start_outer(2)
    partial_sums(0)
    if last:
        start_core(1)
        partial_sums(1)
    if last > 1:
        if last > 2:
            start_inner(3)
        start_core(2)
    for number in range(last + 1):
        later = number + 2
        if later <= last:
            finish_chunk(number, later)
            if later < last:
                if later > 2:
                    start_inner(later + 1)
                start_core(later + 1)
                start_outer(later + 2)
        else:
            finish_chunk(number)
        if 0 < number == last - 1:
            next_outer(0)
        if number < last:
            next_inner(number)
    add_up(range(1, last - 1))
    (arrived,) = order.enter([finals[k] for k in sorted(finals) if k < max(1, last - 1)])
    total = add_all(arrived[0].astype(F32), arrived[1:])
    sums_here = [total[g * rows : (g + 1) * rows] for g in range(groups)]
    by_step = [choose(sums_here, mine_dp)]
    for step in range(1, groups):
        by_step.append(shift_dp(choose(sums_here, (mine_dp + step) % groups).astype(BF), step))
    order.leave(total)
    if last > 1:
        next_outer(last - 1)
    next_inner(last)

    def rows_of(table, index):
        return [table[number][index] for number in range(last + 1)]

    def joined(values):
        return jnp.concatenate(values, axis=0)

    hidden_all, out_all = order.enter(rows_of(ends, 0), rows_of(picked, 2))
    down_grad = dot_tn(joined(hidden_all), joined(out_all)).astype(BF)[None]
    order.leave(down_grad)
    next_outer(last)
    x_all, gate_all = order.enter(rows_of(picked, 0), rows_of(ends, 1))
    x_all = joined(x_all)
    gate_grad = dot_tn(x_all, joined(gate_all)).astype(BF)[None]
    order.leave(gate_grad)
    arrivals = [finals.pop(number) for number in range(max(1, last - 1), last + 1)]
    x_all, up_all = order.enter(x_all, rows_of(ends, 2))
    up_grad = dot_tn(x_all, joined(up_all)).astype(BF)[None]
    order.leave(up_grad)
    by_step, arrivals = order.enter(by_step, arrivals)
    by_step = [
        add_all(value.astype(F32), [sent[step] for sent in arrivals])
        for step, value in enumerate(by_step)
    ]
    by_step = [value.astype(BF) for value in by_step]
    parts = [choose(by_step, (mine_dp - g) % groups) for g in range(groups)]
    mixed = jnp.concatenate([value[:, :part] for value in parts], axis=1)
    tokens_grad = jnp.concatenate([value[:, part + extra :] for value in parts], axis=1)
    route_table = jnp.zeros((), F32)
    for value in parts:
        for number in range(3):
            start = part + number * experts
            route_table = route_table + value[:, start : start + experts].astype(F32)
    route_grad = jnp.sum(jnp.where(chosen, route_table[:, None, :], 0.0), axis=2)
    return (mixed, tokens_grad, route_grad, gate_grad, up_grad, down_grad)


def solution(mesh):
    return jax.shard_map(
        per_device,
        mesh=mesh,
        in_specs=(
            P(("dp", "expert"), None),
            P(("dp", "expert"), None),
            P(("dp", "expert"), None),
            P(("dp", "expert"), None),
            P("expert", "dp", None),
            P("expert", "dp", None),
            P("expert", None, "dp"),
        ),
        out_specs=(
            P(("dp", "expert"), None),
            P(("dp", "expert"), None),
            P(("dp", "expert"), None),
            P("expert", "dp", None),
            P("expert", "dp", None),
            P("expert", None, "dp"),
        ),
        check_vma=False,
    )
```
